512 devices in a mesh: head: 8 (over x, y_lo), ctx: 64 (over y_hi, z, core).
Axes of the slice: x: 4, y: 8 (y_hi: 4, y_lo: 2; y = y_hi * 2 + y_lo), z: 8, core: 2. Of those that a mesh axis runs over, the one named last changes fastest.
Arguments:
- merged_qkv: bfloat16 [16384, 10240], P(('ctx', 'head')), may hold values from -8.5 to 8.5
- out_grads: bfloat16 [16384, 8192], P(('ctx', 'head')), may hold values from -6 to 6
- doc_lengths: int32 [64], replicated, may hold values from 1 to 1536, 16384 in all
Outputs:
- qkv_grads: bfloat16 [16384, 10240], P(('ctx', 'head'))
The draws below stay inside these ranges and needn't reach their ends.
Inputs may be any that keep to these rules, and one draw needn't show every extreme that they name: `doc_lengths`: the lengths sum to 16384; the largest is exactly 1536.
All inputs are finite; a program needn't handle non-finite values.
Results may differ from the reference program's by a relative error of at most 0.0078.
Values may be sent and summed in bfloat16 or wider, within the bound.
A program may use at most 64 MiB of HBM per device.

```python
import math
import jax
import jax.numpy as jnp
import numpy as np
from jax import lax

Q_HEADS = 64
KV_HEADS = 8
HEAD_DIM = 128
QKV = 10240
TOK_DEV = 256
REACH = 6
DOC_MOST = 1536
TOKENS = 16384
DOCS = 64
N_CTX = 64


def draw_merged_qkv(key, part):
    key = jax.random.fold_in(key, 17)
    key_base = jax.random.fold_in(key, 0)
    normal_part = jnp.clip(jax.random.normal(key_base, (TOKENS, QKV), jnp.float32), -6.0, 6.0)
    return normal_part.astype(jnp.bfloat16)


def shard_levels(stream_key, extent, cuts, least, top_value):
    def one(position, shards_of):
        heights = jax.random.uniform(jax.random.fold_in(jax.random.fold_in(stream_key, 6), position), (shards_of,), jnp.float32, least / len(cuts), top_value / len(cuts))
        return jnp.repeat(jnp.exp(heights), extent[position] // shards_of).reshape((-1,) + (1,) * (len(extent) - position - 1))

    gain = one(*cuts[0])
    for cut in cuts[1:]:
        gain = gain * one(*cut)
    return gain


def length_profile(count, total, reach, skew):
    loads = [(1 << 20) // math.isqrt(standing ** skew) + 1 for standing in range(2, count + 1)]
    surplus, holding = total - reach - (count - 1), [1] * (count - 1)
    while surplus > 0:
        movable = [i for i in range(count - 1) if holding[i] < reach]
        pool, budget = sum([loads[i] for i in movable]), surplus
        for i in movable:
            extra = min(reach - holding[i], max(1, budget * loads[i] // pool), surplus)
            holding[i] = holding[i] + extra
            surplus = surplus - extra
    return np.array([reach] + holding)


def ragged(own_key, amount, total, bound, skew):
    if amount == 2:
        one = jax.random.randint(own_key, (), max(1, total - bound), min(bound, total - 1) + 1)
        return jnp.stack([one, total - one])
    tallies = jnp.asarray(length_profile(amount, total, bound, skew), jnp.int32)
    couples = (amount - 1) // 2
    donor, taker = tallies[1:1 + 2 * couples:2], tallies[2:2 + 2 * couples:2]
    margin = jnp.minimum(donor - 1, bound - taker)
    passed = jax.random.randint(jax.random.fold_in(own_key, 1), (couples,), 0, 1 << 20) % (margin + 1)
    tallies = tallies.at[1:1 + 2 * couples:2].set(donor - passed).at[2:2 + 2 * couples:2].set(taker + passed)
    return tallies[jax.random.permutation(jax.random.fold_in(own_key, 2), amount)]


def noise(stream_key, extent, spread, most, shards=(), kind=jnp.bfloat16):
    values = jax.random.normal(stream_key, extent, jnp.float32) * spread
    if len(shards) > 0:
        values = shard_levels(stream_key, extent, shards, -0.22, 0.18) * values
    return jnp.clip(values, min=-most, max=most).astype(kind)


def setup_inputs(seed: int = 0) -> dict:
    key_list = jax.random.split(jax.random.key(seed), 4)
    return {
        "merged_qkv": draw_merged_qkv(jax.random.fold_in(key_list[3], 71), 0),
        "out_grads": noise(key_list[1], (TOKENS, Q_HEADS * HEAD_DIM), 1.0, 6.0, ((0, 512),)),
        "doc_lengths": ragged(key_list[2], DOCS, TOKENS, DOC_MOST, 2).astype(jnp.int32),
    }


def doc_of(bounds, positions):
    return jnp.sum((bounds[None, :] <= positions[:, None]).astype(jnp.int32), axis=1)


def reference(merged_qkv, out_grads, doc_lengths):
    tok_rows = TOK_DEV
    group_q = Q_HEADS // KV_HEADS
    head_dim = HEAD_DIM
    key_span = (REACH + 1) * tok_rows
    scaling = head_dim ** -0.5
    merged_view = merged_qkv.reshape(TOKENS, KV_HEADS, group_q + 2, head_dim)
    queries = merged_view[:, :, :group_q]
    key_rows = merged_view[:, :, group_q]
    value_rows = merged_view[:, :, group_q + 1]
    grad_rows = out_grads.reshape(TOKENS, KV_HEADS, group_q, head_dim)
    bounds = jnp.cumsum(doc_lengths).astype(jnp.int32)
    padding = jnp.zeros((REACH * tok_rows, KV_HEADS, head_dim), merged_qkv.dtype)
    keys_pad = jnp.concatenate([padding, key_rows], axis=0)
    values_pad = jnp.concatenate([padding, value_rows], axis=0)

    def one_block(running, block_idx):
        dk_pad, dv_pad = running
        first_row = (block_idx * tok_rows).astype(jnp.int32)
        query_blk = lax.dynamic_slice_in_dim(queries, first_row, tok_rows, 0).astype(jnp.float32)
        grad_blk = lax.dynamic_slice_in_dim(grad_rows, first_row, tok_rows, 0).astype(jnp.float32)
        key_blk = lax.dynamic_slice_in_dim(keys_pad, first_row, key_span, 0).astype(jnp.float32)
        value_blk = lax.dynamic_slice_in_dim(values_pad, first_row, key_span, 0).astype(jnp.float32)
        query_pos = first_row + jnp.arange(tok_rows, dtype=jnp.int32)
        key_pos = first_row - REACH * tok_rows + jnp.arange(key_span, dtype=jnp.int32)
        visible = (doc_of(bounds, query_pos)[:, None] == doc_of(bounds, key_pos)[None, :])
        visible = visible & (key_pos[None, :] <= query_pos[:, None]) & (key_pos >= 0)[None, :]
        raw_score = jnp.einsum('qgnd,kgd->gnqk', query_blk, key_blk) * scaling
        raw_score = jnp.where(visible[None, None], raw_score, -jnp.inf)
        row_max = jnp.max(raw_score, axis=-1, keepdims=True)
        log_total = row_max + jnp.log(jnp.sum(jnp.exp(raw_score - row_max), axis=-1, keepdims=True))
        prob_full = jnp.exp(raw_score - log_total)
        prob_half = lax.optimization_barrier(prob_full.astype(jnp.bfloat16)).astype(jnp.float32)
        output = jnp.einsum('gnqk,kgd->qgnd', prob_half, value_blk)
        row_delta = jnp.transpose(jnp.sum(grad_blk * output, axis=-1), (1, 2, 0))
        grad_prob = jnp.einsum('qgnd,kgd->gnqk', grad_blk, value_blk)
        grad_score = prob_full * (grad_prob - row_delta[..., None]) * scaling
        grad_score = lax.optimization_barrier(grad_score.astype(jnp.bfloat16)).astype(jnp.float32)
        grad_query = jnp.einsum('gnqk,kgd->qgnd', grad_score, key_blk).astype(jnp.bfloat16)
        grad_key = jnp.einsum('gnqk,qgnd->kgd', grad_score, query_blk)
        grad_value = jnp.einsum('gnqk,qgnd->kgd', prob_half, grad_blk)
        dk_pad = lax.dynamic_update_slice_in_dim(
            dk_pad, lax.dynamic_slice_in_dim(dk_pad, first_row, key_span, 0) + grad_key, first_row, 0)
        dv_pad = lax.dynamic_update_slice_in_dim(
            dv_pad, lax.dynamic_slice_in_dim(dv_pad, first_row, key_span, 0) + grad_value, first_row, 0)
        return (dk_pad, dv_pad), grad_query

    zero_grads = jnp.zeros((TOKENS + REACH * tok_rows, KV_HEADS, head_dim), jnp.float32)
    (dk_pad, dv_pad), grad_query = lax.scan(one_block, (zero_grads, zero_grads),
                                            jnp.arange(N_CTX, dtype=jnp.int32))
    grad_query = grad_query.reshape(TOKENS, KV_HEADS, group_q, head_dim)
    grad_key = dk_pad[REACH * tok_rows:].astype(jnp.bfloat16)
    grad_value = dv_pad[REACH * tok_rows:].astype(jnp.bfloat16)
    joined = jnp.concatenate([grad_query, grad_key[:, :, None], grad_value[:, :, None]], axis=2)
    return joined.reshape(TOKENS, QKV)
```

```python
import functools
import math

import jax
import jax.numpy as jnp
from jax import lax
from jax.experimental import pallas as pl
from jax.experimental.pallas import tpu as pltpu
from jax.sharding import PartitionSpec as P

GROUP_Q = 8
HEAD_DIM = 128
REACH = 6
MESH = pl.DeviceIdType.MESH
SCALE = HEAD_DIM ** -0.5
TO_EXP2 = SCALE * math.log2(math.e)
FAR = 2.0 ** 100
F32, BF16 = jnp.float32, jnp.bfloat16
IN_CHUNKS = 2
HEADS_STEP = 2


def nt(a, b):
    return lax.dot_general(a, b, (((1,), (1,)), ((), ())), preferred_element_type=F32)


def nn(a, b):
    return lax.dot_general(a, b, (((1,), (0,)), ((), ())), preferred_element_type=F32)


def tn(a, b):
    return lax.dot_general(a, b, (((0,), (0,)), ((), ())), preferred_element_type=F32)


def wait_bytes(ref, sem):
    pltpu.make_async_copy(ref, ref, sem).wait()


def kernel(n_head, n_ctx, lens_ref, qkv_ref, grads_ref, out_ref,
           kv, key_doc, query_doc, qb, dob, probs, dprobs, st_m, st_l, st_d, gain, delta,
           dq, home, part, odd_out, odd_in, rail_out, rail_in, stage,
           s_in, r_in, l_in, s_rail, r_rail, s_sib, r_sib, s_grail, r_grail, s_gsib, r_gsib,
           s_out, r_out, l_out):
    rows = qkv_ref.shape[0]
    piece = kv.shape[1]
    width = (GROUP_Q + 2) * HEAD_DIM
    q_width = GROUP_Q * HEAD_DIM
    me = lax.axis_index("head")
    ctx = lax.axis_index("ctx")
    core = lax.rem(ctx, 2)
    sib = ctx + 1 - 2 * core
    after = lax.rem(ctx + 2, n_ctx)
    before = lax.rem(ctx + n_ctx - 2, n_ctx)
    peers = [lax.rem(me + p, n_head) for p in range(1, n_head)]

    barrier = pltpu.get_barrier_semaphore()
    for peer in peers:
        pl.semaphore_signal(barrier, inc=1, device_id={"head": peer}, device_id_type=MESH)
    for other in (sib, after, before):
        pl.semaphore_signal(barrier, inc=1, device_id={"ctx": other}, device_id_type=MESH)
    pl.semaphore_wait(barrier, len(peers) + 3)

    my_rows = pl.ds(pl.multiple_of(me * rows, rows), rows)

    def column(group, first, size):
        return pl.ds(pl.multiple_of(group * width + first, HEAD_DIM), size)

    def grad_column(group, first, size):
        return pl.ds(pl.multiple_of(group * q_width + first, HEAD_DIM), size)

    step_w = q_width // IN_CHUNKS
    sends = [(qkv_ref, lambda g: column(g, q_width, 2 * HEAD_DIM), kv.at[0], pl.ds(0, 2 * HEAD_DIM))]
    for chunk in range(IN_CHUNKS):
        cols = pl.ds(chunk * step_w, step_w)
        sends.append((qkv_ref, lambda g, f=chunk * step_w: column(g, f, step_w), qb, cols))
        sends.append((grads_ref, lambda g, f=chunk * step_w: grad_column(g, f, step_w), dob, cols))
    for i, (src, src_cols, dst, dst_cols) in enumerate(sends):
        for peer in peers:
            pltpu.make_async_remote_copy(
                src_ref=src.at[:, src_cols(peer)], dst_ref=dst.at[my_rows, dst_cols],
                send_sem=s_in.at[i], recv_sem=r_in.at[i],
                device_id={"head": peer}, device_id_type=MESH).start()
        pltpu.make_async_copy(src.at[:, src_cols(me)], dst.at[my_rows, dst_cols], l_in.at[i]).start()

    def arrived(i):
        src, src_cols, dst, dst_cols = sends[i]
        pltpu.make_async_copy(src.at[:, src_cols(me)], dst.at[my_rows, dst_cols], l_in.at[i]).wait()
        wait_bytes(dst.at[pl.ds(0, rows * (n_head - 1)), dst_cols], r_in.at[i])

    def ctx_copy(src, dst, send_sem, recv_sem, device):
        return pltpu.make_async_remote_copy(
            src_ref=src, dst_ref=dst, send_sem=send_sem, recv_sem=recv_sem,
            device_id={"ctx": device}, device_id_type=MESH)

    lane = lax.broadcasted_iota(jnp.int32, (1, HEAD_DIM), 1)
    starts = jnp.full((1, HEAD_DIM), 1 << 20, jnp.int32)
    ends = jnp.full((1, HEAD_DIM), 1 << 20, jnp.int32)
    total = jnp.int32(0)
    for d in range(lens_ref.shape[0]):
        starts = jnp.where(lane == d, total, starts)
        total = total + lens_ref[d]
        ends = jnp.where(lane == d, total, ends)
    row_of = lax.broadcasted_iota(jnp.int32, (piece, HEAD_DIM), 0)
    lane_of = lax.broadcasted_iota(jnp.int32, (piece, HEAD_DIM), 1)
    for r in range(REACH + 1):
        pos = row_of + (ctx - r) * piece
        inside = ((starts <= pos) & (pos < ends)) | ((lane_of == HEAD_DIM - 1) & (pos < 0))
        key_doc[r] = jnp.where(inside, 1.0, 0.0).astype(BF16)
        if r == 0:
            query_doc[...] = jnp.where(inside, 0.0, -FAR).astype(BF16)
    causal = (lax.broadcasted_iota(jnp.int32, (piece, piece), 0)
              <= lax.broadcasted_iota(jnp.int32, (piece, piece), 1))

    def rail_send(r):
        return ctx_copy(kv.at[r], kv.at[r + 2], s_rail.at[r // 2], r_rail.at[r // 2], after)

    def sib_send(k, j):
        return ctx_copy(kv.at[2 * j + 2 * k], kv.at[2 * j + 1], s_sib.at[j], r_sib.at[j], sib)

    def pass_on(r):
        if r < REACH:
            rail_send(r).start()

            @pl.when(core == 0)
            def _():
                sib_send(0, r // 2).start()
        if r > 0:

            @pl.when(core == 1)
            def _():
                sib_send(1, r // 2 - 1).start()

    arrived(0)
    pass_on(0)

    groups = ((1, 2), (3, 4), (5, 6))
    last = len(groups) - 1

    def forward(gi, first_head, heads):
        ra, rb = groups[gi]

        def body(step, carry):
            for u in range(HEADS_STEP):
                j = first_head + step * HEADS_STEP + u
                cols = pl.ds(pl.multiple_of(j * HEAD_DIM, HEAD_DIM), HEAD_DIM)
                query = jnp.concatenate([qb[:, cols], query_doc[...]], axis=1)
                grad = dob[:, cols]

                def both(r):
                    keys = jnp.concatenate([kv[r, :, :HEAD_DIM], key_doc[r]], axis=1)
                    return nt(keys, query), nt(kv[r, :, HEAD_DIM:], grad)

                s_a, dp_a = both(ra)
                s_b, dp_b = both(rb)
                if gi == last:
                    s_0, dp_0 = both(0)
                    s_b = jnp.where(causal, s_0, s_b)
                    dp_b = jnp.where(causal, dp_0, dp_b)
                s = jnp.concatenate([s_a, s_b], axis=0)
                dp = jnp.concatenate([dp_a, dp_b], axis=0)
                top = jnp.max(s, axis=0, keepdims=True)
                p = jnp.exp2(s * TO_EXP2 - top * TO_EXP2)
                probs[gi, j] = p.astype(BF16)
                dprobs[gi, j] = dp
                at = pl.ds(j, 1)
                st_m[gi, at, :] = top * TO_EXP2
                st_l[gi, at, :] = jnp.sum(p, axis=0, keepdims=True)
                st_d[gi, at, :] = jnp.sum(p * dp, axis=0, keepdims=True)
            return carry

        lax.fori_loop(0, heads // HEADS_STEP, body, 0)

    heads_chunk = GROUP_Q // IN_CHUNKS
    for gi in range(len(groups)):
        r = groups[gi][1]
        rail_send(r - 2).wait_recv()
        pass_on(r)
        sib_send(0, gi).wait_recv()
        if gi == 0:
            for chunk in range(IN_CHUNKS):
                arrived(1 + 2 * chunk)
                arrived(2 + 2 * chunk)
                forward(0, chunk * heads_chunk, heads_chunk)
        else:
            forward(gi, 0, GROUP_Q)

    top = jnp.maximum(jnp.maximum(st_m[0], st_m[1]), st_m[2])
    factors = [jnp.exp2(st_m[gi] - top) for gi in range(len(groups))]
    inverse = 1.0 / sum(factors[gi] * st_l[gi] for gi in range(len(groups)))
    row_delta = jnp.zeros_like(inverse)
    for gi in range(len(groups)):
        gain[gi] = factors[gi] * inverse
        row_delta = row_delta + factors[gi] * inverse * st_d[gi]
    delta[...] = row_delta

    def out_send(first, size, peer):
        cols = pl.ds(first if isinstance(first, int) else pl.multiple_of(first, HEAD_DIM), size)
        return pltpu.make_async_remote_copy(
            src_ref=stage.at[pl.ds(pl.multiple_of(peer * rows, rows), rows), cols],
            dst_ref=out_ref.at[:, column(me, first, size)],
            send_sem=s_out, recv_sem=r_out,
            device_id={"head": peer}, device_id_type=MESH)

    def backward(gi, first_step, steps):
        ra, rb = groups[gi]
        final = gi == 0

        def body(step, carry):
            p_all, ds_all, grad_all, query_all = [], [], [], []
            for u in range(HEADS_STEP):
                j = step * HEADS_STEP + u
                cols = pl.ds(pl.multiple_of(j * HEAD_DIM, HEAD_DIM), HEAD_DIM)
                at = pl.ds(j, 1)
                p = probs[gi, j].astype(F32) * gain[gi, at, :]
                ds = p * (dprobs[gi, j] - delta[at, :])
                if gi == last:
                    p_c, ds_c = p[piece:], ds[piece:]
                    p = jnp.concatenate([p[:piece], jnp.where(causal, 0.0, p_c),
                                         jnp.where(causal, p_c, 0.0)], axis=0)
                    ds = jnp.concatenate([ds[:piece], jnp.where(causal, 0.0, ds_c),
                                          jnp.where(causal, ds_c, 0.0)], axis=0)
                    keys = jnp.concatenate([kv[ra, :, :HEAD_DIM], kv[rb, :, :HEAD_DIM],
                                            kv[0, :, :HEAD_DIM]], axis=0)
                else:
                    keys = jnp.concatenate([kv[ra, :, :HEAD_DIM], kv[rb, :, :HEAD_DIM]], axis=0)
                p = p.astype(BF16)
                ds = ds.astype(BF16)
                p_all.append(p)
                ds_all.append(ds)
                grad_all.append(dob[:, cols])
                query_all.append(qb[:, cols])
                grad_query = tn(ds, keys)
                if gi != last:
                    grad_query = grad_query + dq[j]
                if final:
                    stage[:, cols] = (grad_query * SCALE).astype(BF16)
                else:
                    dq[j] = grad_query
            p = jnp.concatenate(p_all, axis=1)
            ds = jnp.concatenate(ds_all, axis=1)
            grad_value = nn(p, jnp.concatenate(grad_all, axis=0))
            grad_key = nn(ds, jnp.concatenate(query_all, axis=0))
            for i in range(2):
                at = pl.ds(i * piece, piece)
                part[i, :, :HEAD_DIM] += grad_key[i * piece:(i + 1) * piece]
                part[i, :, HEAD_DIM:] += grad_value[i * piece:(i + 1) * piece]
            if gi == last:
                home[:, :HEAD_DIM] += grad_key[2 * piece:]
                home[:, HEAD_DIM:] += grad_value[2 * piece:]
            if final:
                first = step * HEADS_STEP * HEAD_DIM
                for peer in peers:
                    out_send(first, HEADS_STEP * HEAD_DIM, peer).start()
            return carry

        lax.fori_loop(first_step, first_step + steps, body, 0)

    def grail(r):
        return ctx_copy(rail_out.at[r // 2 - 1], rail_in.at[r // 2 - 1],
                        s_grail.at[r // 2 - 1], r_grail.at[r // 2 - 1], before)

    def gsib(j):
        return ctx_copy(odd_out.at[j], odd_in.at[j], s_gsib.at[j], r_gsib.at[j], sib)

    def key_scale():
        which = lax.broadcasted_iota(jnp.int32, (1, 2 * HEAD_DIM), 1)
        return jnp.where(which < HEAD_DIM, SCALE, 1.0)

    home[...] = jnp.zeros_like(home)
    for gi in range(last, -1, -1):
        ra, rb = groups[gi]
        j = ra // 2
        part[...] = jnp.zeros_like(part)
        backward(gi, 0, GROUP_Q // HEADS_STEP)
        odd_out[j] = (part[0] * key_scale()).astype(BF16)
        gsib(j).start()
        part[1] = part[1] * key_scale()
        if gi < last:
            grail(rb + 2).wait_recv()
            part[1] += rail_in[rb // 2].astype(F32)

            @pl.when(core == 0)
            def _():
                gsib(j + 1).wait_recv()
                part[1] += odd_in[j + 1].astype(F32)

        @pl.when(core == 1)
        def _():
            gsib(j).wait_recv()
            part[1] += odd_in[j].astype(F32)

        rail_out[rb // 2 - 1] = part[1].astype(BF16)
        grail(rb).start()

    home[...] = home[...] * key_scale()

    @pl.when(core == 0)
    def _():
        gsib(0).wait_recv()
        home[...] += odd_in[0].astype(F32)

    grail(2).wait_recv()
    own = home[...] + rail_in[0].astype(F32)
    stage[:, q_width:] = own.astype(BF16)
    for peer in peers:
        out_send(q_width, 2 * HEAD_DIM, peer).start()
    mine = pltpu.make_async_copy(stage.at[my_rows, :], out_ref.at[:, column(me, 0, width)], l_out)
    mine.start()

    for i, (src, src_cols, dst, dst_cols) in enumerate(sends):
        wait_bytes(dst.at[pl.ds(0, rows * (n_head - 1)), dst_cols], s_in.at[i])
    for j in range(len(groups)):
        rail_send(2 * j).wait_send()
        sib_send(0, j).wait_send()
        gsib(j).wait_send()
        grail(2 * j + 2).wait_send()
    mine.wait()
    wait_bytes(out_ref.at[:, pl.ds(0, width * (n_head - 1))], s_out)
    wait_bytes(out_ref.at[:, pl.ds(0, width * (n_head - 1))], r_out)


def per_device(n_head, n_ctx, merged_qkv, out_grads, doc_lengths):
    rows = merged_qkv.shape[0]
    piece = rows * n_head
    n_groups = REACH // 2
    pair = 2 * HEAD_DIM
    dma = pltpu.SemaphoreType.DMA
    n_in = 1 + 2 * IN_CHUNKS
    macs = 5 * GROUP_Q * piece * (REACH + 1) * piece * HEAD_DIM
    return pl.pallas_call(
        functools.partial(kernel, n_head, n_ctx),
        out_shape=jax.ShapeDtypeStruct(merged_qkv.shape, BF16),
        in_specs=[pl.BlockSpec(memory_space=pltpu.SMEM), pl.BlockSpec(memory_space=pl.ANY),
                  pl.BlockSpec(memory_space=pl.ANY)],
        out_specs=pl.BlockSpec(memory_space=pltpu.VMEM),
        scratch_shapes=[
            pltpu.VMEM((REACH + 1, piece, pair), BF16),
            pltpu.VMEM((REACH + 1, piece, HEAD_DIM), BF16),
            pltpu.VMEM((piece, HEAD_DIM), BF16),
            pltpu.VMEM((piece, GROUP_Q * HEAD_DIM), BF16),
            pltpu.VMEM((piece, GROUP_Q * HEAD_DIM), BF16),
            pltpu.VMEM((n_groups, GROUP_Q, 2 * piece, piece), BF16),
            pltpu.VMEM((n_groups, GROUP_Q, 2 * piece, piece), F32),
            pltpu.VMEM((n_groups, GROUP_Q, piece), F32),
            pltpu.VMEM((n_groups, GROUP_Q, piece), F32),
            pltpu.VMEM((n_groups, GROUP_Q, piece), F32),
            pltpu.VMEM((n_groups, GROUP_Q, piece), F32),
            pltpu.VMEM((GROUP_Q, piece), F32),
            pltpu.VMEM((GROUP_Q, piece, HEAD_DIM), F32),
            pltpu.VMEM((piece, pair), F32),
            pltpu.VMEM((2, piece, pair), F32),
            pltpu.VMEM((n_groups, piece, pair), BF16),
            pltpu.VMEM((n_groups, piece, pair), BF16),
            pltpu.VMEM((n_groups, piece, pair), BF16),
            pltpu.VMEM((n_groups, piece, pair), BF16),
            pltpu.VMEM((piece, (GROUP_Q + 2) * HEAD_DIM), BF16),
            dma((n_in,)), dma((n_in,)), dma((n_in,)),
            dma((n_groups,)), dma((n_groups,)), dma((n_groups,)), dma((n_groups,)),
            dma((n_groups,)), dma((n_groups,)), dma((n_groups,)), dma((n_groups,)),
            dma, dma, dma,
        ],
        compiler_params=pltpu.CompilerParams(
            collective_id=0, has_side_effects=True, vmem_limit_bytes=56 * 1024 * 1024),
        cost_estimate=pl.CostEstimate(
            flops=2 * macs, bytes_accessed=4 * merged_qkv.size * 2,
            transcendentals=GROUP_Q * piece * piece * REACH),
    )(doc_lengths, merged_qkv, out_grads)


def solution(mesh):
    placed = (P(("ctx", "head"), None), P(("ctx", "head"), None), P())
    body = functools.partial(per_device, mesh.shape["head"], mesh.shape["ctx"])
    return jax.shard_map(
        body, mesh=mesh, in_specs=placed, out_specs=P(("ctx", "head"), None), check_vma=False
    )
```

```python
import functools
import math

import jax
import jax.numpy as jnp
from jax import lax
from jax.experimental import pallas as pl
from jax.experimental.pallas import tpu as pltpu
from jax.sharding import PartitionSpec as P

GROUP_Q = 8
HEAD_DIM = 128
REACH = 6
MESH = pl.DeviceIdType.MESH
SCALE = HEAD_DIM ** -0.5
TO_EXP2 = SCALE * math.log2(math.e)
FAR = 2.0 ** 100
F32, BF16 = jnp.float32, jnp.bfloat16
IN_CHUNKS = 4
HEADS_STEP = 2
Z_CHIPS = 8


def nt(a, b):
    return lax.dot_general(a, b, (((1,), (1,)), ((), ())), preferred_element_type=F32)


def nn(a, b):
    return lax.dot_general(a, b, (((1,), (0,)), ((), ())), preferred_element_type=F32)


def tn(a, b):
    return lax.dot_general(a, b, (((0,), (0,)), ((), ())), preferred_element_type=F32)


def wait_bytes(ref, sem):
    pltpu.make_async_copy(ref, ref, sem).wait()


def kernel(n_head, n_ctx, lens_ref, qkv_ref, grads_ref, out_ref,
           kv, key_doc, query_doc, qb, dob, probs, dprobs, st_m, st_l, st_d, gain, delta,
           dq, home, part, even, relay_kv, relay_grads, odd_out, odd_in, rail_out, rail_in, stage,
           s_in, r_in, l_in, s_rail, r_rail, s_relay, r_relay, s_back, r_back, s_sib, r_sib, s_grail, r_grail, s_gsib, r_gsib,
           s_out, r_out, l_out):
    rows = qkv_ref.shape[0]
    piece = kv.shape[1]
    width = (GROUP_Q + 2) * HEAD_DIM
    q_width = GROUP_Q * HEAD_DIM
    me = lax.axis_index("head")
    ctx = lax.axis_index("ctx")
    core = lax.rem(ctx, 2)
    sib = ctx + 1 - 2 * core
    z = lax.rem(ctx // 2, Z_CHIPS)
    odd_row = lax.rem(me, 2) == 1
    starts_run, ends_run = z == 0, z == Z_CHIPS - 1
    relays = (odd_row & starts_run) | (jnp.logical_not(odd_row) & ends_run)

    def shifted(steps):
        return lax.rem(ctx + n_ctx + 2 * steps, n_ctx)

    after = jnp.where(ends_run, jnp.where(odd_row, shifted(1 - Z_CHIPS), shifted(Z_CHIPS)), shifted(1))
    before = jnp.where(starts_run, jnp.where(odd_row, shifted(-Z_CHIPS), shifted(Z_CHIPS - 1)), shifted(-1))
    relay_from = jnp.where(odd_row, shifted(Z_CHIPS - 1), shifted(-Z_CHIPS))
    relay_to = jnp.where(odd_row, shifted(Z_CHIPS), shifted(1 - Z_CHIPS))
    peers = [lax.rem(me + p, n_head) for p in range(1, n_head)]

    barrier = pltpu.get_barrier_semaphore()

    def greet(axis, other):
        pl.semaphore_signal(barrier, inc=1, device_id={axis: other}, device_id_type=MESH)

    for peer in peers:
        greet("head", peer)
    for other in (sib, after, before):
        greet("ctx", other)

    @pl.when(relays)
    def _():
        greet("ctx", relay_from)
        greet("ctx", relay_to)

    pl.semaphore_wait(barrier, jnp.where(relays, len(peers) + 5, len(peers) + 3))

    my_rows = pl.ds(pl.multiple_of(me * rows, rows), rows)

    def column(group, first, size):
        return pl.ds(pl.multiple_of(group * width + first, HEAD_DIM), size)

    def grad_column(group, first, size):
        return pl.ds(pl.multiple_of(group * q_width + first, HEAD_DIM), size)

    step_w = q_width // IN_CHUNKS
    others = pl.ds(0, rows * (n_head - 1))

    def sends(chunk):
        if chunk is None:
            return [(qkv_ref, lambda g: column(g, q_width, 2 * HEAD_DIM), kv.at[0],
                     pl.ds(0, 2 * HEAD_DIM), 0)]
        first = chunk * step_w
        cols = pl.ds(pl.multiple_of(first, HEAD_DIM), step_w)
        return [(qkv_ref, lambda g: column(g, first, step_w), qb, cols, 1 + 2 * chunk),
                (grads_ref, lambda g: grad_column(g, first, step_w), dob, cols, 2 + 2 * chunk)]

    def send_part(chunk):
        for src, src_cols, dst, dst_cols, i in sends(chunk):
            for peer in peers:
                pltpu.make_async_remote_copy(
                    src_ref=src.at[:, src_cols(peer)], dst_ref=dst.at[my_rows, dst_cols],
                    send_sem=s_in.at[i], recv_sem=r_in.at[i],
                    device_id={"head": peer}, device_id_type=MESH).start()
            pltpu.make_async_copy(
                src.at[:, src_cols(me)], dst.at[my_rows, dst_cols], l_in.at[i]).start()

    def arrived(chunk):
        for src, src_cols, dst, dst_cols, i in sends(chunk):
            pltpu.make_async_copy(
                src.at[:, src_cols(me)], dst.at[my_rows, dst_cols], l_in.at[i]).wait()
            wait_bytes(dst.at[others, dst_cols], r_in.at[i])

    def all_sent(chunk):
        for src, src_cols, dst, dst_cols, i in sends(chunk):
            wait_bytes(dst.at[others, dst_cols], s_in.at[i])

    def chunks(first, body):
        def step(chunk, carry):
            body(chunk)
            return carry

        lax.fori_loop(first, IN_CHUNKS, step, 0)

    send_part(None)
    send_part(0)

    def ctx_copy(src, dst, send_sem, recv_sem, device):
        return pltpu.make_async_remote_copy(
            src_ref=src, dst_ref=dst, send_sem=send_sem, recv_sem=recv_sem,
            device_id={"ctx": device}, device_id_type=MESH)

    lane = lax.broadcasted_iota(jnp.int32, (1, HEAD_DIM), 1)
    starts = jnp.full((1, HEAD_DIM), 1 << 20, jnp.int32)
    ends = jnp.full((1, HEAD_DIM), 1 << 20, jnp.int32)
    total = jnp.int32(0)
    for d in range(lens_ref.shape[0]):
        starts = jnp.where(lane == d, total, starts)
        total = total + lens_ref[d]
        ends = jnp.where(lane == d, total, ends)
    row_of = lax.broadcasted_iota(jnp.int32, (piece, HEAD_DIM), 0)
    lane_of = lax.broadcasted_iota(jnp.int32, (piece, HEAD_DIM), 1)
    for r in range(REACH + 1):
        pos = row_of + (ctx - r) * piece
        inside = ((starts <= pos) & (pos < ends)) | ((lane_of == HEAD_DIM - 1) & (pos < 0))
        key_doc[r] = jnp.where(inside, 1.0, 0.0).astype(BF16)
        if r == 0:
            query_doc[...] = jnp.where(inside, 0.0, -FAR).astype(BF16)
    causal = (lax.broadcasted_iota(jnp.int32, (piece, piece), 0)
              <= lax.broadcasted_iota(jnp.int32, (piece, piece), 1))

    def rail_send(r):
        return ctx_copy(kv.at[r], kv.at[r + 2], s_rail.at[r // 2], r_rail.at[r // 2], after)

    def hand_over(r):
        return ctx_copy(kv.at[r], relay_kv.at[r // 2], s_rail.at[r // 2], r_relay.at[r // 2], after)

    def relay_send(r):
        return ctx_copy(relay_kv.at[r // 2], kv.at[r + 2], s_relay.at[r // 2], r_rail.at[r // 2],
                        relay_to)

    def sib_send(k, j):
        return ctx_copy(kv.at[2 * j + 2 * k], kv.at[2 * j + 1], s_sib.at[j], r_sib.at[j], sib)

    def pass_on(r):
        if r < REACH:

            @pl.when(ends_run)
            def _():
                hand_over(r).start()

            @pl.when(jnp.logical_not(ends_run))
            def _():
                rail_send(r).start()

            @pl.when(core == 0)
            def _():
                sib_send(0, r // 2).start()
        if r > 0:

            @pl.when(core == 1)
            def _():
                sib_send(1, r // 2 - 1).start()

    def relay(r):
        @pl.when(relays)
        def _():
            hand_over(r).wait_recv()
            relay_send(r).start()

    arrived(None)
    pass_on(0)
    chunks(1, send_part)

    groups = ((1, 2), (3, 4), (5, 6))
    last = len(groups) - 1

    def forward(gi, first_head, heads):
        ra, rb = groups[gi]

        def body(step, carry):
            for u in range(HEADS_STEP):
                j = first_head + step * HEADS_STEP + u
                cols = pl.ds(pl.multiple_of(j * HEAD_DIM, HEAD_DIM), HEAD_DIM)
                query = jnp.concatenate([qb[:, cols], query_doc[...]], axis=1)
                grad = dob[:, cols]

                blocks = (ra, rb, 0) if gi == last else (ra, rb)
                keys = jnp.concatenate(
                    [jnp.concatenate([kv[r, :, :HEAD_DIM], key_doc[r]], axis=1) for r in blocks], axis=0)
                values = jnp.concatenate([kv[r, :, HEAD_DIM:] for r in blocks], axis=0)
                s = nt(keys, query)
                dp = nt(values, grad)
                if gi == last:
                    s, dp = (jnp.concatenate(
                        [a[:piece], jnp.where(causal, a[2 * piece:], a[piece:2 * piece])], axis=0)
                        for a in (s, dp))
                top = jnp.max(s, axis=0, keepdims=True)
                p = jnp.exp2(s * TO_EXP2 - top * TO_EXP2)
                probs[gi, j] = p.astype(BF16)
                dprobs[gi, j] = dp
                at = pl.ds(j, 1)
                st_m[gi, at, :] = top * TO_EXP2
                st_l[gi, at, :] = jnp.sum(p, axis=0, keepdims=True)
                st_d[gi, at, :] = jnp.sum(p * dp, axis=0, keepdims=True)
            return carry

        lax.fori_loop(0, heads // HEADS_STEP, body, 0)

    heads_chunk = GROUP_Q // IN_CHUNKS
    for gi in range(len(groups)):
        r = groups[gi][1]
        relay(r - 2)
        rail_send(r - 2).wait_recv()
        pass_on(r)
        sib_send(0, gi).wait_recv()
        if gi == 0:
            arrived(0)
        forward(gi, 0, heads_chunk)

    def forward_chunk(chunk):
        arrived(chunk)
        for gi in range(len(groups)):
            forward(gi, chunk * heads_chunk, heads_chunk)

    chunks(1, forward_chunk)

    top = jnp.maximum(jnp.maximum(st_m[0], st_m[1]), st_m[2])
    factors = [jnp.exp2(st_m[gi] - top) for gi in range(len(groups))]
    inverse = 1.0 / sum(factors[gi] * st_l[gi] for gi in range(len(groups)))
    row_delta = jnp.zeros_like(inverse)
    for gi in range(len(groups)):
        gain[gi] = factors[gi] * inverse
        row_delta = row_delta + factors[gi] * inverse * st_d[gi]
    delta[...] = row_delta

    def out_send(first, size, peer):
        cols = pl.ds(first if isinstance(first, int) else pl.multiple_of(first, HEAD_DIM), size)
        return pltpu.make_async_remote_copy(
            src_ref=stage.at[pl.ds(pl.multiple_of(peer * rows, rows), rows), cols],
            dst_ref=out_ref.at[:, column(me, first, size)],
            send_sem=s_out, recv_sem=r_out,
            device_id={"head": peer}, device_id_type=MESH)

    def backward(gi):
        ra, rb = groups[gi]
        final = gi == 0

        def body(step, carry):
            if gi < last:

                @pl.when(step == 1)
                def _():
                    send_sum(gi + 1)

                @pl.when(step == 3)
                def _():
                    relay_back(groups[gi + 1][1])

            p_all, ds_all, grad_all, query_all = [], [], [], []
            for u in range(HEADS_STEP):
                j = step * HEADS_STEP + u
                cols = pl.ds(pl.multiple_of(j * HEAD_DIM, HEAD_DIM), HEAD_DIM)
                at = pl.ds(j, 1)
                p = probs[gi, j].astype(F32) * gain[gi, at, :]
                ds = p * (dprobs[gi, j] - delta[at, :])
                if gi == last:
                    p_c, ds_c = p[piece:], ds[piece:]
                    p = jnp.concatenate([p[:piece], jnp.where(causal, 0.0, p_c),
                                         jnp.where(causal, p_c, 0.0)], axis=0)
                    ds = jnp.concatenate([ds[:piece], jnp.where(causal, 0.0, ds_c),
                                          jnp.where(causal, ds_c, 0.0)], axis=0)
                    keys = jnp.concatenate([kv[ra, :, :HEAD_DIM], kv[rb, :, :HEAD_DIM],
                                            kv[0, :, :HEAD_DIM]], axis=0)
                else:
                    keys = jnp.concatenate([kv[ra, :, :HEAD_DIM], kv[rb, :, :HEAD_DIM]], axis=0)
                p = p.astype(BF16)
                ds = ds.astype(BF16)
                p_all.append(p)
                ds_all.append(ds)
                grad_all.append(dob[:, cols])
                query_all.append(qb[:, cols])
                grad_query = tn(ds, keys)
                if gi != last:
                    grad_query = grad_query + dq[j]
                if final:
                    stage[:, cols] = (grad_query * SCALE).astype(BF16)
                else:
                    dq[j] = grad_query
            p = jnp.concatenate(p_all, axis=1)
            ds = jnp.concatenate(ds_all, axis=1)
            grad_value = nn(p, jnp.concatenate(grad_all, axis=0))
            grad_key = nn(ds, jnp.concatenate(query_all, axis=0))
            for i in range(2):
                at = pl.ds(i * piece, piece)
                part[i, :, :HEAD_DIM] += grad_key[i * piece:(i + 1) * piece]
                part[i, :, HEAD_DIM:] += grad_value[i * piece:(i + 1) * piece]
            if gi == last:
                home[:, :HEAD_DIM] += grad_key[2 * piece:]
                home[:, HEAD_DIM:] += grad_value[2 * piece:]
            if final:
                first = step * HEADS_STEP * HEAD_DIM
                for peer in peers:
                    out_send(first, HEADS_STEP * HEAD_DIM, peer).start()
            return carry

        lax.fori_loop(0, GROUP_Q // HEADS_STEP, body, 0)

    def grail(r):
        i = r // 2 - 1
        return ctx_copy(rail_out.at[i], rail_in.at[i], s_grail.at[i], r_grail.at[i], before)

    def grail_over(r):
        i = r // 2 - 1
        return ctx_copy(rail_out.at[i], relay_grads.at[i], s_grail.at[i], r_back.at[i], before)

    def grail_relay(r):
        i = r // 2 - 1
        return ctx_copy(relay_grads.at[i], rail_in.at[i], s_back.at[i], r_grail.at[i], relay_from)

    def relay_back(r):
        @pl.when(relays)
        def _():
            grail_over(r).wait_recv()
            grail_relay(r).start()

    def gsib(j):
        return ctx_copy(odd_out.at[j], odd_in.at[j], s_gsib.at[j], r_gsib.at[j], sib)

    def key_scale():
        which = lax.broadcasted_iota(jnp.int32, (1, 2 * HEAD_DIM), 1)
        return jnp.where(which < HEAD_DIM, SCALE, 1.0)

    def send_sum(gi):
        rb, j = groups[gi][1], gi
        if gi < last:
            grail(rb + 2).wait_recv()
            even[...] += rail_in[rb // 2].astype(F32)

            @pl.when(core == 0)
            def _():
                gsib(j + 1).wait_recv()
                even[...] += odd_in[j + 1].astype(F32)

        @pl.when(core == 1)
        def _():
            gsib(j).wait_recv()
            even[...] += odd_in[j].astype(F32)

        rail_out[rb // 2 - 1] = even[...].astype(BF16)

        @pl.when(starts_run)
        def _():
            grail_over(rb).start()

        @pl.when(jnp.logical_not(starts_run))
        def _():
            grail(rb).start()

    home[...] = jnp.zeros_like(home)
    for gi in range(last, -1, -1):
        part[...] = jnp.zeros_like(part)
        backward(gi)
        odd_out[gi] = (part[0] * key_scale()).astype(BF16)
        gsib(gi).start()
        even[...] = part[1] * key_scale()
    send_sum(0)
    relay_back(groups[0][1])

    home[...] = home[...] * key_scale()

    @pl.when(core == 0)
    def _():
        gsib(0).wait_recv()
        home[...] += odd_in[0].astype(F32)

    grail(2).wait_recv()
    own = home[...] + rail_in[0].astype(F32)
    stage[:, q_width:] = own.astype(BF16)
    for peer in peers:
        out_send(q_width, 2 * HEAD_DIM, peer).start()
    mine = pltpu.make_async_copy(stage.at[my_rows, :], out_ref.at[:, column(me, 0, width)], l_out)
    mine.start()

    all_sent(None)
    chunks(0, all_sent)
    for j in range(len(groups)):
        rail_send(2 * j).wait_send()

        @pl.when(relays)
        def _():
            relay_send(2 * j).wait_send()
            grail_relay(2 * j + 2).wait_send()

        sib_send(0, j).wait_send()
        gsib(j).wait_send()
        grail(2 * j + 2).wait_send()
    mine.wait()
    wait_bytes(out_ref.at[:, pl.ds(0, width * (n_head - 1))], s_out)
    wait_bytes(out_ref.at[:, pl.ds(0, width * (n_head - 1))], r_out)


def per_device(n_head, n_ctx, merged_qkv, out_grads, doc_lengths):
    rows = merged_qkv.shape[0]
    piece = rows * n_head
    n_groups = REACH // 2
    pair = 2 * HEAD_DIM
    dma = pltpu.SemaphoreType.DMA
    n_in = 1 + 2 * IN_CHUNKS
    macs = 5 * GROUP_Q * piece * (REACH + 1) * piece * HEAD_DIM
    return pl.pallas_call(
        functools.partial(kernel, n_head, n_ctx),
        out_shape=jax.ShapeDtypeStruct(merged_qkv.shape, BF16),
        in_specs=[pl.BlockSpec(memory_space=pltpu.SMEM), pl.BlockSpec(memory_space=pl.ANY),
                  pl.BlockSpec(memory_space=pl.ANY)],
        out_specs=pl.BlockSpec(memory_space=pltpu.VMEM),
        scratch_shapes=[
            pltpu.VMEM((REACH + 1, piece, pair), BF16),
            pltpu.VMEM((REACH + 1, piece, HEAD_DIM), BF16),
            pltpu.VMEM((piece, HEAD_DIM), BF16),
            pltpu.VMEM((piece, GROUP_Q * HEAD_DIM), BF16),
            pltpu.VMEM((piece, GROUP_Q * HEAD_DIM), BF16),
            pltpu.VMEM((n_groups, GROUP_Q, 2 * piece, piece), BF16),
            pltpu.VMEM((n_groups, GROUP_Q, 2 * piece, piece), F32),
            pltpu.VMEM((n_groups, GROUP_Q, piece), F32),
            pltpu.VMEM((n_groups, GROUP_Q, piece), F32),
            pltpu.VMEM((n_groups, GROUP_Q, piece), F32),
            pltpu.VMEM((n_groups, GROUP_Q, piece), F32),
            pltpu.VMEM((GROUP_Q, piece), F32),
            pltpu.VMEM((GROUP_Q, piece, HEAD_DIM), F32),
            pltpu.VMEM((piece, pair), F32),
            pltpu.VMEM((2, piece, pair), F32),
            pltpu.VMEM((piece, pair), F32),
            pltpu.VMEM((n_groups, piece, pair), BF16),
            pltpu.VMEM((n_groups, piece, pair), BF16),
            pltpu.VMEM((n_groups, piece, pair), BF16),
            pltpu.VMEM((n_groups, piece, pair), BF16),
            pltpu.VMEM((n_groups, piece, pair), BF16),
            pltpu.VMEM((n_groups, piece, pair), BF16),
            pltpu.VMEM((piece, (GROUP_Q + 2) * HEAD_DIM), BF16),
            dma((n_in,)), dma((n_in,)), dma((n_in,)),
            dma((n_groups,)), dma((n_groups,)), dma((n_groups,)), dma((n_groups,)),
            dma((n_groups,)), dma((n_groups,)),
            dma((n_groups,)), dma((n_groups,)), dma((n_groups,)), dma((n_groups,)),
            dma((n_groups,)), dma((n_groups,)),
            dma, dma, dma,
        ],
        compiler_params=pltpu.CompilerParams(
            collective_id=0, has_side_effects=True, vmem_limit_bytes=56 * 1024 * 1024),
        cost_estimate=pl.CostEstimate(
            flops=2 * macs, bytes_accessed=4 * merged_qkv.size * 2,
            transcendentals=GROUP_Q * piece * piece * REACH),
    )(doc_lengths, merged_qkv, out_grads)


def solution(mesh):
    placed = (P(("ctx", "head"), None), P(("ctx", "head"), None), P())
    body = functools.partial(per_device, mesh.shape["head"], mesh.shape["ctx"])
    return jax.shard_map(
        body, mesh=mesh, in_specs=placed, out_specs=P(("ctx", "head"), None), check_vma=False
    )
```

```python
import functools
import math

import jax
import jax.numpy as jnp
from jax import lax
from jax.experimental import pallas as pl
from jax.experimental.pallas import tpu as pltpu
from jax.sharding import PartitionSpec as P

GROUP_Q = 8
HEAD_DIM = 128
REACH = 6
MESH = pl.DeviceIdType.MESH
SCALE = HEAD_DIM ** -0.5
TO_EXP2 = SCALE * math.log2(math.e)
FAR = 2.0 ** 100
F32, BF16 = jnp.float32, jnp.bfloat16
IN_CHUNKS = 4
HEADS_STEP = 2
Z_CHIPS = 8


def nt(a, b):
    return lax.dot_general(a, b, (((1,), (1,)), ((), ())), preferred_element_type=F32)


def nn(a, b):
    return lax.dot_general(a, b, (((1,), (0,)), ((), ())), preferred_element_type=F32)


def tn(a, b):
    return lax.dot_general(a, b, (((0,), (0,)), ((), ())), preferred_element_type=F32)


def wait_bytes(ref, sem):
    pltpu.make_async_copy(ref, ref, sem).wait()


def kernel(n_head, n_ctx, lens_ref, qkv_ref, grads_ref, out_ref,
           kv, key_doc, query_doc, qb, dob, probs, dprobs, st_m, st_l, st_d, gain, delta,
           dq, home, part, even, relay_kv, relay_grads, odd_out, odd_in, rail_out, rail_in, stage,
           s_in, r_in, l_in, s_rail, r_rail, s_relay, r_relay, s_back, r_back, s_sib, r_sib, s_grail, r_grail, s_gsib, r_gsib,
           s_out, r_out, l_out):
    rows = qkv_ref.shape[0]
    piece = kv.shape[1]
    width = (GROUP_Q + 2) * HEAD_DIM
    q_width = GROUP_Q * HEAD_DIM
    me = lax.axis_index("head")
    ctx = lax.axis_index("ctx")
    core = lax.rem(ctx, 2)
    sib = ctx + 1 - 2 * core
    z = lax.rem(ctx // 2, Z_CHIPS)
    odd_row = lax.rem(me, 2) == 1
    starts_run, ends_run = z == 0, z == Z_CHIPS - 1
    relays = (odd_row & starts_run) | (jnp.logical_not(odd_row) & ends_run)

    def shifted(steps):
        return lax.rem(ctx + n_ctx + 2 * steps, n_ctx)

    after = jnp.where(ends_run, jnp.where(odd_row, shifted(1 - Z_CHIPS), shifted(Z_CHIPS)), shifted(1))
    before = jnp.where(starts_run, jnp.where(odd_row, shifted(-Z_CHIPS), shifted(Z_CHIPS - 1)), shifted(-1))
    relay_from = jnp.where(odd_row, shifted(Z_CHIPS - 1), shifted(-Z_CHIPS))
    relay_to = jnp.where(odd_row, shifted(Z_CHIPS), shifted(1 - Z_CHIPS))
    peers = [lax.rem(me + p, n_head) for p in range(1, n_head)]

    barrier = pltpu.get_barrier_semaphore()

    def greet(axis, other):
        pl.semaphore_signal(barrier, inc=1, device_id={axis: other}, device_id_type=MESH)

    for peer in peers:
        greet("head", peer)
    for other in (sib, after, before):
        greet("ctx", other)

    @pl.when(relays)
    def _():
        greet("ctx", relay_from)
        greet("ctx", relay_to)

    pl.semaphore_wait(barrier, jnp.where(relays, len(peers) + 5, len(peers) + 3))

    my_rows = pl.ds(pl.multiple_of(me * rows, rows), rows)

    def column(group, first, size):
        return pl.ds(pl.multiple_of(group * width + first, HEAD_DIM), size)

    def grad_column(group, first, size):
        return pl.ds(pl.multiple_of(group * q_width + first, HEAD_DIM), size)

    step_w = q_width // IN_CHUNKS
    others = pl.ds(0, rows * (n_head - 1))

    def sends(chunk):
        if chunk is None:
            return [(qkv_ref, lambda g: column(g, q_width, 2 * HEAD_DIM), kv.at[0],
                     pl.ds(0, 2 * HEAD_DIM), 0)]
        first = chunk * step_w
        cols = pl.ds(pl.multiple_of(first, HEAD_DIM), step_w)
        return [(qkv_ref, lambda g: column(g, first, step_w), qb, cols, 1 + 2 * chunk),
                (grads_ref, lambda g: grad_column(g, first, step_w), dob, cols, 2 + 2 * chunk)]

    def send_part(chunk):
        for src, src_cols, dst, dst_cols, i in sends(chunk):
            for peer in peers:
                pltpu.make_async_remote_copy(
                    src_ref=src.at[:, src_cols(peer)], dst_ref=dst.at[my_rows, dst_cols],
                    send_sem=s_in.at[i], recv_sem=r_in.at[i],
                    device_id={"head": peer}, device_id_type=MESH).start()
            pltpu.make_async_copy(
                src.at[:, src_cols(me)], dst.at[my_rows, dst_cols], l_in.at[i]).start()

    def arrived(chunk):
        for src, src_cols, dst, dst_cols, i in sends(chunk):
            pltpu.make_async_copy(
                src.at[:, src_cols(me)], dst.at[my_rows, dst_cols], l_in.at[i]).wait()
            wait_bytes(dst.at[others, dst_cols], r_in.at[i])

    def all_sent(chunk):
        for src, src_cols, dst, dst_cols, i in sends(chunk):
            wait_bytes(dst.at[others, dst_cols], s_in.at[i])

    def chunks(first, body):
        def step(chunk, carry):
            body(chunk)
            return carry

        lax.fori_loop(first, IN_CHUNKS, step, 0)

    send_part(None)

    def ctx_copy(src, dst, send_sem, recv_sem, device):
        return pltpu.make_async_remote_copy(
            src_ref=src, dst_ref=dst, send_sem=send_sem, recv_sem=recv_sem,
            device_id={"ctx": device}, device_id_type=MESH)

    lane = lax.broadcasted_iota(jnp.int32, (1, HEAD_DIM), 1)
    starts = jnp.full((1, HEAD_DIM), 1 << 20, jnp.int32)
    ends = jnp.full((1, HEAD_DIM), 1 << 20, jnp.int32)
    total = jnp.int32(0)
    for d in range(lens_ref.shape[0]):
        starts = jnp.where(lane == d, total, starts)
        total = total + lens_ref[d]
        ends = jnp.where(lane == d, total, ends)
    row_of = lax.broadcasted_iota(jnp.int32, (piece, HEAD_DIM), 0)
    lane_of = lax.broadcasted_iota(jnp.int32, (piece, HEAD_DIM), 1)
    for r in range(REACH + 1):
        pos = row_of + (ctx - r) * piece
        inside = ((starts <= pos) & (pos < ends)) | ((lane_of == HEAD_DIM - 1) & (pos < 0))
        key_doc[r] = jnp.where(inside, 1.0, 0.0).astype(BF16)
        if r == 0:
            query_doc[...] = jnp.where(inside, 0.0, -FAR).astype(BF16)
    causal = (lax.broadcasted_iota(jnp.int32, (piece, piece), 0)
              <= lax.broadcasted_iota(jnp.int32, (piece, piece), 1))

    def rail_send(r):
        return ctx_copy(kv.at[r], kv.at[r + 2], s_rail.at[r // 2], r_rail.at[r // 2], after)

    def hand_over(r):
        return ctx_copy(kv.at[r], relay_kv.at[r // 2], s_rail.at[r // 2], r_relay.at[r // 2], after)

    def relay_send(r):
        return ctx_copy(relay_kv.at[r // 2], kv.at[r + 2], s_relay.at[r // 2], r_rail.at[r // 2],
                        relay_to)

    def sib_send(k, j):
        return ctx_copy(kv.at[2 * j + 2 * k], kv.at[2 * j + 1], s_sib.at[j], r_sib.at[j], sib)

    def pass_on(r):
        if r < REACH:

            @pl.when(ends_run)
            def _():
                hand_over(r).start()

            @pl.when(jnp.logical_not(ends_run))
            def _():
                rail_send(r).start()

            @pl.when(core == 0)
            def _():
                sib_send(0, r // 2).start()
        if r > 0:

            @pl.when(core == 1)
            def _():
                sib_send(1, r // 2 - 1).start()

    def relay(r):
        @pl.when(relays)
        def _():
            hand_over(r).wait_recv()
            relay_send(r).start()

    arrived(None)
    pass_on(0)
    send_part(0)

    groups = ((1, 2), (3, 4), (5, 6))
    last = len(groups) - 1

    def forward(gi, first_head, heads):
        ra, rb = groups[gi]

        def body(step, carry):
            for u in range(HEADS_STEP):
                j = first_head + step * HEADS_STEP + u
                cols = pl.ds(pl.multiple_of(j * HEAD_DIM, HEAD_DIM), HEAD_DIM)
                query = jnp.concatenate([qb[:, cols], query_doc[...]], axis=1)
                grad = dob[:, cols]

                blocks = (ra, rb, 0) if gi == last else (ra, rb)
                keys = jnp.concatenate(
                    [jnp.concatenate([kv[r, :, :HEAD_DIM], key_doc[r]], axis=1) for r in blocks], axis=0)
                values = jnp.concatenate([kv[r, :, HEAD_DIM:] for r in blocks], axis=0)
                s = nt(keys, query)
                dp = nt(values, grad)
                if gi == last:
                    s, dp = (jnp.concatenate(
                        [a[:piece], jnp.where(causal, a[2 * piece:], a[piece:2 * piece])], axis=0)
                        for a in (s, dp))
                top = jnp.max(s, axis=0, keepdims=True)
                p = jnp.exp2(s * TO_EXP2 - top * TO_EXP2)
                probs[gi, j] = p.astype(BF16)
                dprobs[gi, j] = dp
                at = pl.ds(j, 1)
                st_m[gi, at, :] = top * TO_EXP2
                st_l[gi, at, :] = jnp.sum(p, axis=0, keepdims=True)
                st_d[gi, at, :] = jnp.sum(p * dp, axis=0, keepdims=True)
            return carry

        lax.fori_loop(0, heads // HEADS_STEP, body, 0)

    heads_chunk = GROUP_Q // IN_CHUNKS
    for gi in range(len(groups)):
        r = groups[gi][1]
        relay(r - 2)
        if gi == last:
            arrived(0)
            for g in range(last):
                sib_send(0, g).wait_recv()
                forward(g, 0, heads_chunk)
        rail_send(r - 2).wait_recv()
        pass_on(r)
        if gi == 0:
            send_part(1)
        elif gi == 1:
            chunks(2, send_part)
    sib_send(0, last).wait_recv()
    forward(last, 0, heads_chunk)

    def forward_chunk(chunk):
        arrived(chunk)
        for gi in range(len(groups)):
            forward(gi, chunk * heads_chunk, heads_chunk)

    chunks(1, forward_chunk)

    top = jnp.maximum(jnp.maximum(st_m[0], st_m[1]), st_m[2])
    factors = [jnp.exp2(st_m[gi] - top) for gi in range(len(groups))]
    inverse = 1.0 / sum(factors[gi] * st_l[gi] for gi in range(len(groups)))
    row_delta = jnp.zeros_like(inverse)
    for gi in range(len(groups)):
        gain[gi] = factors[gi] * inverse
        row_delta = row_delta + factors[gi] * inverse * st_d[gi]
    delta[...] = row_delta

    def out_send(first, size, peer):
        cols = pl.ds(first if isinstance(first, int) else pl.multiple_of(first, HEAD_DIM), size)
        return pltpu.make_async_remote_copy(
            src_ref=stage.at[pl.ds(pl.multiple_of(peer * rows, rows), rows), cols],
            dst_ref=out_ref.at[:, column(me, first, size)],
            send_sem=s_out, recv_sem=r_out,
            device_id={"head": peer}, device_id_type=MESH)

    def backward(gi):
        ra, rb = groups[gi]
        final = gi == 0

        def body(step, carry):
            if gi < last:

                @pl.when(step == 1)
                def _():
                    if final:
                        relay_back(groups[last][1])
                    send_sum(gi + 1)


            p_all, ds_all, grad_all, query_all = [], [], [], []
            for u in range(HEADS_STEP):
                j = step * HEADS_STEP + u
                cols = pl.ds(pl.multiple_of(j * HEAD_DIM, HEAD_DIM), HEAD_DIM)
                at = pl.ds(j, 1)
                p = probs[gi, j].astype(F32) * gain[gi, at, :]
                ds = p * (dprobs[gi, j] - delta[at, :])
                if gi == last:
                    p_c, ds_c = p[piece:], ds[piece:]
                    p = jnp.concatenate([p[:piece], jnp.where(causal, 0.0, p_c),
                                         jnp.where(causal, p_c, 0.0)], axis=0)
                    ds = jnp.concatenate([ds[:piece], jnp.where(causal, 0.0, ds_c),
                                          jnp.where(causal, ds_c, 0.0)], axis=0)
                    keys = jnp.concatenate([kv[ra, :, :HEAD_DIM], kv[rb, :, :HEAD_DIM],
                                            kv[0, :, :HEAD_DIM]], axis=0)
                else:
                    keys = jnp.concatenate([kv[ra, :, :HEAD_DIM], kv[rb, :, :HEAD_DIM]], axis=0)
                p = p.astype(BF16)
                ds = ds.astype(BF16)
                p_all.append(p)
                ds_all.append(ds)
                grad_all.append(dob[:, cols])
                query_all.append(qb[:, cols])
                grad_query = tn(ds, keys)
                if gi != last:
                    grad_query = grad_query + dq[j]
                if final:
                    stage[:, cols] = (grad_query * SCALE).astype(BF16)
                else:
                    dq[j] = grad_query
            p = jnp.concatenate(p_all, axis=1)
            ds = jnp.concatenate(ds_all, axis=1)
            grad_value = nn(p, jnp.concatenate(grad_all, axis=0))
            grad_key = nn(ds, jnp.concatenate(query_all, axis=0))
            for i in range(2):
                at = pl.ds(i * piece, piece)
                part[i, :, :HEAD_DIM] += grad_key[i * piece:(i + 1) * piece]
                part[i, :, HEAD_DIM:] += grad_value[i * piece:(i + 1) * piece]
            if gi == last:
                home[:, :HEAD_DIM] += grad_key[2 * piece:]
                home[:, HEAD_DIM:] += grad_value[2 * piece:]
            if final:
                first = step * HEADS_STEP * HEAD_DIM
                for peer in peers:
                    out_send(first, HEADS_STEP * HEAD_DIM, peer).start()
            return carry

        lax.fori_loop(0, GROUP_Q // HEADS_STEP, body, 0)

    def grail(r):
        i = r // 2 - 1
        return ctx_copy(rail_out.at[i], rail_in.at[i], s_grail.at[i], r_grail.at[i], before)

    def grail_over(r):
        i = r // 2 - 1
        return ctx_copy(rail_out.at[i], relay_grads.at[i], s_grail.at[i], r_back.at[i], before)

    def grail_relay(r):
        i = r // 2 - 1
        return ctx_copy(relay_grads.at[i], rail_in.at[i], s_back.at[i], r_grail.at[i], relay_from)

    def relay_back(r):
        @pl.when(relays)
        def _():
            grail_over(r).wait_recv()
            grail_relay(r).start()

    def gsib(j):
        return ctx_copy(odd_out.at[j], odd_in.at[j], s_gsib.at[j], r_gsib.at[j], sib)

    def key_scale():
        which = lax.broadcasted_iota(jnp.int32, (1, 2 * HEAD_DIM), 1)
        return jnp.where(which < HEAD_DIM, SCALE, 1.0)

    def send_sum(gi):
        rb, j = groups[gi][1], gi
        if gi < last:
            grail(rb + 2).wait_recv()
            even[...] += rail_in[rb // 2].astype(F32)

            @pl.when(core == 0)
            def _():
                gsib(j + 1).wait_recv()
                even[...] += odd_in[j + 1].astype(F32)

        @pl.when(core == 1)
        def _():
            gsib(j).wait_recv()
            even[...] += odd_in[j].astype(F32)

        rail_out[rb // 2 - 1] = even[...].astype(BF16)

        @pl.when(starts_run)
        def _():
            grail_over(rb).start()

        @pl.when(jnp.logical_not(starts_run))
        def _():
            grail(rb).start()

    home[...] = jnp.zeros_like(home)
    for gi in range(last, -1, -1):
        part[...] = jnp.zeros_like(part)
        backward(gi)
        odd_out[gi] = (part[0] * key_scale()).astype(BF16)
        gsib(gi).start()
        even[...] = part[1] * key_scale()
    relay_back(groups[1][1])
    send_sum(0)
    relay_back(groups[0][1])

    home[...] = home[...] * key_scale()

    @pl.when(core == 0)
    def _():
        gsib(0).wait_recv()
        home[...] += odd_in[0].astype(F32)

    grail(2).wait_recv()
    own = home[...] + rail_in[0].astype(F32)
    stage[:, q_width:] = own.astype(BF16)
    for peer in peers:
        out_send(q_width, 2 * HEAD_DIM, peer).start()
    mine = pltpu.make_async_copy(stage.at[my_rows, :], out_ref.at[:, column(me, 0, width)], l_out)
    mine.start()

    all_sent(None)
    chunks(0, all_sent)
    for j in range(len(groups)):
        rail_send(2 * j).wait_send()

        @pl.when(relays)
        def _():
            relay_send(2 * j).wait_send()
            grail_relay(2 * j + 2).wait_send()

        sib_send(0, j).wait_send()
        gsib(j).wait_send()
        grail(2 * j + 2).wait_send()
    mine.wait()
    wait_bytes(out_ref.at[:, pl.ds(0, width * (n_head - 1))], s_out)
    wait_bytes(out_ref.at[:, pl.ds(0, width * (n_head - 1))], r_out)


def per_device(n_head, n_ctx, merged_qkv, out_grads, doc_lengths):
    rows = merged_qkv.shape[0]
    piece = rows * n_head
    n_groups = REACH // 2
    pair = 2 * HEAD_DIM
    dma = pltpu.SemaphoreType.DMA
    n_in = 1 + 2 * IN_CHUNKS
    macs = 5 * GROUP_Q * piece * (REACH + 1) * piece * HEAD_DIM
    return pl.pallas_call(
        functools.partial(kernel, n_head, n_ctx),
        out_shape=jax.ShapeDtypeStruct(merged_qkv.shape, BF16),
        in_specs=[pl.BlockSpec(memory_space=pltpu.SMEM), pl.BlockSpec(memory_space=pl.ANY),
                  pl.BlockSpec(memory_space=pl.ANY)],
        out_specs=pl.BlockSpec(memory_space=pltpu.VMEM),
        scratch_shapes=[
            pltpu.VMEM((REACH + 1, piece, pair), BF16),
            pltpu.VMEM((REACH + 1, piece, HEAD_DIM), BF16),
            pltpu.VMEM((piece, HEAD_DIM), BF16),
            pltpu.VMEM((piece, GROUP_Q * HEAD_DIM), BF16),
            pltpu.VMEM((piece, GROUP_Q * HEAD_DIM), BF16),
            pltpu.VMEM((n_groups, GROUP_Q, 2 * piece, piece), BF16),
            pltpu.VMEM((n_groups, GROUP_Q, 2 * piece, piece), F32),
            pltpu.VMEM((n_groups, GROUP_Q, piece), F32),
            pltpu.VMEM((n_groups, GROUP_Q, piece), F32),
            pltpu.VMEM((n_groups, GROUP_Q, piece), F32),
            pltpu.VMEM((n_groups, GROUP_Q, piece), F32),
            pltpu.VMEM((GROUP_Q, piece), F32),
            pltpu.VMEM((GROUP_Q, piece, HEAD_DIM), F32),
            pltpu.VMEM((piece, pair), F32),
            pltpu.VMEM((2, piece, pair), F32),
            pltpu.VMEM((piece, pair), F32),
            pltpu.VMEM((n_groups, piece, pair), BF16),
            pltpu.VMEM((n_groups, piece, pair), BF16),
            pltpu.VMEM((n_groups, piece, pair), BF16),
            pltpu.VMEM((n_groups, piece, pair), BF16),
            pltpu.VMEM((n_groups, piece, pair), BF16),
            pltpu.VMEM((n_groups, piece, pair), BF16),
            pltpu.VMEM((piece, (GROUP_Q + 2) * HEAD_DIM), BF16),
            dma((n_in,)), dma((n_in,)), dma((n_in,)),
            dma((n_groups,)), dma((n_groups,)), dma((n_groups,)), dma((n_groups,)),
            dma((n_groups,)), dma((n_groups,)),
            dma((n_groups,)), dma((n_groups,)), dma((n_groups,)), dma((n_groups,)),
            dma((n_groups,)), dma((n_groups,)),
            dma, dma, dma,
        ],
        compiler_params=pltpu.CompilerParams(
            collective_id=0, has_side_effects=True, vmem_limit_bytes=56 * 1024 * 1024),
        cost_estimate=pl.CostEstimate(
            flops=2 * macs, bytes_accessed=4 * merged_qkv.size * 2,
            transcendentals=GROUP_Q * piece * piece * REACH),
    )(doc_lengths, merged_qkv, out_grads)


def solution(mesh):
    placed = (P(("ctx", "head"), None), P(("ctx", "head"), None), P())
    body = functools.partial(per_device, mesh.shape["head"], mesh.shape["ctx"])
    return jax.shard_map(
        body, mesh=mesh, in_specs=placed, out_specs=P(("ctx", "head"), None), check_vma=False
    )
```

```python
import functools
import math

import jax
import jax.numpy as jnp
from jax import lax
from jax.experimental import pallas as pl
from jax.experimental.pallas import tpu as pltpu
from jax.sharding import PartitionSpec as P

GROUP_Q = 8
HEAD_DIM = 128
REACH = 6
MESH = pl.DeviceIdType.MESH
SCALE = HEAD_DIM ** -0.5
TO_EXP2 = SCALE * math.log2(math.e)
FAR = 2.0 ** 100
F32, BF16 = jnp.float32, jnp.bfloat16
IN_CHUNKS = 4
HEADS_STEP = 2
Z_CHIPS = 8


def nt(a, b):
    return lax.dot_general(a, b, (((1,), (1,)), ((), ())), preferred_element_type=F32)


def nn(a, b):
    return lax.dot_general(a, b, (((1,), (0,)), ((), ())), preferred_element_type=F32)


def wait_bytes(ref, sem):
    pltpu.make_async_copy(ref, ref, sem).wait()


def kernel(n_head, n_ctx, lens_ref, qkv_ref, grads_ref, out_ref,
           kv, key_doc, query_doc, qb, dob, probs, dprobs, st_m, st_l, st_d, gain, delta,
           key_t, dq, home, part, even, relay_kv, relay_grads, cross_in,
           odd_out, odd_in, rail_out, rail_in, stage,
           s_in, r_in, l_in, s_rail, r_rail, s_cross, r_cross, r_back, s_sib, r_sib,
           s_grail, r_grail, s_gsib, r_gsib, s_out, r_out, l_out):
    rows = qkv_ref.shape[0]
    piece = kv.shape[1]
    width = (GROUP_Q + 2) * HEAD_DIM
    q_width = GROUP_Q * HEAD_DIM
    me = lax.axis_index("head")
    ctx = lax.axis_index("ctx")
    core = lax.rem(ctx, 2)
    sib = ctx + 1 - 2 * core
    z = lax.rem(ctx // 2, Z_CHIPS)
    n_groups = REACH // 2
    starts_run, ends_run = z == 0, z == Z_CHIPS - 1
    crosses = z >= Z_CHIPS - n_groups

    def shifted(steps):
        return lax.rem(ctx + n_ctx + 2 * steps, n_ctx)

    after, before = shifted(1), shifted(-1)
    next_run, last_run = shifted(Z_CHIPS), shifted(-Z_CHIPS)
    run_start = shifted(-z)
    run_ends = [shifted(Z_CHIPS - 1 - i) for i in range(n_groups)]
    peers = [lax.rem(me + p, n_head) for p in range(1, n_head)]

    barrier = pltpu.get_barrier_semaphore()

    def greet(axis, other):
        pl.semaphore_signal(barrier, inc=1, device_id={axis: other}, device_id_type=MESH)

    for peer in peers:
        greet("head", peer)
    greet("ctx", sib)

    def where(condition, body):
        pl.when(condition)(body)

    where(jnp.logical_not(starts_run), lambda: greet("ctx", before))
    where(jnp.logical_not(ends_run), lambda: greet("ctx", after))

    @pl.when(crosses)
    def _():
        for other in (next_run, last_run, run_start):
            greet("ctx", other)

    @pl.when(starts_run)
    def _():
        for other in run_ends:
            greet("ctx", other)

    greeted = len(peers) + 3 + jnp.where(starts_run, n_groups - 1, 0)
    pl.semaphore_wait(barrier, greeted + jnp.where(ends_run, 2, jnp.where(crosses, 3, 0)))

    my_rows = pl.ds(pl.multiple_of(me * rows, rows), rows)

    def column(group, first, size):
        return pl.ds(pl.multiple_of(group * width + first, HEAD_DIM), size)

    def grad_column(group, first, size):
        return pl.ds(pl.multiple_of(group * q_width + first, HEAD_DIM), size)

    step_w = q_width // IN_CHUNKS
    others = pl.ds(0, rows * (n_head - 1))

    def sends(chunk):
        if chunk is None:
            return [(qkv_ref, lambda g: column(g, q_width, 2 * HEAD_DIM), kv.at[0],
                     pl.ds(0, 2 * HEAD_DIM), 0)]
        first = chunk * step_w
        cols = pl.ds(pl.multiple_of(first, HEAD_DIM), step_w)
        return [(qkv_ref, lambda g: column(g, first, step_w), qb, cols, 1 + 2 * chunk),
                (grads_ref, lambda g: grad_column(g, first, step_w), dob, cols, 2 + 2 * chunk)]

    def send_part(chunk):
        for src, src_cols, dst, dst_cols, i in sends(chunk):
            for peer in peers:
                pltpu.make_async_remote_copy(
                    src_ref=src.at[:, src_cols(peer)], dst_ref=dst.at[my_rows, dst_cols],
                    send_sem=s_in.at[i], recv_sem=r_in.at[i],
                    device_id={"head": peer}, device_id_type=MESH).start()
            pltpu.make_async_copy(
                src.at[:, src_cols(me)], dst.at[my_rows, dst_cols], l_in.at[i]).start()

    def arrived(chunk):
        for src, src_cols, dst, dst_cols, i in sends(chunk):
            pltpu.make_async_copy(
                src.at[:, src_cols(me)], dst.at[my_rows, dst_cols], l_in.at[i]).wait()
            wait_bytes(dst.at[others, dst_cols], r_in.at[i])

    def all_sent(chunk):
        for src, src_cols, dst, dst_cols, i in sends(chunk):
            wait_bytes(dst.at[others, dst_cols], s_in.at[i])

    def chunks(first, body):
        def step(chunk, carry):
            body(chunk)
            return carry

        lax.fori_loop(first, IN_CHUNKS, step, 0)

    send_part(None)

    def ctx_copy(src, dst, send_sem, recv_sem, device):
        return pltpu.make_async_remote_copy(
            src_ref=src, dst_ref=dst, send_sem=send_sem, recv_sem=recv_sem,
            device_id={"ctx": device}, device_id_type=MESH)

    lane = lax.broadcasted_iota(jnp.int32, (1, HEAD_DIM), 1)
    starts = jnp.full((1, HEAD_DIM), 1 << 20, jnp.int32)
    ends = jnp.full((1, HEAD_DIM), 1 << 20, jnp.int32)
    total = jnp.int32(0)
    for d in range(lens_ref.shape[0]):
        starts = jnp.where(lane == d, total, starts)
        total = total + lens_ref[d]
        ends = jnp.where(lane == d, total, ends)
    row_of = lax.broadcasted_iota(jnp.int32, (piece, HEAD_DIM), 0)
    lane_of = lax.broadcasted_iota(jnp.int32, (piece, HEAD_DIM), 1)
    for r in range(REACH + 1):
        pos = row_of + (ctx - r) * piece
        inside = ((starts <= pos) & (pos < ends)) | ((lane_of == HEAD_DIM - 1) & (pos < 0))
        key_doc[r] = jnp.where(inside, 1.0, 0.0).astype(BF16)
        if r == 0:
            query_doc[...] = jnp.where(inside, 0.0, -FAR).astype(BF16)
    causal = (lax.broadcasted_iota(jnp.int32, (piece, piece), 0)
              <= lax.broadcasted_iota(jnp.int32, (piece, piece), 1))

    def rail_send(r):
        return ctx_copy(kv.at[r], kv.at[r + 2], s_rail.at[r // 2], r_rail.at[r // 2], after)

    def cross_send():
        return ctx_copy(kv.at[0], relay_kv, s_cross.at[0], r_cross.at[0], next_run)

    def cross_on():
        i = Z_CHIPS - 1 - z
        return ctx_copy(relay_kv, kv.at[2 * i + 2], s_cross.at[1], r_rail.at[i], run_start)

    def sib_send(k, j):
        return ctx_copy(kv.at[2 * j + 2 * k], kv.at[2 * j + 1], s_sib.at[j], r_sib.at[j], sib)

    def pass_on(r):
        if r < REACH:

            @pl.when(jnp.logical_not(ends_run))
            def _():
                rail_send(r).start()

            @pl.when(core == 0)
            def _():
                sib_send(0, r // 2).start()
        if r > 0:

            @pl.when(core == 1)
            def _():
                sib_send(1, r // 2 - 1).start()

    arrived(None)
    where(crosses, lambda: cross_send().start())
    pass_on(0)
    send_part(0)

    groups = ((1, 2), (3, 4), (5, 6))
    last = len(groups) - 1

    heads_chunk = GROUP_Q // IN_CHUNKS

    def forward(gi, first_head):
        ra, rb = groups[gi]

        for u in range(heads_chunk):
            j = first_head + u
            cols = pl.ds(pl.multiple_of(j * HEAD_DIM, HEAD_DIM), HEAD_DIM)
            query = jnp.concatenate([qb[:, cols], query_doc[...]], axis=1)
            grad = dob[:, cols]

            blocks = (ra, rb, 0) if gi == last else (ra, rb)
            keys = jnp.concatenate(
                [jnp.concatenate([kv[r, :, :HEAD_DIM], key_doc[r]], axis=1) for r in blocks], axis=0)
            values = jnp.concatenate([kv[r, :, HEAD_DIM:] for r in blocks], axis=0)
            s = nt(keys, query)
            dp = nt(values, grad)
            if gi == last:
                s, dp = (jnp.concatenate(
                    [a[:piece], jnp.where(causal, a[2 * piece:], a[piece:2 * piece])], axis=0)
                    for a in (s, dp))
            top = jnp.max(s, axis=0, keepdims=True)
            p = jnp.exp2(s * TO_EXP2 - top * TO_EXP2)
            probs[gi, j] = p.astype(BF16)
            dprobs[gi, j] = dp
            at = pl.ds(j, 1)
            st_m[gi, at, :] = top * TO_EXP2
            st_l[gi, at, :] = jnp.sum(p, axis=0, keepdims=True)
            st_d[gi, at, :] = jnp.sum(p * dp, axis=0, keepdims=True)

    for gi in range(len(groups)):
        r = groups[gi][1]
        if gi == last:
            arrived(0)
            for g in range(last):
                sib_send(0, g).wait_recv()
                forward(g, 0)
        rail_send(r - 2).wait_recv()
        pass_on(r)
        if gi == 0:
            send_part(1)

            @pl.when(crosses)
            def _():
                cross_send().wait_recv()
                cross_on().start()

        elif gi == 1:
            chunks(2, send_part)
    sib_send(0, last).wait_recv()
    forward(last, 0)

    def forward_chunk(chunk):
        arrived(chunk)
        for gi in range(len(groups)):
            forward(gi, chunk * heads_chunk)

    chunks(1, forward_chunk)

    top = jnp.maximum(jnp.maximum(st_m[0], st_m[1]), st_m[2])
    factors = [jnp.exp2(st_m[gi] - top) for gi in range(len(groups))]
    inverse = 1.0 / sum(factors[gi] * st_l[gi] for gi in range(len(groups)))
    row_delta = jnp.zeros_like(inverse)
    for gi in range(len(groups)):
        gain[gi] = factors[gi] * inverse
        row_delta = row_delta + factors[gi] * inverse * st_d[gi]
    delta[...] = row_delta

    def out_send(first, size, peer):
        cols = pl.ds(first if isinstance(first, int) else pl.multiple_of(first, HEAD_DIM), size)
        return pltpu.make_async_remote_copy(
            src_ref=stage.at[pl.ds(pl.multiple_of(peer * rows, rows), rows), cols],
            dst_ref=out_ref.at[:, column(me, first, size)],
            send_sem=s_out, recv_sem=r_out,
            device_id={"head": peer}, device_id_type=MESH)

    def backward(gi):
        ra, rb = groups[gi]
        final = gi == 0
        heads_step = HEADS_STEP if final else 2 * HEADS_STEP

        def body(step, carry):
            if gi < last:

                @pl.when(step == 1)
                def _():
                    if final:
                        cross_back(last)
                    send_sum(gi + 1)

            blocks = (ra, rb, 0) if gi == last else (ra, rb)
            keys_t = jnp.concatenate([key_t[r] for r in blocks], axis=1)
            p_all, ds_all, grad_all, query_all = [], [], [], []
            for u in range(heads_step):
                j = step * heads_step + u
                cols = pl.ds(pl.multiple_of(j * HEAD_DIM, HEAD_DIM), HEAD_DIM)
                at = pl.ds(j, 1)
                p = probs[gi, j].astype(F32) * gain[gi, at, :]
                ds = p * (dprobs[gi, j] - delta[at, :])
                if gi == last:
                    p_c, ds_c = p[piece:], ds[piece:]
                    p = jnp.concatenate([p[:piece], jnp.where(causal, 0.0, p_c),
                                         jnp.where(causal, p_c, 0.0)], axis=0)
                    ds = jnp.concatenate([ds[:piece], jnp.where(causal, 0.0, ds_c),
                                          jnp.where(causal, ds_c, 0.0)], axis=0)
                p = p.astype(BF16)
                ds = ds.astype(BF16)
                p_all.append(p)
                ds_all.append(ds)
                grad_all.append(dob[:, cols])
                query_all.append(qb[:, cols])
                grad_query = nn(keys_t, ds)
                if gi != last:
                    grad_query = grad_query + dq[j]
                if final:
                    stage[:, cols] = jnp.transpose(grad_query * SCALE).astype(BF16)
                else:
                    dq[j] = grad_query
            p = jnp.concatenate(p_all, axis=1)
            ds = jnp.concatenate(ds_all, axis=1)
            grad_value = nn(p, jnp.concatenate(grad_all, axis=0))
            grad_key = nn(ds, jnp.concatenate(query_all, axis=0))
            for i in range(2):
                at = pl.ds(i * piece, piece)
                part[i, :, :HEAD_DIM] += grad_key[i * piece:(i + 1) * piece]
                part[i, :, HEAD_DIM:] += grad_value[i * piece:(i + 1) * piece]
            if gi == last:
                home[:, :HEAD_DIM] += grad_key[2 * piece:]
                home[:, HEAD_DIM:] += grad_value[2 * piece:]
            if final:
                first = step * HEADS_STEP * HEAD_DIM
                for peer in peers:
                    out_send(first, HEADS_STEP * HEAD_DIM, peer).start()
            return carry

        lax.fori_loop(0, GROUP_Q // heads_step, body, 0)

    def grail(r):
        i = r // 2 - 1
        return ctx_copy(rail_out.at[i], rail_in.at[i], s_grail.at[i], r_grail.at[i], before)

    def grail_over(gi):
        return ctx_copy(rail_out.at[gi], relay_grads, s_grail.at[gi], r_back.at[0], run_ends[gi])

    def grail_home():
        return ctx_copy(relay_grads, cross_in, s_cross.at[2], r_back.at[1], last_run)

    def cross_back(gi):
        @pl.when(z == Z_CHIPS - 1 - gi)
        def _():
            grail_over(gi).wait_recv()
            grail_home().start()

    def gsib(j):
        return ctx_copy(odd_out.at[j], odd_in.at[j], s_gsib.at[j], r_gsib.at[j], sib)

    def key_scale():
        which = lax.broadcasted_iota(jnp.int32, (1, 2 * HEAD_DIM), 1)
        return jnp.where(which < HEAD_DIM, SCALE, 1.0)

    def send_sum(gi):
        rb, j = groups[gi][1], gi
        if gi < last:
            @pl.when(jnp.logical_not(ends_run))
            def _():
                grail(rb + 2).wait_recv()
                even[...] += rail_in[rb // 2].astype(F32)

            @pl.when(core == 0)
            def _():
                gsib(j + 1).wait_recv()
                even[...] += odd_in[j + 1].astype(F32)

        @pl.when(core == 1)
        def _():
            gsib(j).wait_recv()
            even[...] += odd_in[j].astype(F32)

        rail_out[rb // 2 - 1] = even[...].astype(BF16)

        @pl.when(starts_run)
        def _():
            grail_over(gi).start()

        @pl.when(jnp.logical_not(starts_run))
        def _():
            grail(rb).start()

    for r in range(REACH + 1):
        key_t[r] = jnp.transpose(kv[r, :, :HEAD_DIM])
    home[...] = jnp.zeros_like(home)
    for gi in range(last, -1, -1):
        part[...] = jnp.zeros_like(part)
        backward(gi)
        odd_out[gi] = (part[0] * key_scale()).astype(BF16)
        gsib(gi).start()
        even[...] = part[1] * key_scale()
    cross_back(1)
    send_sum(0)
    cross_back(0)

    home[...] = home[...] * key_scale()

    @pl.when(core == 0)
    def _():
        gsib(0).wait_recv()
        home[...] += odd_in[0].astype(F32)

    @pl.when(jnp.logical_not(ends_run))
    def _():
        grail(2).wait_recv()
        home[...] += rail_in[0].astype(F32)

    @pl.when(crosses)
    def _():
        grail_home().wait_recv()
        home[...] += cross_in[...].astype(F32)

    own = home[...]
    stage[:, q_width:] = own.astype(BF16)
    for peer in peers:
        out_send(q_width, 2 * HEAD_DIM, peer).start()
    mine = pltpu.make_async_copy(stage.at[my_rows, :], out_ref.at[:, column(me, 0, width)], l_out)
    mine.start()

    all_sent(None)
    chunks(0, all_sent)
    for j in range(len(groups)):
        where(jnp.logical_not(ends_run), lambda j=j: rail_send(2 * j).wait_send())
        sib_send(0, j).wait_send()
        gsib(j).wait_send()
        grail(2 * j + 2).wait_send()

    @pl.when(crosses)
    def _():
        cross_send().wait_send()
        cross_on().wait_send()
        grail_home().wait_send()

    mine.wait()
    wait_bytes(out_ref.at[:, pl.ds(0, width * (n_head - 1))], s_out)
    wait_bytes(out_ref.at[:, pl.ds(0, width * (n_head - 1))], r_out)


def per_device(n_head, n_ctx, merged_qkv, out_grads, doc_lengths):
    rows = merged_qkv.shape[0]
    piece = rows * n_head
    n_groups = REACH // 2
    pair = 2 * HEAD_DIM
    dma = pltpu.SemaphoreType.DMA
    n_in = 1 + 2 * IN_CHUNKS
    macs = 5 * GROUP_Q * piece * (REACH + 1) * piece * HEAD_DIM
    return pl.pallas_call(
        functools.partial(kernel, n_head, n_ctx),
        out_shape=jax.ShapeDtypeStruct(merged_qkv.shape, BF16),
        in_specs=[pl.BlockSpec(memory_space=pltpu.SMEM), pl.BlockSpec(memory_space=pl.ANY),
                  pl.BlockSpec(memory_space=pl.ANY)],
        out_specs=pl.BlockSpec(memory_space=pltpu.VMEM),
        scratch_shapes=[
            pltpu.VMEM((REACH + 1, piece, pair), BF16),
            pltpu.VMEM((REACH + 1, piece, HEAD_DIM), BF16),
            pltpu.VMEM((piece, HEAD_DIM), BF16),
            pltpu.VMEM((piece, GROUP_Q * HEAD_DIM), BF16),
            pltpu.VMEM((piece, GROUP_Q * HEAD_DIM), BF16),
            pltpu.VMEM((n_groups, GROUP_Q, 2 * piece, piece), BF16),
            pltpu.VMEM((n_groups, GROUP_Q, 2 * piece, piece), F32),
            pltpu.VMEM((n_groups, GROUP_Q, piece), F32),
            pltpu.VMEM((n_groups, GROUP_Q, piece), F32),
            pltpu.VMEM((n_groups, GROUP_Q, piece), F32),
            pltpu.VMEM((n_groups, GROUP_Q, piece), F32),
            pltpu.VMEM((GROUP_Q, piece), F32),
            pltpu.VMEM((REACH + 1, HEAD_DIM, piece), BF16),
            pltpu.VMEM((GROUP_Q, HEAD_DIM, piece), F32),
            pltpu.VMEM((piece, pair), F32),
            pltpu.VMEM((2, piece, pair), F32),
            pltpu.VMEM((piece, pair), F32),
            pltpu.VMEM((piece, pair), BF16),
            pltpu.VMEM((piece, pair), BF16),
            pltpu.VMEM((piece, pair), BF16),
            pltpu.VMEM((n_groups, piece, pair), BF16),
            pltpu.VMEM((n_groups, piece, pair), BF16),
            pltpu.VMEM((n_groups, piece, pair), BF16),
            pltpu.VMEM((n_groups, piece, pair), BF16),
            pltpu.VMEM((piece, (GROUP_Q + 2) * HEAD_DIM), BF16),
            dma((n_in,)), dma((n_in,)), dma((n_in,)),
            dma((n_groups,)), dma((n_groups,)), dma((3,)), dma((1,)), dma((2,)),
            dma((n_groups,)), dma((n_groups,)),
            dma((n_groups,)), dma((n_groups,)),
            dma((n_groups,)), dma((n_groups,)),
            dma, dma, dma,
        ],
        compiler_params=pltpu.CompilerParams(
            collective_id=0, has_side_effects=True, vmem_limit_bytes=56 * 1024 * 1024),
        cost_estimate=pl.CostEstimate(
            flops=2 * macs, bytes_accessed=4 * merged_qkv.size * 2,
            transcendentals=GROUP_Q * piece * piece * REACH),
    )(doc_lengths, merged_qkv, out_grads)


def solution(mesh):
    placed = (P(("ctx", "head"), None), P(("ctx", "head"), None), P())
    body = functools.partial(per_device, mesh.shape["head"], mesh.shape["ctx"])
    return jax.shard_map(
        body, mesh=mesh, in_specs=placed, out_specs=P(("ctx", "head"), None), check_vma=False
    )
```

```python
import functools
import math

import jax
import jax.numpy as jnp
from jax import lax
from jax.experimental import pallas as pl
from jax.experimental.pallas import tpu as pltpu
from jax.sharding import PartitionSpec as P

GROUP_Q = 8
HEAD_DIM = 128
REACH = 6
MESH = pl.DeviceIdType.MESH
SCALE = HEAD_DIM ** -0.5
TO_EXP2 = SCALE * math.log2(math.e)
FAR = 2.0 ** 100
F32, BF16 = jnp.float32, jnp.bfloat16
IN_CHUNKS = 4
HEADS_STEP = 2
Z_CHIPS = 8


def nt(a, b):
    return lax.dot_general(a, b, (((1,), (1,)), ((), ())), preferred_element_type=F32)


def nn(a, b):
    return lax.dot_general(a, b, (((1,), (0,)), ((), ())), preferred_element_type=F32)


def tn(a, b):
    return lax.dot_general(a, b, (((0,), (0,)), ((), ())), preferred_element_type=F32)


def wait_bytes(ref, sem):
    pltpu.make_async_copy(ref, ref, sem).wait()


def kernel(n_head, n_ctx, lens_ref, qkv_ref, grads_ref, out_ref,
           kv, key_doc, query_doc, qb, dob, probs, dprobs, st_m, st_l, st_d, gain, delta,
           dq, home, part, even, relay_kv, relay_grads, cross_in,
           odd_out, odd_in, rail_out, rail_in, stage,
           s_in, r_in, l_in, s_rail, r_rail, s_cross, r_cross, r_back, s_sib, r_sib,
           s_grail, r_grail, s_gsib, r_gsib, s_out, r_out, l_out):
    rows = qkv_ref.shape[0]
    piece = kv.shape[1]
    width = (GROUP_Q + 2) * HEAD_DIM
    q_width = GROUP_Q * HEAD_DIM
    me = lax.axis_index("head")
    ctx = lax.axis_index("ctx")
    core = lax.rem(ctx, 2)
    sib = ctx + 1 - 2 * core
    z = lax.rem(ctx // 2, Z_CHIPS)
    n_groups = REACH // 2
    starts_run, ends_run = z == 0, z == Z_CHIPS - 1
    crosses = z >= Z_CHIPS - n_groups

    def shifted(steps):
        return lax.rem(ctx + n_ctx + 2 * steps, n_ctx)

    after, before = shifted(1), shifted(-1)
    next_run, last_run = shifted(Z_CHIPS), shifted(-Z_CHIPS)
    run_start = shifted(-z)
    run_ends = [shifted(Z_CHIPS - 1 - i) for i in range(n_groups)]
    peers = [lax.rem(me + p, n_head) for p in range(1, n_head)]

    barrier = pltpu.get_barrier_semaphore()

    def greet(axis, other):
        pl.semaphore_signal(barrier, inc=1, device_id={axis: other}, device_id_type=MESH)

    for peer in peers:
        greet("head", peer)
    greet("ctx", sib)

    def where(condition, body):
        @pl.when(condition)
        def _():
            body()

    where(jnp.logical_not(starts_run), lambda: greet("ctx", before))
    where(jnp.logical_not(ends_run), lambda: greet("ctx", after))

    @pl.when(crosses)
    def _():
        for other in (next_run, last_run, run_start):
            greet("ctx", other)

    @pl.when(starts_run)
    def _():
        for other in run_ends:
            greet("ctx", other)

    greeted = len(peers) + 3 + jnp.where(starts_run, n_groups - 1, 0)
    pl.semaphore_wait(barrier, greeted + jnp.where(ends_run, 2, jnp.where(crosses, 3, 0)))

    my_rows = pl.ds(pl.multiple_of(me * rows, rows), rows)

    def column(group, first, size):
        return pl.ds(pl.multiple_of(group * width + first, HEAD_DIM), size)

    def grad_column(group, first, size):
        return pl.ds(pl.multiple_of(group * q_width + first, HEAD_DIM), size)

    step_w = q_width // IN_CHUNKS
    others = pl.ds(0, rows * (n_head - 1))

    def sends(chunk):
        if chunk is None:
            return [(qkv_ref, lambda g: column(g, q_width, 2 * HEAD_DIM), kv.at[0],
                     pl.ds(0, 2 * HEAD_DIM), 0)]
        first = chunk * step_w
        cols = pl.ds(pl.multiple_of(first, HEAD_DIM), step_w)
        return [(qkv_ref, lambda g: column(g, first, step_w), qb, cols, 1 + 2 * chunk),
                (grads_ref, lambda g: grad_column(g, first, step_w), dob, cols, 2 + 2 * chunk)]

    def send_to(chunk, targets):
        for src, src_cols, dst, dst_cols, i in sends(chunk):
            for peer in targets:
                pltpu.make_async_remote_copy(
                    src_ref=src.at[:, src_cols(peer)], dst_ref=dst.at[my_rows, dst_cols],
                    send_sem=s_in.at[i], recv_sem=r_in.at[i],
                    device_id={"head": peer}, device_id_type=MESH).start()

    def send_along_x(chunk):
        for src, src_cols, dst, dst_cols, i in sends(chunk):
            pltpu.make_async_copy(
                src.at[:, src_cols(me)], dst.at[my_rows, dst_cols], l_in.at[i]).start()
        send_to(chunk, peers[1::2])

    def send_across_y(chunk):
        send_to(chunk, peers[0::2])

    def send_all(chunk):
        send_along_x(chunk)
        send_across_y(chunk)

    def arrived(chunk):
        for src, src_cols, dst, dst_cols, i in sends(chunk):
            pltpu.make_async_copy(
                src.at[:, src_cols(me)], dst.at[my_rows, dst_cols], l_in.at[i]).wait()
            wait_bytes(dst.at[others, dst_cols], r_in.at[i])

    def all_sent(chunk):
        for src, src_cols, dst, dst_cols, i in sends(chunk):
            wait_bytes(dst.at[others, dst_cols], s_in.at[i])

    def chunks(first, end, body):
        def step(chunk, carry):
            body(chunk)
            return carry

        lax.fori_loop(first, end, step, 0)

    send_all(None)

    def ctx_copy(src, dst, send_sem, recv_sem, device):
        return pltpu.make_async_remote_copy(
            src_ref=src, dst_ref=dst, send_sem=send_sem, recv_sem=recv_sem,
            device_id={"ctx": device}, device_id_type=MESH)

    lane = lax.broadcasted_iota(jnp.int32, (1, HEAD_DIM), 1)
    starts = jnp.full((1, HEAD_DIM), 1 << 20, jnp.int32)
    ends = jnp.full((1, HEAD_DIM), 1 << 20, jnp.int32)
    total = jnp.int32(0)
    for d in range(lens_ref.shape[0]):
        starts = jnp.where(lane == d, total, starts)
        total = total + lens_ref[d]
        ends = jnp.where(lane == d, total, ends)
    row_of = lax.broadcasted_iota(jnp.int32, (piece, HEAD_DIM), 0)
    lane_of = lax.broadcasted_iota(jnp.int32, (piece, HEAD_DIM), 1)
    for r in range(REACH + 1):
        pos = row_of + (ctx - r) * piece
        inside = ((starts <= pos) & (pos < ends)) | ((lane_of == HEAD_DIM - 1) & (pos < 0))
        key_doc[r] = jnp.where(inside, 1.0, 0.0).astype(BF16)
        if r == 0:
            query_doc[...] = jnp.where(inside, 0.0, -FAR).astype(BF16)
    causal = (lax.broadcasted_iota(jnp.int32, (piece, piece), 0)
              <= lax.broadcasted_iota(jnp.int32, (piece, piece), 1))

    def half(part_no):
        return pl.ds(part_no * (piece // 2), piece // 2)

    def rail_send(r, part_no):
        at, i = half(part_no), r // 2
        return ctx_copy(kv.at[r, at], kv.at[r + 2, at], s_rail.at[i, part_no], r_rail.at[i, part_no], after)

    def cross_send(part_no):
        at = half(part_no)
        return ctx_copy(kv.at[0, at], relay_kv.at[at], s_cross.at[part_no], r_cross.at[part_no], next_run)

    def cross_on(part_no):
        i, at = Z_CHIPS - 1 - z, half(part_no)
        return ctx_copy(relay_kv.at[at], kv.at[2 * i + 2, at], s_cross.at[2 + part_no],
                        r_rail.at[i, part_no], run_start)

    def sib_send(k, j):
        return ctx_copy(kv.at[2 * j + 2 * k], kv.at[2 * j + 1], s_sib.at[j], r_sib.at[j], sib)

    def pass_on(r):
        for part_no in range(2):
            if r > 0:
                rail_send(r - 2, part_no).wait_recv()
            if r < REACH:
                where(jnp.logical_not(ends_run), lambda: rail_send(r, part_no).start())
        if r < REACH:
            where(core == 0, lambda: sib_send(0, r // 2).start())
        if r > 0:
            where(core == 1, lambda: sib_send(1, r // 2 - 1).start())

    arrived(None)

    @pl.when(crosses)
    def _():
        for part_no in range(2):
            cross_send(part_no).start()

    pass_on(0)
    chunks(0, IN_CHUNKS, send_along_x)
    where(jnp.logical_not(crosses), lambda: chunks(0, IN_CHUNKS, send_across_y))

    groups = ((1, 2), (3, 4), (5, 6))
    last = len(groups) - 1

    heads_chunk = GROUP_Q // IN_CHUNKS

    def forward(gi, first_head):
        ra, rb = groups[gi]

        for u in range(heads_chunk):
            j = first_head + u
            cols = pl.ds(pl.multiple_of(j * HEAD_DIM, HEAD_DIM), HEAD_DIM)
            query = jnp.concatenate([qb[:, cols], query_doc[...]], axis=1)
            grad = dob[:, cols]

            blocks = (ra, rb, 0) if gi == last else (ra, rb)
            keys = jnp.concatenate(
                [jnp.concatenate([kv[r, :, :HEAD_DIM], key_doc[r]], axis=1) for r in blocks], axis=0)
            values = jnp.concatenate([kv[r, :, HEAD_DIM:] for r in blocks], axis=0)
            s = nt(keys, query)
            dp = nt(values, grad)
            if gi == last:
                s, dp = (jnp.concatenate(
                    [a[:piece], jnp.where(causal, a[2 * piece:], a[piece:2 * piece])], axis=0)
                    for a in (s, dp))
            top = jnp.max(s, axis=0, keepdims=True)
            p = jnp.exp2(s * TO_EXP2 - top * TO_EXP2)
            probs[gi, j] = p.astype(BF16)
            dprobs[gi, j] = dp
            at = pl.ds(j, 1)
            st_m[gi, at, :] = top * TO_EXP2
            st_l[gi, at, :] = jnp.sum(p, axis=0, keepdims=True)
            st_d[gi, at, :] = jnp.sum(p * dp, axis=0, keepdims=True)

    pass_on(2)

    @pl.when(crosses)
    def _():
        for part_no in range(2):
            cross_send(part_no).wait_recv()
            cross_on(part_no).start()
        chunks(0, IN_CHUNKS, send_across_y)

    pass_on(4)
    for gi in range(last):
        sib_send(0, gi).wait_recv()

    def early_groups(chunk):
        where(chunk == IN_CHUNKS - 1, lambda: pass_on(REACH))
        arrived(chunk)
        for gi in range(last):
            forward(gi, chunk * heads_chunk)

    chunks(0, IN_CHUNKS, early_groups)
    sib_send(0, last).wait_recv()
    chunks(0, IN_CHUNKS, lambda chunk: forward(last, chunk * heads_chunk))

    top = jnp.maximum(jnp.maximum(st_m[0], st_m[1]), st_m[2])
    factors = [jnp.exp2(st_m[gi] - top) for gi in range(len(groups))]
    inverse = 1.0 / sum(factors[gi] * st_l[gi] for gi in range(len(groups)))
    row_delta = jnp.zeros_like(inverse)
    for gi in range(len(groups)):
        gain[gi] = factors[gi] * inverse
        row_delta = row_delta + factors[gi] * inverse * st_d[gi]
    delta[...] = row_delta

    def out_send(first, size, peer):
        cols = pl.ds(first if isinstance(first, int) else pl.multiple_of(first, HEAD_DIM), size)
        return pltpu.make_async_remote_copy(
            src_ref=stage.at[pl.ds(pl.multiple_of(peer * rows, rows), rows), cols],
            dst_ref=out_ref.at[:, column(me, first, size)],
            send_sem=s_out, recv_sem=r_out,
            device_id={"head": peer}, device_id_type=MESH)

    def backward(gi):
        ra, rb = groups[gi]
        final = gi == 0
        heads_step = HEADS_STEP if final else 2 * HEADS_STEP

        def body(step, carry):
            if gi < last:

                @pl.when(step == 1)
                def _():
                    if final:
                        cross_back(last)
                    send_sum(gi + 1)

            blocks = (ra, rb, 0) if gi == last else (ra, rb)
            keys = jnp.concatenate([kv[r, :, :HEAD_DIM] for r in blocks], axis=0)
            p_all, ds_all, grad_all, query_all = [], [], [], []
            for u in range(heads_step):
                j = step * heads_step + u
                cols = pl.ds(pl.multiple_of(j * HEAD_DIM, HEAD_DIM), HEAD_DIM)
                at = pl.ds(j, 1)
                p = probs[gi, j].astype(F32) * gain[gi, at, :]
                ds = p * (dprobs[gi, j] - delta[at, :])
                if gi == last:
                    p_c, ds_c = p[piece:], ds[piece:]
                    p = jnp.concatenate([p[:piece], jnp.where(causal, 0.0, p_c),
                                         jnp.where(causal, p_c, 0.0)], axis=0)
                    ds = jnp.concatenate([ds[:piece], jnp.where(causal, 0.0, ds_c),
                                          jnp.where(causal, ds_c, 0.0)], axis=0)
                p = p.astype(BF16)
                ds = ds.astype(BF16)
                p_all.append(p)
                ds_all.append(ds)
                grad_all.append(dob[:, cols])
                query_all.append(qb[:, cols])
                grad_query = tn(ds, keys)
                if gi != last:
                    grad_query = grad_query + dq[j]
                if final:
                    stage[:, cols] = (grad_query * SCALE).astype(BF16)
                else:
                    dq[j] = grad_query
            p = jnp.concatenate(p_all, axis=1)
            ds = jnp.concatenate(ds_all, axis=1)
            grad_value = nn(p, jnp.concatenate(grad_all, axis=0))
            grad_key = nn(ds, jnp.concatenate(query_all, axis=0))
            for i in range(2):
                at = pl.ds(i * piece, piece)
                part[i, :, :HEAD_DIM] += grad_key[i * piece:(i + 1) * piece]
                part[i, :, HEAD_DIM:] += grad_value[i * piece:(i + 1) * piece]
            if gi == last:
                home[:, :HEAD_DIM] += grad_key[2 * piece:]
                home[:, HEAD_DIM:] += grad_value[2 * piece:]
            if final:
                first = step * HEADS_STEP * HEAD_DIM
                for peer in peers:
                    out_send(first, HEADS_STEP * HEAD_DIM, peer).start()
            return carry

        lax.fori_loop(0, GROUP_Q // heads_step, body, 0)

    def grail(r):
        i = r // 2 - 1
        return ctx_copy(rail_out.at[i], rail_in.at[i], s_grail.at[i], r_grail.at[i], before)

    def grail_over(gi):
        return ctx_copy(rail_out.at[gi], relay_grads, s_grail.at[gi], r_back.at[0], run_ends[gi])

    def grail_home():
        return ctx_copy(relay_grads, cross_in, s_cross.at[4], r_back.at[1], last_run)

    def cross_back(gi):
        @pl.when(z == Z_CHIPS - 1 - gi)
        def _():
            grail_over(gi).wait_recv()
            grail_home().start()

    def gsib(j):
        return ctx_copy(odd_out.at[j], odd_in.at[j], s_gsib.at[j], r_gsib.at[j], sib)

    def key_scale():
        which = lax.broadcasted_iota(jnp.int32, (1, 2 * HEAD_DIM), 1)
        return jnp.where(which < HEAD_DIM, SCALE, 1.0)

    def send_sum(gi):
        rb, j = groups[gi][1], gi
        if gi < last:
            @pl.when(jnp.logical_not(ends_run))
            def _():
                grail(rb + 2).wait_recv()
                even[...] += rail_in[rb // 2].astype(F32)

            @pl.when(core == 0)
            def _():
                gsib(j + 1).wait_recv()
                even[...] += odd_in[j + 1].astype(F32)

        @pl.when(core == 1)
        def _():
            gsib(j).wait_recv()
            even[...] += odd_in[j].astype(F32)

        rail_out[rb // 2 - 1] = even[...].astype(BF16)

        @pl.when(starts_run)
        def _():
            grail_over(gi).start()

        @pl.when(jnp.logical_not(starts_run))
        def _():
            grail(rb).start()

    home[...] = jnp.zeros_like(home)
    for gi in range(last, -1, -1):
        part[...] = jnp.zeros_like(part)
        backward(gi)
        odd_out[gi] = (part[0] * key_scale()).astype(BF16)
        gsib(gi).start()
        even[...] = part[1] * key_scale()
    cross_back(1)
    send_sum(0)
    cross_back(0)

    home[...] = home[...] * key_scale()

    @pl.when(core == 0)
    def _():
        gsib(0).wait_recv()
        home[...] += odd_in[0].astype(F32)

    @pl.when(jnp.logical_not(ends_run))
    def _():
        grail(2).wait_recv()
        home[...] += rail_in[0].astype(F32)

    @pl.when(crosses)
    def _():
        grail_home().wait_recv()
        home[...] += cross_in[...].astype(F32)

    own = home[...]
    stage[:, q_width:] = own.astype(BF16)
    for peer in peers:
        out_send(q_width, 2 * HEAD_DIM, peer).start()
    mine = pltpu.make_async_copy(stage.at[my_rows, :], out_ref.at[:, column(me, 0, width)], l_out)
    mine.start()

    all_sent(None)
    chunks(0, IN_CHUNKS, all_sent)
    for j in range(len(groups)):
        where(jnp.logical_not(ends_run), lambda j=j: [rail_send(2 * j, i).wait_send() for i in range(2)])
        sib_send(0, j).wait_send()
        gsib(j).wait_send()
        grail(2 * j + 2).wait_send()

    @pl.when(crosses)
    def _():
        for part_no in range(2):
            cross_send(part_no).wait_send()
            cross_on(part_no).wait_send()
        grail_home().wait_send()

    mine.wait()
    wait_bytes(out_ref.at[:, pl.ds(0, width * (n_head - 1))], s_out)
    wait_bytes(out_ref.at[:, pl.ds(0, width * (n_head - 1))], r_out)


def copy_kernel(src_ref, dst_ref):
    dst_ref[...] = src_ref[...]


def per_device(n_head, n_ctx, merged_qkv, out_grads, doc_lengths):
    rows = merged_qkv.shape[0]
    piece = rows * n_head
    n_groups = REACH // 2
    pair = 2 * HEAD_DIM
    dma = pltpu.SemaphoreType.DMA
    n_in = 1 + 2 * IN_CHUNKS
    macs = 5 * GROUP_Q * piece * (REACH + 1) * piece * HEAD_DIM
    result = pl.pallas_call(
        functools.partial(kernel, n_head, n_ctx),
        out_shape=jax.ShapeDtypeStruct(merged_qkv.shape, BF16),
        in_specs=[pl.BlockSpec(memory_space=pltpu.SMEM), pl.BlockSpec(memory_space=pl.ANY),
                  pl.BlockSpec(memory_space=pl.ANY)],
        out_specs=pl.BlockSpec(memory_space=pltpu.VMEM),
        scratch_shapes=[
            pltpu.VMEM((REACH + 1, piece, pair), BF16),
            pltpu.VMEM((REACH + 1, piece, HEAD_DIM), BF16),
            pltpu.VMEM((piece, HEAD_DIM), BF16),
            pltpu.VMEM((piece, GROUP_Q * HEAD_DIM), BF16),
            pltpu.VMEM((piece, GROUP_Q * HEAD_DIM), BF16),
            pltpu.VMEM((n_groups, GROUP_Q, 2 * piece, piece), BF16),
            pltpu.VMEM((n_groups, GROUP_Q, 2 * piece, piece), F32),
            pltpu.VMEM((n_groups, GROUP_Q, piece), F32),
            pltpu.VMEM((n_groups, GROUP_Q, piece), F32),
            pltpu.VMEM((n_groups, GROUP_Q, piece), F32),
            pltpu.VMEM((n_groups, GROUP_Q, piece), F32),
            pltpu.VMEM((GROUP_Q, piece), F32),
            pltpu.VMEM((GROUP_Q, piece, HEAD_DIM), F32),
            pltpu.VMEM((piece, pair), F32),
            pltpu.VMEM((2, piece, pair), F32),
            pltpu.VMEM((piece, pair), F32),
            pltpu.VMEM((piece, pair), BF16),
            pltpu.VMEM((piece, pair), BF16),
            pltpu.VMEM((piece, pair), BF16),
            pltpu.VMEM((n_groups, piece, pair), BF16),
            pltpu.VMEM((n_groups, piece, pair), BF16),
            pltpu.VMEM((n_groups, piece, pair), BF16),
            pltpu.VMEM((n_groups, piece, pair), BF16),
            pltpu.VMEM((piece, (GROUP_Q + 2) * HEAD_DIM), BF16),
            dma((n_in,)), dma((n_in,)), dma((n_in,)),
            dma((n_groups, 2)), dma((n_groups, 2)), dma((5,)), dma((2,)), dma((2,)),
            dma((n_groups,)), dma((n_groups,)),
            dma((n_groups,)), dma((n_groups,)),
            dma((n_groups,)), dma((n_groups,)),
            dma, dma, dma,
        ],
        compiler_params=pltpu.CompilerParams(
            collective_id=0, has_side_effects=True, vmem_limit_bytes=56 * 1024 * 1024),
        cost_estimate=pl.CostEstimate(
            flops=2 * macs, bytes_accessed=4 * merged_qkv.size * 2,
            transcendentals=GROUP_Q * piece * piece * REACH),
    )(doc_lengths, merged_qkv, out_grads)
    return pl.pallas_call(
        copy_kernel, out_shape=jax.ShapeDtypeStruct(result.shape, result.dtype)
    )(result)


def solution(mesh):
    placed = (P(("ctx", "head"), None), P(("ctx", "head"), None), P())
    body = functools.partial(per_device, mesh.shape["head"], mesh.shape["ctx"])
    return jax.shard_map(
        body, mesh=mesh, in_specs=placed, out_specs=P(("ctx", "head"), None), check_vma=False
    )
```

```python
import functools
import math

import jax
import jax.numpy as jnp
from jax import lax
from jax.experimental import pallas as pl
from jax.experimental.pallas import tpu as pltpu
from jax.sharding import PartitionSpec as P

GROUP_Q = 8
HEAD_DIM = 128
REACH = 6
MESH = pl.DeviceIdType.MESH
SCALE = HEAD_DIM ** -0.5
TO_EXP2 = SCALE * math.log2(math.e)
FAR = 2.0 ** 100
F32, BF16 = jnp.float32, jnp.bfloat16
IN_CHUNKS = 4
HEADS_STEP = 2
ROWS_STEP = 64
Z_CHIPS = 8


def nt(a, b):
    return lax.dot_general(a, b, (((1,), (1,)), ((), ())), preferred_element_type=F32)


def nn(a, b):
    return lax.dot_general(a, b, (((1,), (0,)), ((), ())), preferred_element_type=F32)


def tn(a, b):
    return lax.dot_general(a, b, (((0,), (0,)), ((), ())), preferred_element_type=F32)


def wait_bytes(ref, sem):
    pltpu.make_async_copy(ref, ref, sem).wait()


def kernel(n_head, n_ctx, lens_ref, qkv_ref, grads_ref, out_ref,
           kv, key_doc, query_doc, qb, dob, probs, dprobs, st_m, st_l, st_d, gain, delta,
           dq, home, part, even, relay_kv, relay_grads, cross_in,
           odd_out, odd_in, rail_out, rail_in, stage,
           s_in, r_in, l_in, s_rail, r_rail, s_cross, r_cross, r_back, s_sib, r_sib,
           s_grail, r_grail, s_gsib, r_gsib, s_out, r_out, l_out):
    rows = qkv_ref.shape[0]
    piece = kv.shape[1]
    width = (GROUP_Q + 2) * HEAD_DIM
    q_width = GROUP_Q * HEAD_DIM
    me = lax.axis_index("head")
    ctx = lax.axis_index("ctx")
    core = lax.rem(ctx, 2)
    sib = ctx + 1 - 2 * core
    z = lax.rem(ctx // 2, Z_CHIPS)
    n_groups = REACH // 2
    starts_run, ends_run = z == 0, z == Z_CHIPS - 1
    crosses = z >= Z_CHIPS - n_groups

    def shifted(steps):
        return lax.rem(ctx + n_ctx + 2 * steps, n_ctx)

    after, before = shifted(1), shifted(-1)
    next_run, last_run = shifted(Z_CHIPS), shifted(-Z_CHIPS)
    run_start = shifted(-z)
    run_ends = [shifted(Z_CHIPS - 1 - i) for i in range(n_groups)]
    peers = [lax.rem(me + p, n_head) for p in range(1, n_head)]

    barrier = pltpu.get_barrier_semaphore()

    def greet(axis, other):
        pl.semaphore_signal(barrier, inc=1, device_id={axis: other}, device_id_type=MESH)

    for peer in peers:
        greet("head", peer)
    greet("ctx", sib)

    def where(condition, body):
        @pl.when(condition)
        def _():
            body()

    where(jnp.logical_not(starts_run), lambda: greet("ctx", before))
    where(jnp.logical_not(ends_run), lambda: greet("ctx", after))

    @pl.when(crosses)
    def _():
        for other in (next_run, last_run, run_start):
            greet("ctx", other)

    @pl.when(starts_run)
    def _():
        for other in run_ends:
            greet("ctx", other)

    greeted = len(peers) + 3 + jnp.where(starts_run, n_groups - 1, 0)
    pl.semaphore_wait(barrier, greeted + jnp.where(ends_run, 2, jnp.where(crosses, 3, 0)))

    my_rows = pl.ds(pl.multiple_of(me * rows, rows), rows)

    def column(group, first, size):
        return pl.ds(pl.multiple_of(group * width + first, HEAD_DIM), size)

    def grad_column(group, first, size):
        return pl.ds(pl.multiple_of(group * q_width + first, HEAD_DIM), size)

    step_w = q_width // IN_CHUNKS
    others = pl.ds(0, rows * (n_head - 1))

    def sends(chunk):
        if chunk is None:
            return [(qkv_ref, lambda g: column(g, q_width, 2 * HEAD_DIM), kv.at[0],
                     pl.ds(0, 2 * HEAD_DIM), 0)]
        first = chunk * step_w
        cols = pl.ds(pl.multiple_of(first, HEAD_DIM), step_w)
        return [(qkv_ref, lambda g: column(g, first, step_w), qb, cols, 1 + 2 * chunk),
                (grads_ref, lambda g: grad_column(g, first, step_w), dob, cols, 2 + 2 * chunk)]

    def send_to(chunk, targets):
        for src, src_cols, dst, dst_cols, i in sends(chunk):
            for peer in targets:
                pltpu.make_async_remote_copy(
                    src_ref=src.at[:, src_cols(peer)], dst_ref=dst.at[my_rows, dst_cols],
                    send_sem=s_in.at[i], recv_sem=r_in.at[i],
                    device_id={"head": peer}, device_id_type=MESH).start()

    def send_along_x(chunk):
        for src, src_cols, dst, dst_cols, i in sends(chunk):
            pltpu.make_async_copy(
                src.at[:, src_cols(me)], dst.at[my_rows, dst_cols], l_in.at[i]).start()
        send_to(chunk, peers[1::2])

    def send_across_y(chunk):
        send_to(chunk, peers[0::2])

    def send_all(chunk):
        send_along_x(chunk)
        send_across_y(chunk)

    def arrived(chunk):
        for src, src_cols, dst, dst_cols, i in sends(chunk):
            pltpu.make_async_copy(
                src.at[:, src_cols(me)], dst.at[my_rows, dst_cols], l_in.at[i]).wait()
            wait_bytes(dst.at[others, dst_cols], r_in.at[i])

    def all_sent(chunk):
        for src, src_cols, dst, dst_cols, i in sends(chunk):
            wait_bytes(dst.at[others, dst_cols], s_in.at[i])

    def chunks(first, end, body):
        def step(chunk, carry):
            body(chunk)
            return carry

        lax.fori_loop(first, end, step, 0)

    send_all(None)

    def ctx_copy(src, dst, send_sem, recv_sem, device):
        return pltpu.make_async_remote_copy(
            src_ref=src, dst_ref=dst, send_sem=send_sem, recv_sem=recv_sem,
            device_id={"ctx": device}, device_id_type=MESH)

    lane = lax.broadcasted_iota(jnp.int32, (1, HEAD_DIM), 1)
    starts = jnp.full((1, HEAD_DIM), 1 << 20, jnp.int32)
    ends = jnp.full((1, HEAD_DIM), 1 << 20, jnp.int32)
    total = jnp.int32(0)
    for d in range(lens_ref.shape[0]):
        starts = jnp.where(lane == d, total, starts)
        total = total + lens_ref[d]
        ends = jnp.where(lane == d, total, ends)
    row_of = lax.broadcasted_iota(jnp.int32, (piece, HEAD_DIM), 0)
    lane_of = lax.broadcasted_iota(jnp.int32, (piece, HEAD_DIM), 1)
    for r in range(REACH + 1):
        pos = row_of + (ctx - r) * piece
        inside = ((starts <= pos) & (pos < ends)) | ((lane_of == HEAD_DIM - 1) & (pos < 0))
        key_doc[r] = jnp.where(inside, 1.0, 0.0).astype(BF16)
        if r == 0:
            query_doc[...] = jnp.where(inside, 0.0, -FAR).astype(BF16)
    row_iota = lax.broadcasted_iota(jnp.int32, (ROWS_STEP, piece), 0)
    col_iota = lax.broadcasted_iota(jnp.int32, (ROWS_STEP, piece), 1)

    def half(part_no):
        return pl.ds(part_no * (piece // 2), piece // 2)

    def rail_send(r, part_no):
        at, i = half(part_no), r // 2
        return ctx_copy(kv.at[r, at], kv.at[r + 2, at], s_rail.at[i, part_no], r_rail.at[i, part_no], after)

    def cross_send(part_no):
        at = half(part_no)
        return ctx_copy(kv.at[0, at], relay_kv.at[at], s_cross.at[part_no], r_cross.at[part_no], next_run)

    def cross_on(part_no):
        i, at = Z_CHIPS - 1 - z, half(part_no)
        return ctx_copy(relay_kv.at[at], kv.at[2 * i + 2, at], s_cross.at[2 + part_no],
                        r_rail.at[i, part_no], run_start)

    def sib_send(k, j):
        return ctx_copy(kv.at[2 * j + 2 * k], kv.at[2 * j + 1], s_sib.at[j], r_sib.at[j], sib)

    def pass_on(r):
        for part_no in range(2):
            if r > 0:
                rail_send(r - 2, part_no).wait_recv()
            if r < REACH:
                where(jnp.logical_not(ends_run), lambda: rail_send(r, part_no).start())
        if r < REACH:
            where(core == 0, lambda: sib_send(0, r // 2).start())
        if r > 0:
            where(core == 1, lambda: sib_send(1, r // 2 - 1).start())

    arrived(None)

    @pl.when(crosses)
    def _():
        for part_no in range(2):
            cross_send(part_no).start()

    pass_on(0)
    where(crosses, lambda: chunks(0, 2, send_along_x))
    where(jnp.logical_not(crosses), lambda: chunks(0, IN_CHUNKS, send_all))

    groups = ((1, 2), (3, 4), (5, 6))
    last = len(groups) - 1

    heads_chunk = GROUP_Q // IN_CHUNKS

    def forward(gi, first_head):
        ra, rb = groups[gi]

        for u in range(heads_chunk):
            j = first_head + u
            cols = pl.ds(pl.multiple_of(j * HEAD_DIM, HEAD_DIM), HEAD_DIM)
            query = jnp.concatenate([qb[:, cols], query_doc[...]], axis=1)
            grad = dob[:, cols]

            blocks = (ra, rb, 0) if gi == last else (ra, rb)
            keys = jnp.concatenate(
                [jnp.concatenate([kv[r, :, :HEAD_DIM], key_doc[r]], axis=1) for r in blocks], axis=0)
            values = jnp.concatenate([kv[r, :, HEAD_DIM:] for r in blocks], axis=0)
            s = nt(keys, query)
            dp = nt(values, grad)
            blocks_of = [pl.ds(i * ROWS_STEP, ROWS_STEP) for i in range(2 * piece // ROWS_STEP)]

            def rows_of(a, i):
                first = i * ROWS_STEP
                part_a = a[first:first + ROWS_STEP]
                if gi == last and first >= piece:
                    tri = row_iota + (first - piece) <= col_iota
                    part_a = jnp.where(tri, a[first + piece:first + piece + ROWS_STEP], part_a)
                return part_a

            s = [rows_of(s, i) for i in range(len(blocks_of))]
            top = functools.reduce(jnp.maximum, [jnp.max(a, axis=0, keepdims=True) for a in s])
            top = top * TO_EXP2
            total_p = total_d = jnp.zeros((1, piece), F32)
            for i, at in enumerate(blocks_of):
                dp_i = rows_of(dp, i)
                p = jnp.exp2(s[i] * TO_EXP2 - top)
                probs[gi, j, at] = p.astype(BF16)
                dprobs[gi, j, at] = dp_i
                total_p = total_p + jnp.sum(p, axis=0, keepdims=True)
                total_d = total_d + jnp.sum(p * dp_i, axis=0, keepdims=True)
            at = pl.ds(j, 1)
            st_m[gi, at, :] = top
            st_l[gi, at, :] = total_p
            st_d[gi, at, :] = total_d

    pass_on(2)

    @pl.when(crosses)
    def _():
        for part_no in range(2):
            cross_send(part_no).wait_recv()
            cross_on(part_no).start()
        chunks(0, 2, send_across_y)
        chunks(2, IN_CHUNKS, send_all)

    pass_on(4)
    for gi in range(last):
        sib_send(0, gi).wait_recv()

    def early_groups(chunk):
        where(chunk == IN_CHUNKS - 1, lambda: pass_on(REACH))
        arrived(chunk)
        for gi in range(last):
            forward(gi, chunk * heads_chunk)

    chunks(0, IN_CHUNKS, early_groups)
    sib_send(0, last).wait_recv()
    chunks(0, IN_CHUNKS, lambda chunk: forward(last, chunk * heads_chunk))

    top = jnp.maximum(jnp.maximum(st_m[0], st_m[1]), st_m[2])
    factors = [jnp.exp2(st_m[gi] - top) for gi in range(len(groups))]
    inverse = 1.0 / sum(factors[gi] * st_l[gi] for gi in range(len(groups)))
    row_delta = jnp.zeros_like(inverse)
    for gi in range(len(groups)):
        gain[gi] = factors[gi] * inverse
        row_delta = row_delta + factors[gi] * inverse * st_d[gi]
    delta[...] = row_delta

    def out_send(first, size, peer):
        cols = pl.ds(first if isinstance(first, int) else pl.multiple_of(first, HEAD_DIM), size)
        return pltpu.make_async_remote_copy(
            src_ref=stage.at[pl.ds(pl.multiple_of(peer * rows, rows), rows), cols],
            dst_ref=out_ref.at[:, column(me, first, size)],
            send_sem=s_out, recv_sem=r_out,
            device_id={"head": peer}, device_id_type=MESH)

    def backward(gi):
        ra, rb = groups[gi]
        final = gi == 0
        heads_step = HEADS_STEP if final else 2 * HEADS_STEP

        def body(step, carry):
            if gi < last:

                @pl.when(step == 1)
                def _():
                    if final:
                        cross_back(last)
                    send_sum(gi + 1)

            blocks = (ra, rb, 0) if gi == last else (ra, rb)
            keys = jnp.concatenate([kv[r, :, :HEAD_DIM] for r in blocks], axis=0)
            p_all, ds_all, grad_all, query_all = [], [], [], []
            for u in range(heads_step):
                j = step * heads_step + u
                cols = pl.ds(pl.multiple_of(j * HEAD_DIM, HEAD_DIM), HEAD_DIM)
                at = pl.ds(j, 1)
                gain_j, delta_j = gain[gi, at, :], delta[at, :]
                p, ds, p_own, ds_own = [], [], [], []
                for i in range(2 * piece // ROWS_STEP):
                    rows_i = pl.ds(i * ROWS_STEP, ROWS_STEP)
                    p_i = probs[gi, j, rows_i].astype(F32) * gain_j
                    ds_i = p_i * (dprobs[gi, j, rows_i] - delta_j)
                    if gi == last and i * ROWS_STEP >= piece:
                        tri = row_iota + (i * ROWS_STEP - piece) <= col_iota
                        p_own.append(jnp.where(tri, p_i, 0.0).astype(BF16))
                        ds_own.append(jnp.where(tri, ds_i, 0.0).astype(BF16))
                        p_i, ds_i = jnp.where(tri, 0.0, p_i), jnp.where(tri, 0.0, ds_i)
                    p.append(p_i.astype(BF16))
                    ds.append(ds_i.astype(BF16))
                p = jnp.concatenate(p + p_own, axis=0)
                ds = jnp.concatenate(ds + ds_own, axis=0)
                p_all.append(p)
                ds_all.append(ds)
                grad_all.append(dob[:, cols])
                query_all.append(qb[:, cols])
                grad_query = tn(ds, keys)
                if gi != last:
                    grad_query = grad_query + dq[j]
                if final:
                    stage[:, cols] = (grad_query * SCALE).astype(BF16)
                else:
                    dq[j] = grad_query
            p = jnp.concatenate(p_all, axis=1)
            ds = jnp.concatenate(ds_all, axis=1)
            grad_value = nn(p, jnp.concatenate(grad_all, axis=0))
            grad_key = nn(ds, jnp.concatenate(query_all, axis=0))
            for i in range(2):
                at = pl.ds(i * piece, piece)
                part[i, :, :HEAD_DIM] += grad_key[i * piece:(i + 1) * piece]
                part[i, :, HEAD_DIM:] += grad_value[i * piece:(i + 1) * piece]
            if gi == last:
                home[:, :HEAD_DIM] += grad_key[2 * piece:]
                home[:, HEAD_DIM:] += grad_value[2 * piece:]
            if final:
                first = step * HEADS_STEP * HEAD_DIM
                for peer in peers:
                    out_send(first, HEADS_STEP * HEAD_DIM, peer).start()
            return carry

        lax.fori_loop(0, GROUP_Q // heads_step, body, 0)

    def grail(r):
        i = r // 2 - 1
        return ctx_copy(rail_out.at[i], rail_in.at[i], s_grail.at[i], r_grail.at[i], before)

    def grail_over(gi):
        return ctx_copy(rail_out.at[gi], relay_grads, s_grail.at[gi], r_back.at[0], run_ends[gi])

    def grail_home():
        return ctx_copy(relay_grads, cross_in, s_cross.at[4], r_back.at[1], last_run)

    def cross_back(gi):
        @pl.when(z == Z_CHIPS - 1 - gi)
        def _():
            grail_over(gi).wait_recv()
            grail_home().start()

    def gsib(j):
        return ctx_copy(odd_out.at[j], odd_in.at[j], s_gsib.at[j], r_gsib.at[j], sib)

    def key_scale():
        which = lax.broadcasted_iota(jnp.int32, (1, 2 * HEAD_DIM), 1)
        return jnp.where(which < HEAD_DIM, SCALE, 1.0)

    def send_sum(gi):
        rb, j = groups[gi][1], gi
        if gi < last:
            @pl.when(jnp.logical_not(ends_run))
            def _():
                grail(rb + 2).wait_recv()
                even[...] += rail_in[rb // 2].astype(F32)

            @pl.when(core == 0)
            def _():
                gsib(j + 1).wait_recv()
                even[...] += odd_in[j + 1].astype(F32)

        @pl.when(core == 1)
        def _():
            gsib(j).wait_recv()
            even[...] += odd_in[j].astype(F32)

        rail_out[rb // 2 - 1] = even[...].astype(BF16)

        @pl.when(starts_run)
        def _():
            grail_over(gi).start()

        @pl.when(jnp.logical_not(starts_run))
        def _():
            grail(rb).start()

    home[...] = jnp.zeros_like(home)
    for gi in range(last, -1, -1):
        part[...] = jnp.zeros_like(part)
        backward(gi)
        odd_out[gi] = (part[0] * key_scale()).astype(BF16)
        gsib(gi).start()
        even[...] = part[1] * key_scale()
    cross_back(1)
    send_sum(0)
    cross_back(0)

    home[...] = home[...] * key_scale()

    @pl.when(core == 0)
    def _():
        gsib(0).wait_recv()
        home[...] += odd_in[0].astype(F32)

    @pl.when(jnp.logical_not(ends_run))
    def _():
        grail(2).wait_recv()
        home[...] += rail_in[0].astype(F32)

    @pl.when(crosses)
    def _():
        grail_home().wait_recv()
        home[...] += cross_in[...].astype(F32)

    own = home[...]
    stage[:, q_width:] = own.astype(BF16)
    for peer in peers:
        out_send(q_width, 2 * HEAD_DIM, peer).start()
    mine = pltpu.make_async_copy(stage.at[my_rows, :], out_ref.at[:, column(me, 0, width)], l_out)
    mine.start()

    all_sent(None)
    chunks(0, IN_CHUNKS, all_sent)
    for j in range(len(groups)):
        where(jnp.logical_not(ends_run), lambda j=j: [rail_send(2 * j, i).wait_send() for i in range(2)])
        sib_send(0, j).wait_send()
        gsib(j).wait_send()
        grail(2 * j + 2).wait_send()

    @pl.when(crosses)
    def _():
        for part_no in range(2):
            cross_send(part_no).wait_send()
            cross_on(part_no).wait_send()
        grail_home().wait_send()

    mine.wait()
    wait_bytes(out_ref.at[:, pl.ds(0, width * (n_head - 1))], s_out)
    wait_bytes(out_ref.at[:, pl.ds(0, width * (n_head - 1))], r_out)


def per_device(n_head, n_ctx, merged_qkv, out_grads, doc_lengths):
    rows = merged_qkv.shape[0]
    piece = rows * n_head
    n_groups = REACH // 2
    pair = 2 * HEAD_DIM
    dma = pltpu.SemaphoreType.DMA
    n_in = 1 + 2 * IN_CHUNKS
    macs = 5 * GROUP_Q * piece * (REACH + 1) * piece * HEAD_DIM
    return pl.pallas_call(
        functools.partial(kernel, n_head, n_ctx),
        out_shape=jax.ShapeDtypeStruct(merged_qkv.shape, BF16),
        in_specs=[pl.BlockSpec(memory_space=pltpu.SMEM), pl.BlockSpec(memory_space=pl.ANY),
                  pl.BlockSpec(memory_space=pl.ANY)],
        out_specs=pl.BlockSpec(memory_space=pltpu.VMEM),
        scratch_shapes=[
            pltpu.VMEM((REACH + 1, piece, pair), BF16),
            pltpu.VMEM((REACH + 1, piece, HEAD_DIM), BF16),
            pltpu.VMEM((piece, HEAD_DIM), BF16),
            pltpu.VMEM((piece, GROUP_Q * HEAD_DIM), BF16),
            pltpu.VMEM((piece, GROUP_Q * HEAD_DIM), BF16),
            pltpu.VMEM((n_groups, GROUP_Q, 2 * piece, piece), BF16),
            pltpu.VMEM((n_groups, GROUP_Q, 2 * piece, piece), F32),
            pltpu.VMEM((n_groups, GROUP_Q, piece), F32),
            pltpu.VMEM((n_groups, GROUP_Q, piece), F32),
            pltpu.VMEM((n_groups, GROUP_Q, piece), F32),
            pltpu.VMEM((n_groups, GROUP_Q, piece), F32),
            pltpu.VMEM((GROUP_Q, piece), F32),
            pltpu.VMEM((GROUP_Q, piece, HEAD_DIM), F32),
            pltpu.VMEM((piece, pair), F32),
            pltpu.VMEM((2, piece, pair), F32),
            pltpu.VMEM((piece, pair), F32),
            pltpu.VMEM((piece, pair), BF16),
            pltpu.VMEM((piece, pair), BF16),
            pltpu.VMEM((piece, pair), BF16),
            pltpu.VMEM((n_groups, piece, pair), BF16),
            pltpu.VMEM((n_groups, piece, pair), BF16),
            pltpu.VMEM((n_groups, piece, pair), BF16),
            pltpu.VMEM((n_groups, piece, pair), BF16),
            pltpu.VMEM((piece, (GROUP_Q + 2) * HEAD_DIM), BF16),
            dma((n_in,)), dma((n_in,)), dma((n_in,)),
            dma((n_groups, 2)), dma((n_groups, 2)), dma((5,)), dma((2,)), dma((2,)),
            dma((n_groups,)), dma((n_groups,)),
            dma((n_groups,)), dma((n_groups,)),
            dma((n_groups,)), dma((n_groups,)),
            dma, dma, dma,
        ],
        compiler_params=pltpu.CompilerParams(
            collective_id=0, has_side_effects=True, vmem_limit_bytes=56 * 1024 * 1024),
        cost_estimate=pl.CostEstimate(
            flops=2 * macs, bytes_accessed=4 * merged_qkv.size * 2,
            transcendentals=GROUP_Q * piece * piece * REACH),
    )(doc_lengths, merged_qkv, out_grads)


def solution(mesh):
    placed = (P(("ctx", "head"), None), P(("ctx", "head"), None), P())
    body = functools.partial(per_device, mesh.shape["head"], mesh.shape["ctx"])
    return jax.shard_map(
        body, mesh=mesh, in_specs=placed, out_specs=P(("ctx", "head"), None), check_vma=False
    )
```

```python
import functools
import math

import jax
import jax.numpy as jnp
from jax import lax
from jax.experimental import pallas as pl
from jax.experimental.pallas import tpu as pltpu
from jax.sharding import PartitionSpec as P

GROUP_Q = 8
HEAD_DIM = 128
REACH = 6
MESH = pl.DeviceIdType.MESH
SCALE = HEAD_DIM ** -0.5
TO_EXP2 = SCALE * math.log2(math.e)
FAR = 2.0 ** 100
F32, BF16 = jnp.float32, jnp.bfloat16
IN_CHUNKS = 4
HEADS_STEP = 2
ROWS_STEP = 64
Z_CHIPS = 8


def nt(a, b):
    return lax.dot_general(a, b, (((1,), (1,)), ((), ())), preferred_element_type=F32)


def nn(a, b):
    return lax.dot_general(a, b, (((1,), (0,)), ((), ())), preferred_element_type=F32)


def tn(a, b):
    return lax.dot_general(a, b, (((0,), (0,)), ((), ())), preferred_element_type=F32)


def wait_bytes(ref, sem):
    pltpu.make_async_copy(ref, ref, sem).wait()


def kernel(n_head, n_ctx, lens_ref, qkv_ref, grads_ref, out_ref,
           kv, key_doc, query_doc, qb, dob, probs, dprobs, st_m, st_l, st_d, gain, delta,
           dq, home, part, even, cross_in,
           odd_out, odd_in, rail_out, rail_in, stage,
           s_in, r_in, l_in, s_rail, r_rail, r_back, s_sib, r_sib,
           s_grail, r_grail, s_gsib, r_gsib, s_out, r_out, l_out):
    rows = qkv_ref.shape[0]
    piece = kv.shape[1]
    width = (GROUP_Q + 2) * HEAD_DIM
    q_width = GROUP_Q * HEAD_DIM
    me = lax.axis_index("head")
    ctx = lax.axis_index("ctx")
    core = lax.rem(ctx, 2)
    sib = ctx + 1 - 2 * core
    z = lax.rem(ctx // 2, Z_CHIPS)
    n_groups = REACH // 2
    starts_run, ends_run = z == 0, z == Z_CHIPS - 1
    crosses = z >= Z_CHIPS - n_groups

    def shifted(steps):
        return lax.rem(ctx + n_ctx + 2 * steps, n_ctx)

    after, before = shifted(1), shifted(-1)
    peers = [lax.rem(me + p, n_head) for p in range(1, n_head)]

    barrier = pltpu.get_barrier_semaphore()

    def greet(axis, other):
        pl.semaphore_signal(barrier, inc=1, device_id={axis: other}, device_id_type=MESH)

    for peer in peers:
        greet("head", peer)
    greet("ctx", sib)

    def where(condition, body):
        @pl.when(condition)
        def _():
            body()

    greet("ctx", before)
    greet("ctx", after)
    for steps in range(2, n_groups + 1):
        where(starts_run, lambda: greet("ctx", shifted(-steps)))
        where(z == Z_CHIPS - steps, lambda: greet("ctx", shifted(steps)))
    more = jnp.where(starts_run, n_groups - 1, jnp.where(crosses & jnp.logical_not(ends_run), 1, 0))
    pl.semaphore_wait(barrier, len(peers) + 3 + more)

    my_rows = pl.ds(pl.multiple_of(me * rows, rows), rows)

    def column(group, first, size):
        return pl.ds(pl.multiple_of(group * width + first, HEAD_DIM), size)

    def grad_column(group, first, size):
        return pl.ds(pl.multiple_of(group * q_width + first, HEAD_DIM), size)

    step_w = q_width // IN_CHUNKS
    others = pl.ds(0, rows * (n_head - 1))

    def sends(chunk):
        if chunk is None:
            return [(qkv_ref, lambda g: column(g, q_width, 2 * HEAD_DIM), kv.at[0],
                     pl.ds(0, 2 * HEAD_DIM), 0)]
        first = chunk * step_w
        cols = pl.ds(pl.multiple_of(first, HEAD_DIM), step_w)
        return [(qkv_ref, lambda g: column(g, first, step_w), qb, cols, 1 + 2 * chunk),
                (grads_ref, lambda g: grad_column(g, first, step_w), dob, cols, 2 + 2 * chunk)]

    def send_to(chunk, targets):
        for src, src_cols, dst, dst_cols, i in sends(chunk):
            for peer in targets:
                pltpu.make_async_remote_copy(
                    src_ref=src.at[:, src_cols(peer)], dst_ref=dst.at[my_rows, dst_cols],
                    send_sem=s_in.at[i], recv_sem=r_in.at[i],
                    device_id={"head": peer}, device_id_type=MESH).start()

    def send_along_x(chunk):
        for src, src_cols, dst, dst_cols, i in sends(chunk):
            pltpu.make_async_copy(
                src.at[:, src_cols(me)], dst.at[my_rows, dst_cols], l_in.at[i]).start()
        send_to(chunk, peers[1::2])

    def send_across_y(chunk):
        send_to(chunk, peers[0::2])

    def send_all(chunk):
        send_along_x(chunk)
        send_across_y(chunk)

    def arrived(chunk):
        for src, src_cols, dst, dst_cols, i in sends(chunk):
            pltpu.make_async_copy(
                src.at[:, src_cols(me)], dst.at[my_rows, dst_cols], l_in.at[i]).wait()
            wait_bytes(dst.at[others, dst_cols], r_in.at[i])

    def all_sent(chunk):
        for src, src_cols, dst, dst_cols, i in sends(chunk):
            wait_bytes(dst.at[others, dst_cols], s_in.at[i])

    def chunks(first, end, body):
        def step(chunk, carry):
            body(chunk)
            return carry

        lax.fori_loop(first, end, step, 0)

    send_all(None)

    def ctx_copy(src, dst, send_sem, recv_sem, device):
        return pltpu.make_async_remote_copy(
            src_ref=src, dst_ref=dst, send_sem=send_sem, recv_sem=recv_sem,
            device_id={"ctx": device}, device_id_type=MESH)

    lane = lax.broadcasted_iota(jnp.int32, (1, HEAD_DIM), 1)
    starts = jnp.full((1, HEAD_DIM), 1 << 20, jnp.int32)
    ends = jnp.full((1, HEAD_DIM), 1 << 20, jnp.int32)
    total = jnp.int32(0)
    for d in range(lens_ref.shape[0]):
        starts = jnp.where(lane == d, total, starts)
        total = total + lens_ref[d]
        ends = jnp.where(lane == d, total, ends)
    row_of = lax.broadcasted_iota(jnp.int32, (piece, HEAD_DIM), 0)
    lane_of = lax.broadcasted_iota(jnp.int32, (piece, HEAD_DIM), 1)
    for r in range(REACH + 1):
        pos = row_of + (ctx - r) * piece
        inside = ((starts <= pos) & (pos < ends)) | ((lane_of == HEAD_DIM - 1) & (pos < 0))
        key_doc[r] = jnp.where(inside, 1.0, 0.0).astype(BF16)
        if r == 0:
            query_doc[...] = jnp.where(inside, 0.0, -FAR).astype(BF16)
    row_iota = lax.broadcasted_iota(jnp.int32, (ROWS_STEP, piece), 0)
    col_iota = lax.broadcasted_iota(jnp.int32, (ROWS_STEP, piece), 1)

    def half(part_no):
        return pl.ds(part_no * (piece // 2), piece // 2)

    def rail_send(r, part_no):
        at, i = half(part_no), r // 2
        return ctx_copy(kv.at[r, at], kv.at[r + 2, at], s_rail.at[i, part_no], r_rail.at[i, part_no], after)

    def sib_send(k, j):
        return ctx_copy(kv.at[2 * j + 2 * k], kv.at[2 * j + 1], s_sib.at[j], r_sib.at[j], sib)

    def pass_on(r):
        for part_no in range(2):
            if r > 0:
                rail_send(r - 2, part_no).wait_recv()
            if r < REACH:
                rail_send(r, part_no).start()
        if r < REACH:
            where(core == 0, lambda: sib_send(0, r // 2).start())
        if r > 0:
            where(core == 1, lambda: sib_send(1, r // 2 - 1).start())

    arrived(None)

    pass_on(0)
    turn = starts_run | ends_run
    where(turn, lambda: chunks(0, 2, send_along_x))
    where(jnp.logical_not(turn), lambda: chunks(0, IN_CHUNKS, send_all))

    groups = ((1, 2), (3, 4), (5, 6))
    last = len(groups) - 1

    heads_chunk = GROUP_Q // IN_CHUNKS

    def forward(gi, first_head):
        ra, rb = groups[gi]

        for u in range(heads_chunk):
            j = first_head + u
            cols = pl.ds(pl.multiple_of(j * HEAD_DIM, HEAD_DIM), HEAD_DIM)
            query = jnp.concatenate([qb[:, cols], query_doc[...]], axis=1)
            grad = dob[:, cols]

            blocks = (ra, rb, 0) if gi == last else (ra, rb)
            keys = jnp.concatenate(
                [jnp.concatenate([kv[r, :, :HEAD_DIM], key_doc[r]], axis=1) for r in blocks], axis=0)
            values = jnp.concatenate([kv[r, :, HEAD_DIM:] for r in blocks], axis=0)
            s = nt(keys, query)
            dp = nt(values, grad)
            blocks_of = [pl.ds(i * ROWS_STEP, ROWS_STEP) for i in range(2 * piece // ROWS_STEP)]

            def rows_of(a, i):
                first = i * ROWS_STEP
                part_a = a[first:first + ROWS_STEP]
                if gi == last and first >= piece:
                    tri = row_iota + (first - piece) <= col_iota
                    part_a = jnp.where(tri, a[first + piece:first + piece + ROWS_STEP], part_a)
                return part_a

            s = [rows_of(s, i) for i in range(len(blocks_of))]
            top = functools.reduce(jnp.maximum, [jnp.max(a, axis=0, keepdims=True) for a in s])
            top = top * TO_EXP2
            total_p = total_d = jnp.zeros((1, piece), F32)
            for i, at in enumerate(blocks_of):
                dp_i = rows_of(dp, i)
                p = jnp.exp2(s[i] * TO_EXP2 - top)
                probs[gi, j, at] = p.astype(BF16)
                dprobs[gi, j, at] = dp_i
                total_p = total_p + jnp.sum(p, axis=0, keepdims=True)
                total_d = total_d + jnp.sum(p * dp_i, axis=0, keepdims=True)
            at = pl.ds(j, 1)
            st_m[gi, at, :] = top
            st_l[gi, at, :] = total_p
            st_d[gi, at, :] = total_d

    pass_on(2)

    where(turn, lambda: chunks(0, 2, send_across_y))
    pass_on(4)
    where(turn, lambda: chunks(2, IN_CHUNKS, send_all))
    for gi in range(last):
        sib_send(0, gi).wait_recv()

    def early_groups(chunk):
        where(chunk == IN_CHUNKS - 1, lambda: pass_on(REACH))
        arrived(chunk)
        for gi in range(last):
            forward(gi, chunk * heads_chunk)

    chunks(0, IN_CHUNKS, early_groups)
    sib_send(0, last).wait_recv()
    chunks(0, IN_CHUNKS, lambda chunk: forward(last, chunk * heads_chunk))

    top = jnp.maximum(jnp.maximum(st_m[0], st_m[1]), st_m[2])
    factors = [jnp.exp2(st_m[gi] - top) for gi in range(len(groups))]
    inverse = 1.0 / sum(factors[gi] * st_l[gi] for gi in range(len(groups)))
    row_delta = jnp.zeros_like(inverse)
    for gi in range(len(groups)):
        gain[gi] = factors[gi] * inverse
        row_delta = row_delta + factors[gi] * inverse * st_d[gi]
    delta[...] = row_delta

    def out_send(first, size, peer):
        cols = pl.ds(first if isinstance(first, int) else pl.multiple_of(first, HEAD_DIM), size)
        return pltpu.make_async_remote_copy(
            src_ref=stage.at[pl.ds(pl.multiple_of(peer * rows, rows), rows), cols],
            dst_ref=out_ref.at[:, column(me, first, size)],
            send_sem=s_out, recv_sem=r_out,
            device_id={"head": peer}, device_id_type=MESH)

    def backward(gi):
        ra, rb = groups[gi]
        final = gi == 0
        heads_step = HEADS_STEP if final else 2 * HEADS_STEP

        def body(step, carry):
            if gi < last:

                @pl.when(step == 1)
                def _():
                    send_sum(gi + 1)

            blocks = (ra, rb, 0) if gi == last else (ra, rb)
            keys = jnp.concatenate([kv[r, :, :HEAD_DIM] for r in blocks], axis=0)
            p_all, ds_all, grad_all, query_all = [], [], [], []
            for u in range(heads_step):
                j = step * heads_step + u
                cols = pl.ds(pl.multiple_of(j * HEAD_DIM, HEAD_DIM), HEAD_DIM)
                at = pl.ds(j, 1)
                gain_j, delta_j = gain[gi, at, :], delta[at, :]
                p, ds, p_own, ds_own = [], [], [], []
                for i in range(2 * piece // ROWS_STEP):
                    rows_i = pl.ds(i * ROWS_STEP, ROWS_STEP)
                    p_i = probs[gi, j, rows_i].astype(F32) * gain_j
                    ds_i = p_i * (dprobs[gi, j, rows_i] - delta_j)
                    if gi == last and i * ROWS_STEP >= piece:
                        tri = row_iota + (i * ROWS_STEP - piece) <= col_iota
                        p_own.append(jnp.where(tri, p_i, 0.0).astype(BF16))
                        ds_own.append(jnp.where(tri, ds_i, 0.0).astype(BF16))
                        p_i, ds_i = jnp.where(tri, 0.0, p_i), jnp.where(tri, 0.0, ds_i)
                    p.append(p_i.astype(BF16))
                    ds.append(ds_i.astype(BF16))
                p = jnp.concatenate(p + p_own, axis=0)
                ds = jnp.concatenate(ds + ds_own, axis=0)
                p_all.append(p)
                ds_all.append(ds)
                grad_all.append(dob[:, cols])
                query_all.append(qb[:, cols])
                grad_query = tn(ds, keys)
                if gi != last:
                    grad_query = grad_query + dq[j]
                if final:
                    stage[:, cols] = (grad_query * SCALE).astype(BF16)
                else:
                    dq[j] = grad_query
            p = jnp.concatenate(p_all, axis=1)
            ds = jnp.concatenate(ds_all, axis=1)
            grad_value = nn(p, jnp.concatenate(grad_all, axis=0))
            grad_key = nn(ds, jnp.concatenate(query_all, axis=0))
            for i in range(2):
                at = pl.ds(i * piece, piece)
                part[i, :, :HEAD_DIM] += grad_key[i * piece:(i + 1) * piece]
                part[i, :, HEAD_DIM:] += grad_value[i * piece:(i + 1) * piece]
            if gi == last:
                home[:, :HEAD_DIM] += grad_key[2 * piece:]
                home[:, HEAD_DIM:] += grad_value[2 * piece:]
            if final:
                first = step * HEADS_STEP * HEAD_DIM
                for peer in peers:
                    out_send(first, HEADS_STEP * HEAD_DIM, peer).start()
            return carry

        lax.fori_loop(0, GROUP_Q // heads_step, body, 0)

    def grail(r):
        i = r // 2 - 1
        return ctx_copy(rail_out.at[i], rail_in.at[i], s_grail.at[i], r_grail.at[i], before)

    def grail_home(gi):
        return ctx_copy(rail_out.at[gi], cross_in, s_grail.at[gi], r_back, shifted(-1 - gi))

    def gsib(j):
        return ctx_copy(odd_out.at[j], odd_in.at[j], s_gsib.at[j], r_gsib.at[j], sib)

    def key_scale():
        which = lax.broadcasted_iota(jnp.int32, (1, 2 * HEAD_DIM), 1)
        return jnp.where(which < HEAD_DIM, SCALE, 1.0)

    def send_sum(gi):
        rb, j = groups[gi][1], gi
        if gi < last:
            @pl.when(jnp.logical_not(ends_run))
            def _():
                grail(rb + 2).wait_recv()
                even[...] += rail_in[rb // 2].astype(F32)

            @pl.when(core == 0)
            def _():
                gsib(j + 1).wait_recv()
                even[...] += odd_in[j + 1].astype(F32)

        @pl.when(core == 1)
        def _():
            gsib(j).wait_recv()
            even[...] += odd_in[j].astype(F32)

        rail_out[rb // 2 - 1] = even[...].astype(BF16)

        @pl.when(starts_run)
        def _():
            grail_home(gi).start()

        @pl.when(jnp.logical_not(starts_run))
        def _():
            grail(rb).start()

    home[...] = jnp.zeros_like(home)
    for gi in range(last, -1, -1):
        part[...] = jnp.zeros_like(part)
        backward(gi)
        odd_out[gi] = (part[0] * key_scale()).astype(BF16)
        gsib(gi).start()
        even[...] = part[1] * key_scale()
    send_sum(0)

    home[...] = home[...] * key_scale()

    @pl.when(core == 0)
    def _():
        gsib(0).wait_recv()
        home[...] += odd_in[0].astype(F32)

    @pl.when(jnp.logical_not(ends_run))
    def _():
        grail(2).wait_recv()
        home[...] += rail_in[0].astype(F32)

    @pl.when(crosses)
    def _():
        grail_home(0).wait_recv()
        home[...] += cross_in[...].astype(F32)

    own = home[...]
    stage[:, q_width:] = own.astype(BF16)
    for peer in peers:
        out_send(q_width, 2 * HEAD_DIM, peer).start()
    mine = pltpu.make_async_copy(stage.at[my_rows, :], out_ref.at[:, column(me, 0, width)], l_out)
    mine.start()

    all_sent(None)
    chunks(0, IN_CHUNKS, all_sent)
    for j in range(len(groups)):
        rail_send(2 * j, 0).wait_send()
        rail_send(2 * j, 1).wait_send()
        sib_send(0, j).wait_send()
        gsib(j).wait_send()
        grail(2 * j + 2).wait_send()

    mine.wait()
    wait_bytes(out_ref.at[:, pl.ds(0, width * (n_head - 1))], s_out)
    wait_bytes(out_ref.at[:, pl.ds(0, width * (n_head - 1))], r_out)


def per_device(n_head, n_ctx, merged_qkv, out_grads, doc_lengths):
    rows = merged_qkv.shape[0]
    piece = rows * n_head
    n_groups = REACH // 2
    pair = 2 * HEAD_DIM
    dma = pltpu.SemaphoreType.DMA
    n_in = 1 + 2 * IN_CHUNKS
    macs = 5 * GROUP_Q * piece * (REACH + 1) * piece * HEAD_DIM
    return pl.pallas_call(
        functools.partial(kernel, n_head, n_ctx),
        out_shape=jax.ShapeDtypeStruct(merged_qkv.shape, BF16),
        in_specs=[pl.BlockSpec(memory_space=pltpu.SMEM), pl.BlockSpec(memory_space=pl.ANY),
                  pl.BlockSpec(memory_space=pl.ANY)],
        out_specs=pl.BlockSpec(memory_space=pltpu.VMEM),
        scratch_shapes=[
            pltpu.VMEM((REACH + 1, piece, pair), BF16),
            pltpu.VMEM((REACH + 1, piece, HEAD_DIM), BF16),
            pltpu.VMEM((piece, HEAD_DIM), BF16),
            pltpu.VMEM((piece, GROUP_Q * HEAD_DIM), BF16),
            pltpu.VMEM((piece, GROUP_Q * HEAD_DIM), BF16),
            pltpu.VMEM((n_groups, GROUP_Q, 2 * piece, piece), BF16),
            pltpu.VMEM((n_groups, GROUP_Q, 2 * piece, piece), F32),
            pltpu.VMEM((n_groups, GROUP_Q, piece), F32),
            pltpu.VMEM((n_groups, GROUP_Q, piece), F32),
            pltpu.VMEM((n_groups, GROUP_Q, piece), F32),
            pltpu.VMEM((n_groups, GROUP_Q, piece), F32),
            pltpu.VMEM((GROUP_Q, piece), F32),
            pltpu.VMEM((GROUP_Q, piece, HEAD_DIM), F32),
            pltpu.VMEM((piece, pair), F32),
            pltpu.VMEM((2, piece, pair), F32),
            pltpu.VMEM((piece, pair), F32),
            pltpu.VMEM((piece, pair), BF16),
            pltpu.VMEM((n_groups, piece, pair), BF16),
            pltpu.VMEM((n_groups, piece, pair), BF16),
            pltpu.VMEM((n_groups, piece, pair), BF16),
            pltpu.VMEM((n_groups, piece, pair), BF16),
            pltpu.VMEM((piece, (GROUP_Q + 2) * HEAD_DIM), BF16),
            dma((n_in,)), dma((n_in,)), dma((n_in,)),
            dma((n_groups, 2)), dma((n_groups, 2)), dma,
            dma((n_groups,)), dma((n_groups,)),
            dma((n_groups,)), dma((n_groups,)),
            dma((n_groups,)), dma((n_groups,)),
            dma, dma, dma,
        ],
        compiler_params=pltpu.CompilerParams(
            collective_id=0, has_side_effects=True, vmem_limit_bytes=56 * 1024 * 1024),
        cost_estimate=pl.CostEstimate(
            flops=2 * macs, bytes_accessed=4 * merged_qkv.size * 2,
            transcendentals=GROUP_Q * piece * piece * REACH),
    )(doc_lengths, merged_qkv, out_grads)


def solution(mesh):
    placed = (P(("ctx", "head"), None), P(("ctx", "head"), None), P())
    body = functools.partial(per_device, mesh.shape["head"], mesh.shape["ctx"])
    return jax.shard_map(
        body, mesh=mesh, in_specs=placed, out_specs=P(("ctx", "head"), None), check_vma=False
    )
```

```python
import functools
import math

import jax
import jax.numpy as jnp
from jax import lax
from jax.experimental import pallas as pl
from jax.experimental.pallas import tpu as pltpu
from jax.sharding import PartitionSpec as P

GROUP_Q = 8
HEAD_DIM = 128
REACH = 6
MESH = pl.DeviceIdType.MESH
SCALE = HEAD_DIM ** -0.5
TO_EXP2 = SCALE * math.log2(math.e)
FAR = 2.0 ** 100
F32, BF16 = jnp.float32, jnp.bfloat16
IN_CHUNKS = 4
HEADS_STEP = 2
ROWS_STEP = 64
Z_CHIPS = 8


def nt(a, b):
    return lax.dot_general(a, b, (((1,), (1,)), ((), ())), preferred_element_type=F32)


def nn(a, b):
    return lax.dot_general(a, b, (((1,), (0,)), ((), ())), preferred_element_type=F32)


def tn(a, b):
    return lax.dot_general(a, b, (((0,), (0,)), ((), ())), preferred_element_type=F32)


def wait_bytes(ref, sem):
    pltpu.make_async_copy(ref, ref, sem).wait()


def kernel(n_head, n_ctx, lens_ref, qkv_ref, grads_ref, out_ref,
           kv, key_doc, query_doc, qb, dob, probs, dprobs, st_m, st_l, st_d, gain, delta,
           dq, home, part, even, relay_kv, cross_in,
           odd_out, odd_in, rail_out, rail_in, stage,
           s_in, r_in, l_in, s_rail, r_rail, s_cross, r_cross, r_back, s_sib, r_sib,
           s_grail, r_grail, s_gsib, r_gsib, s_out, r_out, l_out):
    rows = qkv_ref.shape[0]
    piece = kv.shape[1]
    width = (GROUP_Q + 2) * HEAD_DIM
    q_width = GROUP_Q * HEAD_DIM
    me = lax.axis_index("head")
    ctx = lax.axis_index("ctx")
    core = lax.rem(ctx, 2)
    sib = ctx + 1 - 2 * core
    z = lax.rem(ctx // 2, Z_CHIPS)
    n_groups = REACH // 2
    starts_run, ends_run = z == 0, z == Z_CHIPS - 1
    crosses = z >= Z_CHIPS - n_groups

    def shifted(steps):
        return lax.rem(ctx + n_ctx + 2 * steps, n_ctx)

    after, before = shifted(1), shifted(-1)
    next_run, last_run = shifted(Z_CHIPS), shifted(-Z_CHIPS)
    run_start = shifted(-z)
    run_ends = [shifted(Z_CHIPS - 1 - i) for i in range(n_groups)]
    peers = [lax.rem(me + p, n_head) for p in range(1, n_head)]

    barrier = pltpu.get_barrier_semaphore()

    def greet(axis, other):
        pl.semaphore_signal(barrier, inc=1, device_id={axis: other}, device_id_type=MESH)

    for peer in peers:
        greet("head", peer)
    greet("ctx", sib)

    def where(condition, body):
        @pl.when(condition)
        def _():
            body()

    where(jnp.logical_not(starts_run), lambda: greet("ctx", before))
    where(jnp.logical_not(ends_run), lambda: greet("ctx", after))

    @pl.when(crosses)
    def _():
        for other in (next_run, last_run, run_start, shifted(Z_CHIPS - z)):
            greet("ctx", other)

    @pl.when(starts_run)
    def _():
        for other in run_ends + [shifted(-1 - i) for i in range(n_groups)]:
            greet("ctx", other)

    more = jnp.where(starts_run, 2 * n_groups - 1, jnp.where(ends_run, 3, jnp.where(crosses, 4, 0)))
    pl.semaphore_wait(barrier, len(peers) + 3 + more)

    my_rows = pl.ds(pl.multiple_of(me * rows, rows), rows)

    def column(group, first, size):
        return pl.ds(pl.multiple_of(group * width + first, HEAD_DIM), size)

    def grad_column(group, first, size):
        return pl.ds(pl.multiple_of(group * q_width + first, HEAD_DIM), size)

    step_w = q_width // IN_CHUNKS
    others = pl.ds(0, rows * (n_head - 1))

    def sends(chunk):
        if chunk is None:
            return [(qkv_ref, lambda g: column(g, q_width, 2 * HEAD_DIM), kv.at[0],
                     pl.ds(0, 2 * HEAD_DIM), 0)]
        first = chunk * step_w
        cols = pl.ds(pl.multiple_of(first, HEAD_DIM), step_w)
        return [(qkv_ref, lambda g: column(g, first, step_w), qb, cols, 1 + 2 * chunk),
                (grads_ref, lambda g: grad_column(g, first, step_w), dob, cols, 2 + 2 * chunk)]

    def send_to(chunk, targets):
        for src, src_cols, dst, dst_cols, i in sends(chunk):
            for peer in targets:
                pltpu.make_async_remote_copy(
                    src_ref=src.at[:, src_cols(peer)], dst_ref=dst.at[my_rows, dst_cols],
                    send_sem=s_in.at[i], recv_sem=r_in.at[i],
                    device_id={"head": peer}, device_id_type=MESH).start()

    def send_all(chunk):
        for src, src_cols, dst, dst_cols, i in sends(chunk):
            pltpu.make_async_copy(
                src.at[:, src_cols(me)], dst.at[my_rows, dst_cols], l_in.at[i]).start()
        send_to(chunk, peers)

    def arrived(chunk):
        for src, src_cols, dst, dst_cols, i in sends(chunk):
            pltpu.make_async_copy(
                src.at[:, src_cols(me)], dst.at[my_rows, dst_cols], l_in.at[i]).wait()
            wait_bytes(dst.at[others, dst_cols], r_in.at[i])

    def all_sent(chunk):
        for src, src_cols, dst, dst_cols, i in sends(chunk):
            wait_bytes(dst.at[others, dst_cols], s_in.at[i])

    def chunks(first, end, body):
        def step(chunk, carry):
            body(chunk)
            return carry

        lax.fori_loop(first, end, step, 0)

    send_all(None)

    def ctx_copy(src, dst, send_sem, recv_sem, device):
        return pltpu.make_async_remote_copy(
            src_ref=src, dst_ref=dst, send_sem=send_sem, recv_sem=recv_sem,
            device_id={"ctx": device}, device_id_type=MESH)

    lane = lax.broadcasted_iota(jnp.int32, (1, HEAD_DIM), 1)
    starts = jnp.full((1, HEAD_DIM), 1 << 20, jnp.int32)
    ends = jnp.full((1, HEAD_DIM), 1 << 20, jnp.int32)
    total = jnp.int32(0)
    for d in range(lens_ref.shape[0]):
        starts = jnp.where(lane == d, total, starts)
        total = total + lens_ref[d]
        ends = jnp.where(lane == d, total, ends)
    row_of = lax.broadcasted_iota(jnp.int32, (piece, HEAD_DIM), 0)
    lane_of = lax.broadcasted_iota(jnp.int32, (piece, HEAD_DIM), 1)
    for r in range(REACH + 1):
        pos = row_of + (ctx - r) * piece
        inside = ((starts <= pos) & (pos < ends)) | ((lane_of == HEAD_DIM - 1) & (pos < 0))
        key_doc[r] = jnp.where(inside, 1.0, 0.0).astype(BF16)
        if r == 0:
            query_doc[...] = jnp.where(inside, 0.0, -FAR).astype(BF16)
    row_iota = lax.broadcasted_iota(jnp.int32, (ROWS_STEP, piece), 0)
    col_iota = lax.broadcasted_iota(jnp.int32, (ROWS_STEP, piece), 1)

    def half(part_no):
        return pl.ds(part_no * (piece // 2), piece // 2)

    def rail_send(r, part_no):
        at, i = half(part_no), r // 2
        return ctx_copy(kv.at[r, at], kv.at[r + 2, at], s_rail.at[i, part_no], r_rail.at[i, part_no], after)

    def cross_send(part_no):
        at = half(part_no)
        return ctx_copy(kv.at[0, at], relay_kv.at[at], s_cross.at[part_no], r_cross.at[part_no], next_run)

    def cross_on(part_no):
        i, at = Z_CHIPS - 1 - z, half(part_no)
        return ctx_copy(relay_kv.at[at], kv.at[2 * i + 2, at], s_cross.at[2 + part_no],
                        r_rail.at[i, part_no], run_start)

    def sib_send(k, j):
        return ctx_copy(kv.at[2 * j + 2 * k], kv.at[2 * j + 1], s_sib.at[j], r_sib.at[j], sib)

    def pass_on(r):
        for part_no in range(2):
            if r > 0:
                rail_send(r - 2, part_no).wait_recv()
            if r < REACH:
                where(jnp.logical_not(ends_run), lambda: rail_send(r, part_no).start())
        if r < REACH:
            where(core == 0, lambda: sib_send(0, r // 2).start())
        if r > 0:
            where(core == 1, lambda: sib_send(1, r // 2 - 1).start())

    arrived(None)

    @pl.when(crosses)
    def _():
        for part_no in range(2):
            cross_send(part_no).start()

    pass_on(0)
    where(jnp.logical_not(crosses), lambda: chunks(0, IN_CHUNKS, send_all))

    groups = ((1, 2), (3, 4), (5, 6))
    last = len(groups) - 1

    heads_chunk = GROUP_Q // IN_CHUNKS

    def forward(gi, first_head):
        ra, rb = groups[gi]

        for u in range(heads_chunk):
            j = first_head + u
            cols = pl.ds(pl.multiple_of(j * HEAD_DIM, HEAD_DIM), HEAD_DIM)
            query = jnp.concatenate([qb[:, cols], query_doc[...]], axis=1)
            grad = dob[:, cols]

            blocks = (ra, rb, 0) if gi == last else (ra, rb)
            keys = jnp.concatenate(
                [jnp.concatenate([kv[r, :, :HEAD_DIM], key_doc[r]], axis=1) for r in blocks], axis=0)
            values = jnp.concatenate([kv[r, :, HEAD_DIM:] for r in blocks], axis=0)
            s = nt(keys, query)
            dp = nt(values, grad)
            blocks_of = [pl.ds(i * ROWS_STEP, ROWS_STEP) for i in range(2 * piece // ROWS_STEP)]

            def rows_of(a, i):
                first = i * ROWS_STEP
                part_a = a[first:first + ROWS_STEP]
                if gi == last and first >= piece:
                    tri = row_iota + (first - piece) <= col_iota
                    part_a = jnp.where(tri, a[first + piece:first + piece + ROWS_STEP], part_a)
                return part_a

            s = [rows_of(s, i) for i in range(len(blocks_of))]
            top = functools.reduce(jnp.maximum, [jnp.max(a, axis=0, keepdims=True) for a in s])
            top = top * TO_EXP2
            total_p = total_d = jnp.zeros((1, piece), F32)
            for i, at in enumerate(blocks_of):
                dp_i = rows_of(dp, i)
                p = jnp.exp2(s[i] * TO_EXP2 - top)
                probs[gi, j, at] = p.astype(BF16)
                dprobs[gi, j, at] = dp_i
                total_p = total_p + jnp.sum(p, axis=0, keepdims=True)
                total_d = total_d + jnp.sum(p * dp_i, axis=0, keepdims=True)
            at = pl.ds(j, 1)
            st_m[gi, at, :] = top
            st_l[gi, at, :] = total_p
            st_d[gi, at, :] = total_d

    pass_on(2)

    @pl.when(crosses)
    def _():
        for part_no in range(2):
            cross_send(part_no).wait_recv()
            cross_on(part_no).start()
        chunks(0, IN_CHUNKS, send_all)

    pass_on(4)
    for gi in range(last):
        sib_send(0, gi).wait_recv()

    def early_groups(chunk):
        where(chunk == IN_CHUNKS - 1, lambda: pass_on(REACH))
        arrived(chunk)
        for gi in range(last):
            forward(gi, chunk * heads_chunk)

    chunks(0, IN_CHUNKS, early_groups)
    sib_send(0, last).wait_recv()
    chunks(0, IN_CHUNKS, lambda chunk: forward(last, chunk * heads_chunk))

    top = jnp.maximum(jnp.maximum(st_m[0], st_m[1]), st_m[2])
    factors = [jnp.exp2(st_m[gi] - top) for gi in range(len(groups))]
    inverse = 1.0 / sum(factors[gi] * st_l[gi] for gi in range(len(groups)))
    row_delta = jnp.zeros_like(inverse)
    for gi in range(len(groups)):
        gain[gi] = factors[gi] * inverse
        row_delta = row_delta + factors[gi] * inverse * st_d[gi]
    delta[...] = row_delta

    def out_send(first, size, peer):
        cols = pl.ds(first if isinstance(first, int) else pl.multiple_of(first, HEAD_DIM), size)
        return pltpu.make_async_remote_copy(
            src_ref=stage.at[pl.ds(pl.multiple_of(peer * rows, rows), rows), cols],
            dst_ref=out_ref.at[:, column(me, first, size)],
            send_sem=s_out, recv_sem=r_out,
            device_id={"head": peer}, device_id_type=MESH)

    def backward(gi):
        ra, rb = groups[gi]
        final = gi == 0
        heads_step = HEADS_STEP if final else 2 * HEADS_STEP

        def body(step, carry):
            if gi < last:

                @pl.when(step == 1)
                def _():
                    send_sum(gi + 1)

            blocks = (ra, rb, 0) if gi == last else (ra, rb)
            keys = jnp.concatenate([kv[r, :, :HEAD_DIM] for r in blocks], axis=0)
            p_all, ds_all, grad_all, query_all = [], [], [], []
            for u in range(heads_step):
                j = step * heads_step + u
                cols = pl.ds(pl.multiple_of(j * HEAD_DIM, HEAD_DIM), HEAD_DIM)
                at = pl.ds(j, 1)
                gain_j, delta_j = gain[gi, at, :], delta[at, :]
                p, ds, p_own, ds_own = [], [], [], []
                for i in range(2 * piece // ROWS_STEP):
                    rows_i = pl.ds(i * ROWS_STEP, ROWS_STEP)
                    p_i = probs[gi, j, rows_i].astype(F32) * gain_j
                    ds_i = p_i * (dprobs[gi, j, rows_i] - delta_j)
                    if gi == last and i * ROWS_STEP >= piece:
                        tri = row_iota + (i * ROWS_STEP - piece) <= col_iota
                        p_own.append(jnp.where(tri, p_i, 0.0).astype(BF16))
                        ds_own.append(jnp.where(tri, ds_i, 0.0).astype(BF16))
                        p_i, ds_i = jnp.where(tri, 0.0, p_i), jnp.where(tri, 0.0, ds_i)
                    p.append(p_i.astype(BF16))
                    ds.append(ds_i.astype(BF16))
                p = jnp.concatenate(p + p_own, axis=0)
                ds = jnp.concatenate(ds + ds_own, axis=0)
                p_all.append(p)
                ds_all.append(ds)
                grad_all.append(dob[:, cols])
                query_all.append(qb[:, cols])
                grad_query = tn(ds, keys)
                if gi != last:
                    grad_query = grad_query + dq[j]
                if final:
                    stage[:, cols] = (grad_query * SCALE).astype(BF16)
                else:
                    dq[j] = grad_query
            p = jnp.concatenate(p_all, axis=1)
            ds = jnp.concatenate(ds_all, axis=1)
            grad_value = nn(p, jnp.concatenate(grad_all, axis=0))
            grad_key = nn(ds, jnp.concatenate(query_all, axis=0))
            for i in range(2):
                at = pl.ds(i * piece, piece)
                part[i, :, :HEAD_DIM] += grad_key[i * piece:(i + 1) * piece]
                part[i, :, HEAD_DIM:] += grad_value[i * piece:(i + 1) * piece]
            if gi == last:
                home[:, :HEAD_DIM] += grad_key[2 * piece:]
                home[:, HEAD_DIM:] += grad_value[2 * piece:]
            if final:
                first = step * HEADS_STEP * HEAD_DIM
                for peer in peers:
                    out_send(first, HEADS_STEP * HEAD_DIM, peer).start()
            return carry

        lax.fori_loop(0, GROUP_Q // heads_step, body, 0)

    def grail(r):
        i = r // 2 - 1
        return ctx_copy(rail_out.at[i], rail_in.at[i], s_grail.at[i], r_grail.at[i], before)

    def grail_home(gi):
        return ctx_copy(rail_out.at[gi], cross_in, s_grail.at[gi], r_back, shifted(-1 - gi))

    def gsib(j):
        return ctx_copy(odd_out.at[j], odd_in.at[j], s_gsib.at[j], r_gsib.at[j], sib)

    def key_scale():
        which = lax.broadcasted_iota(jnp.int32, (1, 2 * HEAD_DIM), 1)
        return jnp.where(which < HEAD_DIM, SCALE, 1.0)

    def send_sum(gi):
        rb, j = groups[gi][1], gi
        if gi < last:
            @pl.when(jnp.logical_not(ends_run))
            def _():
                grail(rb + 2).wait_recv()
                even[...] += rail_in[rb // 2].astype(F32)

            @pl.when(core == 0)
            def _():
                gsib(j + 1).wait_recv()
                even[...] += odd_in[j + 1].astype(F32)

        @pl.when(core == 1)
        def _():
            gsib(j).wait_recv()
            even[...] += odd_in[j].astype(F32)

        rail_out[rb // 2 - 1] = even[...].astype(BF16)

        @pl.when(starts_run)
        def _():
            grail_home(gi).start()

        @pl.when(jnp.logical_not(starts_run))
        def _():
            grail(rb).start()

    home[...] = jnp.zeros_like(home)
    for gi in range(last, -1, -1):
        part[...] = jnp.zeros_like(part)
        backward(gi)
        odd_out[gi] = (part[0] * key_scale()).astype(BF16)
        gsib(gi).start()
        even[...] = part[1] * key_scale()
    send_sum(0)

    home[...] = home[...] * key_scale()

    @pl.when(core == 0)
    def _():
        gsib(0).wait_recv()
        home[...] += odd_in[0].astype(F32)

    @pl.when(jnp.logical_not(ends_run))
    def _():
        grail(2).wait_recv()
        home[...] += rail_in[0].astype(F32)

    @pl.when(crosses)
    def _():
        grail_home(0).wait_recv()
        home[...] += cross_in[...].astype(F32)

    own = home[...]
    stage[:, q_width:] = own.astype(BF16)
    for peer in peers:
        out_send(q_width, 2 * HEAD_DIM, peer).start()
    mine = pltpu.make_async_copy(stage.at[my_rows, :], out_ref.at[:, column(me, 0, width)], l_out)
    mine.start()

    all_sent(None)
    chunks(0, IN_CHUNKS, all_sent)
    for j in range(len(groups)):
        where(jnp.logical_not(ends_run), lambda j=j: [rail_send(2 * j, i).wait_send() for i in range(2)])
        sib_send(0, j).wait_send()
        gsib(j).wait_send()
        grail(2 * j + 2).wait_send()

    @pl.when(crosses)
    def _():
        for part_no in range(2):
            cross_send(part_no).wait_send()
            cross_on(part_no).wait_send()

    mine.wait()
    wait_bytes(out_ref.at[:, pl.ds(0, width * (n_head - 1))], s_out)
    wait_bytes(out_ref.at[:, pl.ds(0, width * (n_head - 1))], r_out)


def per_device(n_head, n_ctx, merged_qkv, out_grads, doc_lengths):
    rows = merged_qkv.shape[0]
    piece = rows * n_head
    n_groups = REACH // 2
    pair = 2 * HEAD_DIM
    dma = pltpu.SemaphoreType.DMA
    n_in = 1 + 2 * IN_CHUNKS
    macs = 5 * GROUP_Q * piece * (REACH + 1) * piece * HEAD_DIM
    return pl.pallas_call(
        functools.partial(kernel, n_head, n_ctx),
        out_shape=jax.ShapeDtypeStruct(merged_qkv.shape, BF16),
        in_specs=[pl.BlockSpec(memory_space=pltpu.SMEM), pl.BlockSpec(memory_space=pl.ANY),
                  pl.BlockSpec(memory_space=pl.ANY)],
        out_specs=pl.BlockSpec(memory_space=pltpu.VMEM),
        scratch_shapes=[
            pltpu.VMEM((REACH + 1, piece, pair), BF16),
            pltpu.VMEM((REACH + 1, piece, HEAD_DIM), BF16),
            pltpu.VMEM((piece, HEAD_DIM), BF16),
            pltpu.VMEM((piece, GROUP_Q * HEAD_DIM), BF16),
            pltpu.VMEM((piece, GROUP_Q * HEAD_DIM), BF16),
            pltpu.VMEM((n_groups, GROUP_Q, 2 * piece, piece), BF16),
            pltpu.VMEM((n_groups, GROUP_Q, 2 * piece, piece), F32),
            pltpu.VMEM((n_groups, GROUP_Q, piece), F32),
            pltpu.VMEM((n_groups, GROUP_Q, piece), F32),
            pltpu.VMEM((n_groups, GROUP_Q, piece), F32),
            pltpu.VMEM((n_groups, GROUP_Q, piece), F32),
            pltpu.VMEM((GROUP_Q, piece), F32),
            pltpu.VMEM((GROUP_Q, piece, HEAD_DIM), F32),
            pltpu.VMEM((piece, pair), F32),
            pltpu.VMEM((2, piece, pair), F32),
            pltpu.VMEM((piece, pair), F32),
            pltpu.VMEM((piece, pair), BF16),
            pltpu.VMEM((piece, pair), BF16),
            pltpu.VMEM((n_groups, piece, pair), BF16),
            pltpu.VMEM((n_groups, piece, pair), BF16),
            pltpu.VMEM((n_groups, piece, pair), BF16),
            pltpu.VMEM((n_groups, piece, pair), BF16),
            pltpu.VMEM((piece, (GROUP_Q + 2) * HEAD_DIM), BF16),
            dma((n_in,)), dma((n_in,)), dma((n_in,)),
            dma((n_groups, 2)), dma((n_groups, 2)), dma((4,)), dma((2,)), dma,
            dma((n_groups,)), dma((n_groups,)),
            dma((n_groups,)), dma((n_groups,)),
            dma((n_groups,)), dma((n_groups,)),
            dma, dma, dma,
        ],
        compiler_params=pltpu.CompilerParams(
            collective_id=0, has_side_effects=True, vmem_limit_bytes=56 * 1024 * 1024),
        cost_estimate=pl.CostEstimate(
            flops=2 * macs, bytes_accessed=4 * merged_qkv.size * 2,
            transcendentals=GROUP_Q * piece * piece * REACH),
    )(doc_lengths, merged_qkv, out_grads)


def solution(mesh):
    placed = (P(("ctx", "head"), None), P(("ctx", "head"), None), P())
    body = functools.partial(per_device, mesh.shape["head"], mesh.shape["ctx"])
    return jax.shard_map(
        body, mesh=mesh, in_specs=placed, out_specs=P(("ctx", "head"), None), check_vma=False
    )
```

```python
import functools
import math

import jax
import jax.numpy as jnp
from jax import lax
from jax.experimental import pallas as pl
from jax.experimental.pallas import tpu as pltpu
from jax.sharding import PartitionSpec as P

GROUP_Q = 8
HEAD_DIM = 128
REACH = 6
MESH = pl.DeviceIdType.MESH
SCALE = HEAD_DIM ** -0.5
TO_EXP2 = SCALE * math.log2(math.e)
FAR = 2.0 ** 100
F32, BF16 = jnp.float32, jnp.bfloat16
IN_CHUNKS = 4
HEADS_STEP = 2
ROWS_STEP = 64
Z_CHIPS = 8


def nt(a, b):
    return lax.dot_general(a, b, (((1,), (1,)), ((), ())), preferred_element_type=F32)


def nn(a, b):
    return lax.dot_general(a, b, (((1,), (0,)), ((), ())), preferred_element_type=F32)


def tn(a, b):
    return lax.dot_general(a, b, (((0,), (0,)), ((), ())), preferred_element_type=F32)


def wait_bytes(ref, sem):
    pltpu.make_async_copy(ref, ref, sem).wait()


def kernel(n_head, n_ctx, lens_ref, qkv_ref, grads_ref, out_ref,
           kv, key_doc, query_doc, qb, dob, probs, dprobs, st_m, st_l, st_d, gain, delta,
           dq, home, part, even, relay_kv, cross_in,
           odd_out, odd_in, rail_out, rail_in, stage,
           s_in, r_in, l_in, s_rail, r_rail, s_cross, r_cross, r_back, s_sib, r_sib,
           s_grail, r_grail, s_gsib, r_gsib, s_out, r_out, l_out):
    rows = qkv_ref.shape[0]
    piece = kv.shape[1]
    width = (GROUP_Q + 2) * HEAD_DIM
    q_width = GROUP_Q * HEAD_DIM
    me = lax.axis_index("head")
    ctx = lax.axis_index("ctx")
    core = lax.rem(ctx, 2)
    sib = ctx + 1 - 2 * core
    z = lax.rem(ctx // 2, Z_CHIPS)
    n_groups = REACH // 2
    starts_run, ends_run = z == 0, z == Z_CHIPS - 1
    crosses = z >= Z_CHIPS - n_groups

    def shifted(steps):
        return lax.rem(ctx + n_ctx + 2 * steps, n_ctx)

    after, before = shifted(1), shifted(-1)
    next_run, last_run = shifted(Z_CHIPS), shifted(-Z_CHIPS)
    run_start = shifted(-z)
    run_ends = [shifted(Z_CHIPS - 1 - i) for i in range(n_groups)]
    peers = [lax.rem(me + p, n_head) for p in range(1, n_head)]

    barrier = pltpu.get_barrier_semaphore()

    def greet(axis, other):
        pl.semaphore_signal(barrier, inc=1, device_id={axis: other}, device_id_type=MESH)

    for peer in peers:
        greet("head", peer)
    greet("ctx", sib)

    def where(condition, body):
        @pl.when(condition)
        def _():
            body()

    where(jnp.logical_not(starts_run), lambda: greet("ctx", before))
    where(jnp.logical_not(ends_run), lambda: greet("ctx", after))

    @pl.when(crosses)
    def _():
        for other in (next_run, last_run, run_start, shifted(Z_CHIPS - z)):
            greet("ctx", other)

    @pl.when(starts_run)
    def _():
        for other in run_ends + [shifted(-1 - i) for i in range(n_groups)]:
            greet("ctx", other)

    more = jnp.where(starts_run, 2 * n_groups - 1, jnp.where(ends_run, 3, jnp.where(crosses, 4, 0)))
    pl.semaphore_wait(barrier, len(peers) + 3 + more)

    my_rows = pl.ds(pl.multiple_of(me * rows, rows), rows)

    def column(group, first, size):
        return pl.ds(pl.multiple_of(group * width + first, HEAD_DIM), size)

    def grad_column(group, first, size):
        return pl.ds(pl.multiple_of(group * q_width + first, HEAD_DIM), size)

    step_w = q_width // IN_CHUNKS
    others = pl.ds(0, rows * (n_head - 1))

    def sends(chunk):
        if chunk is None:
            return [(qkv_ref, lambda g: column(g, q_width, 2 * HEAD_DIM), kv.at[0],
                     pl.ds(0, 2 * HEAD_DIM), 0)]
        first = chunk * step_w
        cols = pl.ds(pl.multiple_of(first, HEAD_DIM), step_w)
        return [(qkv_ref, lambda g: column(g, first, step_w), qb, cols, 1 + 2 * chunk),
                (grads_ref, lambda g: grad_column(g, first, step_w), dob, cols, 2 + 2 * chunk)]

    def send_to(chunk, targets):
        for src, src_cols, dst, dst_cols, i in sends(chunk):
            for peer in targets:
                pltpu.make_async_remote_copy(
                    src_ref=src.at[:, src_cols(peer)], dst_ref=dst.at[my_rows, dst_cols],
                    send_sem=s_in.at[i], recv_sem=r_in.at[i],
                    device_id={"head": peer}, device_id_type=MESH).start()

    def send_along_x(chunk):
        for src, src_cols, dst, dst_cols, i in sends(chunk):
            pltpu.make_async_copy(
                src.at[:, src_cols(me)], dst.at[my_rows, dst_cols], l_in.at[i]).start()
        send_to(chunk, peers[1::2])

    def send_across_y(chunk):
        send_to(chunk, peers[0::2])

    def send_all(chunk):
        send_along_x(chunk)
        send_across_y(chunk)

    def arrived(chunk):
        for src, src_cols, dst, dst_cols, i in sends(chunk):
            pltpu.make_async_copy(
                src.at[:, src_cols(me)], dst.at[my_rows, dst_cols], l_in.at[i]).wait()
            wait_bytes(dst.at[others, dst_cols], r_in.at[i])

    def all_sent(chunk):
        for src, src_cols, dst, dst_cols, i in sends(chunk):
            wait_bytes(dst.at[others, dst_cols], s_in.at[i])

    def chunks(first, end, body):
        def step(chunk, carry):
            body(chunk)
            return carry

        lax.fori_loop(first, end, step, 0)

    send_all(None)

    def ctx_copy(src, dst, send_sem, recv_sem, device):
        return pltpu.make_async_remote_copy(
            src_ref=src, dst_ref=dst, send_sem=send_sem, recv_sem=recv_sem,
            device_id={"ctx": device}, device_id_type=MESH)

    lane = lax.broadcasted_iota(jnp.int32, (1, HEAD_DIM), 1)
    starts = jnp.full((1, HEAD_DIM), 1 << 20, jnp.int32)
    ends = jnp.full((1, HEAD_DIM), 1 << 20, jnp.int32)
    total = jnp.int32(0)
    for d in range(lens_ref.shape[0]):
        starts = jnp.where(lane == d, total, starts)
        total = total + lens_ref[d]
        ends = jnp.where(lane == d, total, ends)
    row_of = lax.broadcasted_iota(jnp.int32, (piece, HEAD_DIM), 0)
    lane_of = lax.broadcasted_iota(jnp.int32, (piece, HEAD_DIM), 1)
    for r in range(REACH + 1):
        pos = row_of + (ctx - r) * piece
        inside = ((starts <= pos) & (pos < ends)) | ((lane_of == HEAD_DIM - 1) & (pos < 0))
        key_doc[r] = jnp.where(inside, 1.0, 0.0).astype(BF16)
        if r == 0:
            query_doc[...] = jnp.where(inside, 0.0, -FAR).astype(BF16)
    row_iota = lax.broadcasted_iota(jnp.int32, (ROWS_STEP, piece), 0)
    col_iota = lax.broadcasted_iota(jnp.int32, (ROWS_STEP, piece), 1)

    def half(part_no):
        return pl.ds(part_no * (piece // 2), piece // 2)

    def rail_send(r, part_no):
        at, i = half(part_no), r // 2
        return ctx_copy(kv.at[r, at], kv.at[r + 2, at], s_rail.at[i, part_no], r_rail.at[i, part_no], after)

    def cross_send(part_no):
        at = half(part_no)
        return ctx_copy(kv.at[0, at], relay_kv.at[at], s_cross.at[part_no], r_cross.at[part_no], next_run)

    def cross_on(part_no):
        i, at = Z_CHIPS - 1 - z, half(part_no)
        return ctx_copy(relay_kv.at[at], kv.at[2 * i + 2, at], s_cross.at[2 + part_no],
                        r_rail.at[i, part_no], run_start)

    def sib_send(k, j):
        return ctx_copy(kv.at[2 * j + 2 * k], kv.at[2 * j + 1], s_sib.at[j], r_sib.at[j], sib)

    def pass_on(r):
        for part_no in range(2):
            if r > 0:
                rail_send(r - 2, part_no).wait_recv()
            if r < REACH:
                where(jnp.logical_not(ends_run), lambda: rail_send(r, part_no).start())
        if r < REACH:
            where(core == 0, lambda: sib_send(0, r // 2).start())
        if r > 0:
            where(core == 1, lambda: sib_send(1, r // 2 - 1).start())

    arrived(None)

    @pl.when(crosses)
    def _():
        for part_no in range(2):
            cross_send(part_no).start()

    pass_on(0)
    where(crosses, lambda: chunks(0, 2, send_along_x))
    where(jnp.logical_not(crosses), lambda: chunks(0, IN_CHUNKS, send_all))

    groups = ((1, 2), (3, 4), (5, 6))
    last = len(groups) - 1

    heads_chunk = GROUP_Q // IN_CHUNKS

    def forward(gi, first_head):
        ra, rb = groups[gi]

        for u in range(heads_chunk):
            j = first_head + u
            cols = pl.ds(pl.multiple_of(j * HEAD_DIM, HEAD_DIM), HEAD_DIM)
            query = jnp.concatenate([qb[:, cols], query_doc[...]], axis=1)
            grad = dob[:, cols]

            blocks = (ra, rb, 0) if gi == last else (ra, rb)
            keys = jnp.concatenate(
                [jnp.concatenate([kv[r, :, :HEAD_DIM], key_doc[r]], axis=1) for r in blocks], axis=0)
            values = jnp.concatenate([kv[r, :, HEAD_DIM:] for r in blocks], axis=0)
            s = nt(keys, query)
            dp = nt(values, grad)
            blocks_of = [pl.ds(i * ROWS_STEP, ROWS_STEP) for i in range(2 * piece // ROWS_STEP)]

            def rows_of(a, i):
                first = i * ROWS_STEP
                part_a = a[first:first + ROWS_STEP]
                if gi == last and first >= piece:
                    tri = row_iota + (first - piece) <= col_iota
                    part_a = jnp.where(tri, a[first + piece:first + piece + ROWS_STEP], part_a)
                return part_a

            s = [rows_of(s, i) for i in range(len(blocks_of))]
            top = functools.reduce(jnp.maximum, [jnp.max(a, axis=0, keepdims=True) for a in s])
            top = top * TO_EXP2
            total_p = total_d = jnp.zeros((1, piece), F32)
            for i, at in enumerate(blocks_of):
                dp_i = rows_of(dp, i)
                p = jnp.exp2(s[i] * TO_EXP2 - top)
                probs[gi, j, at] = p.astype(BF16)
                dprobs[gi, j, at] = dp_i
                total_p = total_p + jnp.sum(p, axis=0, keepdims=True)
                total_d = total_d + jnp.sum(p * dp_i, axis=0, keepdims=True)
            at = pl.ds(j, 1)
            st_m[gi, at, :] = top
            st_l[gi, at, :] = total_p
            st_d[gi, at, :] = total_d

    pass_on(2)

    @pl.when(crosses)
    def _():
        for part_no in range(2):
            cross_send(part_no).wait_recv()
            cross_on(part_no).start()
        chunks(0, 2, send_across_y)
        chunks(2, IN_CHUNKS, send_all)

    pass_on(4)
    for gi in range(last):
        sib_send(0, gi).wait_recv()

    def early_groups(chunk):
        where(chunk == IN_CHUNKS - 1, lambda: pass_on(REACH))
        arrived(chunk)
        for gi in range(last):
            forward(gi, chunk * heads_chunk)

    chunks(0, IN_CHUNKS, early_groups)
    sib_send(0, last).wait_recv()
    chunks(0, IN_CHUNKS, lambda chunk: forward(last, chunk * heads_chunk))

    top = jnp.maximum(jnp.maximum(st_m[0], st_m[1]), st_m[2])
    factors = [jnp.exp2(st_m[gi] - top) for gi in range(len(groups))]
    inverse = 1.0 / sum(factors[gi] * st_l[gi] for gi in range(len(groups)))
    row_delta = jnp.zeros_like(inverse)
    for gi in range(len(groups)):
        gain[gi] = factors[gi] * inverse
        row_delta = row_delta + factors[gi] * inverse * st_d[gi]
    delta[...] = row_delta

    def out_send(first, size, peer):
        cols = pl.ds(first if isinstance(first, int) else pl.multiple_of(first, HEAD_DIM), size)
        return pltpu.make_async_remote_copy(
            src_ref=stage.at[pl.ds(pl.multiple_of(peer * rows, rows), rows), cols],
            dst_ref=out_ref.at[:, column(me, first, size)],
            send_sem=s_out, recv_sem=r_out,
            device_id={"head": peer}, device_id_type=MESH)

    def backward(gi):
        ra, rb = groups[gi]
        final = gi == 0
        heads_step = HEADS_STEP if final else 2 * HEADS_STEP

        def body(step, carry):
            if gi < last:

                @pl.when(step == 1)
                def _():
                    send_sum(gi + 1)

            blocks = (ra, rb, 0) if gi == last else (ra, rb)
            keys = jnp.concatenate([kv[r, :, :HEAD_DIM] for r in blocks], axis=0)
            p_all, ds_all, grad_all, query_all = [], [], [], []
            for u in range(heads_step):
                j = step * heads_step + u
                cols = pl.ds(pl.multiple_of(j * HEAD_DIM, HEAD_DIM), HEAD_DIM)
                at = pl.ds(j, 1)
                gain_j, delta_j = gain[gi, at, :], delta[at, :]
                p, ds, p_own, ds_own = [], [], [], []
                for i in range(2 * piece // ROWS_STEP):
                    rows_i = pl.ds(i * ROWS_STEP, ROWS_STEP)
                    p_i = probs[gi, j, rows_i].astype(F32) * gain_j
                    ds_i = p_i * (dprobs[gi, j, rows_i] - delta_j)
                    if gi == last and i * ROWS_STEP >= piece:
                        tri = row_iota + (i * ROWS_STEP - piece) <= col_iota
                        p_own.append(jnp.where(tri, p_i, 0.0).astype(BF16))
                        ds_own.append(jnp.where(tri, ds_i, 0.0).astype(BF16))
                        p_i, ds_i = jnp.where(tri, 0.0, p_i), jnp.where(tri, 0.0, ds_i)
                    p.append(p_i.astype(BF16))
                    ds.append(ds_i.astype(BF16))
                p = jnp.concatenate(p + p_own, axis=0)
                ds = jnp.concatenate(ds + ds_own, axis=0)
                p_all.append(p)
                ds_all.append(ds)
                grad_all.append(dob[:, cols])
                query_all.append(qb[:, cols])
                grad_query = tn(ds, keys)
                if gi != last:
                    grad_query = grad_query + dq[j]
                if final:
                    stage[:, cols] = (grad_query * SCALE).astype(BF16)
                else:
                    dq[j] = grad_query
            p = jnp.concatenate(p_all, axis=1)
            ds = jnp.concatenate(ds_all, axis=1)
            grad_value = nn(p, jnp.concatenate(grad_all, axis=0))
            grad_key = nn(ds, jnp.concatenate(query_all, axis=0))
            for i in range(2):
                at = pl.ds(i * piece, piece)
                part[i, :, :HEAD_DIM] += grad_key[i * piece:(i + 1) * piece]
                part[i, :, HEAD_DIM:] += grad_value[i * piece:(i + 1) * piece]
            if gi == last:
                home[:, :HEAD_DIM] += grad_key[2 * piece:]
                home[:, HEAD_DIM:] += grad_value[2 * piece:]
            if final:
                first = step * HEADS_STEP * HEAD_DIM
                for peer in peers:
                    out_send(first, HEADS_STEP * HEAD_DIM, peer).start()
            return carry

        lax.fori_loop(0, GROUP_Q // heads_step, body, 0)

    def grail(r):
        i = r // 2 - 1
        return ctx_copy(rail_out.at[i], rail_in.at[i], s_grail.at[i], r_grail.at[i], before)

    def grail_home(gi):
        return ctx_copy(rail_out.at[gi], cross_in, s_grail.at[gi], r_back, shifted(-1 - gi))

    def gsib(j):
        return ctx_copy(odd_out.at[j], odd_in.at[j], s_gsib.at[j], r_gsib.at[j], sib)

    def key_scale():
        which = lax.broadcasted_iota(jnp.int32, (1, 2 * HEAD_DIM), 1)
        return jnp.where(which < HEAD_DIM, SCALE, 1.0)

    def send_sum(gi):
        rb, j = groups[gi][1], gi
        if gi < last:
            @pl.when(jnp.logical_not(ends_run))
            def _():
                grail(rb + 2).wait_recv()
                even[...] += rail_in[rb // 2].astype(F32)

            @pl.when(core == 0)
            def _():
                gsib(j + 1).wait_recv()
                even[...] += odd_in[j + 1].astype(F32)

        @pl.when(core == 1)
        def _():
            gsib(j).wait_recv()
            even[...] += odd_in[j].astype(F32)

        rail_out[rb // 2 - 1] = even[...].astype(BF16)

        @pl.when(starts_run)
        def _():
            grail_home(gi).start()

        @pl.when(jnp.logical_not(starts_run))
        def _():
            grail(rb).start()

    home[...] = jnp.zeros_like(home)
    for gi in range(last, -1, -1):
        part[...] = jnp.zeros_like(part)
        backward(gi)
        odd_out[gi] = (part[0] * key_scale()).astype(BF16)
        gsib(gi).start()
        even[...] = part[1] * key_scale()
    send_sum(0)

    home[...] = home[...] * key_scale()

    @pl.when(core == 0)
    def _():
        gsib(0).wait_recv()
        home[...] += odd_in[0].astype(F32)

    @pl.when(jnp.logical_not(ends_run))
    def _():
        grail(2).wait_recv()
        home[...] += rail_in[0].astype(F32)

    @pl.when(crosses)
    def _():
        grail_home(0).wait_recv()
        home[...] += cross_in[...].astype(F32)

    own = home[...]
    stage[:, q_width:] = own.astype(BF16)
    for peer in peers:
        out_send(q_width, 2 * HEAD_DIM, peer).start()
    mine = pltpu.make_async_copy(stage.at[my_rows, :], out_ref.at[:, column(me, 0, width)], l_out)
    mine.start()

    all_sent(None)
    chunks(0, IN_CHUNKS, all_sent)
    for j in range(len(groups)):
        where(jnp.logical_not(ends_run), lambda j=j: [rail_send(2 * j, i).wait_send() for i in range(2)])
        sib_send(0, j).wait_send()
        gsib(j).wait_send()
        grail(2 * j + 2).wait_send()

    @pl.when(crosses)
    def _():
        for part_no in range(2):
            cross_send(part_no).wait_send()
            cross_on(part_no).wait_send()

    mine.wait()
    wait_bytes(out_ref.at[:, pl.ds(0, width * (n_head - 1))], s_out)
    wait_bytes(out_ref.at[:, pl.ds(0, width * (n_head - 1))], r_out)


def per_device(n_head, n_ctx, merged_qkv, out_grads, doc_lengths):
    rows = merged_qkv.shape[0]
    piece = rows * n_head
    n_groups = REACH // 2
    pair = 2 * HEAD_DIM
    dma = pltpu.SemaphoreType.DMA
    n_in = 1 + 2 * IN_CHUNKS
    macs = 5 * GROUP_Q * piece * (REACH + 1) * piece * HEAD_DIM
    return pl.pallas_call(
        functools.partial(kernel, n_head, n_ctx),
        out_shape=jax.ShapeDtypeStruct(merged_qkv.shape, BF16),
        in_specs=[pl.BlockSpec(memory_space=pltpu.SMEM), pl.BlockSpec(memory_space=pl.ANY),
                  pl.BlockSpec(memory_space=pl.ANY)],
        out_specs=pl.BlockSpec(memory_space=pltpu.VMEM),
        scratch_shapes=[
            pltpu.VMEM((REACH + 1, piece, pair), BF16),
            pltpu.VMEM((REACH + 1, piece, HEAD_DIM), BF16),
            pltpu.VMEM((piece, HEAD_DIM), BF16),
            pltpu.VMEM((piece, GROUP_Q * HEAD_DIM), BF16),
            pltpu.VMEM((piece, GROUP_Q * HEAD_DIM), BF16),
            pltpu.VMEM((n_groups, GROUP_Q, 2 * piece, piece), BF16),
            pltpu.VMEM((n_groups, GROUP_Q, 2 * piece, piece), F32),
            pltpu.VMEM((n_groups, GROUP_Q, piece), F32),
            pltpu.VMEM((n_groups, GROUP_Q, piece), F32),
            pltpu.VMEM((n_groups, GROUP_Q, piece), F32),
            pltpu.VMEM((n_groups, GROUP_Q, piece), F32),
            pltpu.VMEM((GROUP_Q, piece), F32),
            pltpu.VMEM((GROUP_Q, piece, HEAD_DIM), F32),
            pltpu.VMEM((piece, pair), F32),
            pltpu.VMEM((2, piece, pair), F32),
            pltpu.VMEM((piece, pair), F32),
            pltpu.VMEM((piece, pair), BF16),
            pltpu.VMEM((piece, pair), BF16),
            pltpu.VMEM((n_groups, piece, pair), BF16),
            pltpu.VMEM((n_groups, piece, pair), BF16),
            pltpu.VMEM((n_groups, piece, pair), BF16),
            pltpu.VMEM((n_groups, piece, pair), BF16),
            pltpu.VMEM((piece, (GROUP_Q + 2) * HEAD_DIM), BF16),
            dma((n_in,)), dma((n_in,)), dma((n_in,)),
            dma((n_groups, 2)), dma((n_groups, 2)), dma((4,)), dma((2,)), dma,
            dma((n_groups,)), dma((n_groups,)),
            dma((n_groups,)), dma((n_groups,)),
            dma((n_groups,)), dma((n_groups,)),
            dma, dma, dma,
        ],
        compiler_params=pltpu.CompilerParams(
            collective_id=0, has_side_effects=True, vmem_limit_bytes=56 * 1024 * 1024),
        cost_estimate=pl.CostEstimate(
            flops=2 * macs, bytes_accessed=4 * merged_qkv.size * 2,
            transcendentals=GROUP_Q * piece * piece * REACH),
    )(doc_lengths, merged_qkv, out_grads)


def solution(mesh):
    placed = (P(("ctx", "head"), None), P(("ctx", "head"), None), P())
    body = functools.partial(per_device, mesh.shape["head"], mesh.shape["ctx"])
    return jax.shard_map(
        body, mesh=mesh, in_specs=placed, out_specs=P(("ctx", "head"), None), check_vma=False
    )
```
